32 devices in a mesh: expert: 8 (over y, x, core), hidden: 4 (over z).
Axes of the slice: x: 2, y: 2, z: 4, core: 2. Of those that a mesh axis runs over, the one named last changes fastest.
Arguments:
- tokens: bfloat16 [8192, 1024], P(('expert', 'hidden')), may hold values from -6 to 6
- assignment: int32 [8192, 1], P(('expert', 'hidden')), may hold values from 0 to 15; in each aligned block of 256 rows (0 to 255, 256 to 511, ...) at most 18 rows name the same one
- lengths: int32 [8], replicated, may hold values from 32 to 1024
- centroids: bfloat16 [16, 1024], P('expert', 'hidden'), may hold values from -0.125 to 0.125
- ln_gain: float32 [16, 1024], P('expert', 'hidden'), may hold values from 0.5 to 1.5
- ln_bias: float32 [16, 1024], P('expert', 'hidden'), may hold values from -2 to 2
- w_in: bfloat16 [16, 1024, 4096], P('expert', None, 'hidden'), may hold values from -0.1875 to 0.1875
- b_in: float32 [16, 4096], P('expert', 'hidden'), may hold values from -2 to 2
- w_out: bfloat16 [16, 4096, 1024], P('expert', 'hidden'), may hold values from -0.1875 to 0.1875
- b_out: float32 [16, 1024], P('expert', 'hidden'), may hold values from -2 to 2
- cotangent: bfloat16 [8192, 1024], P(('expert', 'hidden')), may hold values from -6 to 6
Outputs:
- mixed: bfloat16 [8192, 1024], P(('expert', 'hidden'))
- tokens_grad: bfloat16 [8192, 1024], P(('expert', 'hidden'))
- centroids_grad: float32 [16, 1024], P('expert', 'hidden')
- ln_gain_grad: float32 [16, 1024], P('expert', 'hidden')
- ln_bias_grad: float32 [16, 1024], P('expert', 'hidden')
- w_in_grad: float32 [16, 1024, 4096], P('expert', None, 'hidden')
- b_in_grad: float32 [16, 4096], P('expert', 'hidden')
- w_out_grad: float32 [16, 4096, 1024], P('expert', 'hidden')
- b_out_grad: float32 [16, 1024], P('expert', 'hidden')
- mean_gate: float32 [16], replicated
The draws below stay inside these ranges and needn't reach their ends.
Inputs may be any that keep to these rules, and one draw needn't show every extreme that they name: `assignment`: in each aligned block of 256 rows (the rows of one device) no expert is named by more than 18 rows, a bound that some block reaches; every expert is named by some row.
All inputs are finite; a program needn't handle non-finite values.
Results may differ from the reference program's by a relative error of at most 0.0061.
Values may be sent and summed in bfloat16 or wider, within the bound.
A program may use at most 128 MiB of HBM per device.

```python
import math
import jax
import jax.numpy as jnp
import numpy as np
from jax import lax

D = 1024
FF = 4096
TOK_DEV = 256
SEQ = 1024
EXPERTS = 16
CAP = 18
TOKENS = 8192
SEQS = 8
N_EXPERT = 8
N_HIDDEN = 4


def set_ends(array, stream_key, smallest, top_value):
    dims = array.shape
    spot = [jax.random.randint(jax.random.fold_in(stream_key, axis), (), 0, dims[axis]) for axis in range(len(dims))]
    array = array.at[tuple(spot)].set(smallest)
    longest = dims.index(max(dims))
    spot[longest] = (spot[longest] + 1) % dims[longest]
    return array.at[tuple(spot)].set(top_value)


def steps_of(rng, dims, pieces, smallest, high):
    factor_of = 1.0
    for axis_at, parts in pieces:
        steps = jax.random.uniform(jax.random.fold_in(jax.random.fold_in(rng, 6), axis_at), (parts,), jnp.float32, smallest / len(pieces), high / len(pieces))
        factor_of = factor_of * jnp.repeat(jnp.exp(steps), dims[axis_at] // parts).reshape((-1,) + (1,) * (len(dims) - 1 - axis_at))
    return factor_of


def assign_block(rng, own, number, rows, number_of, top, bound, slope):
    order = jax.random.permutation(rng, number_of)
    crowded, common = load_shares(number_of, rows * top, bound, slope, True), load_shares(number_of, rows * top, bound, slope, False)
    places = jnp.arange(number_of)

    def named(sizes, offset_by):
        used = int((sizes > 0).sum())
        fixed = max(1, used // 4)
        shifted = fixed + (places - fixed + offset_by * (used - fixed)) % max(1, number_of - fixed)
        return jnp.zeros((number_of,), jnp.int32).at[order[jnp.where(places < fixed, places, shifted)]].set(jnp.asarray(sizes, jnp.int32))

    sizes = jnp.where(number % 4 == 0, named(crowded, number // 4), named(common, number - number // 4 - 1))
    mixed = jax.random.permutation(jax.random.fold_in(own, 3), number_of)
    donor, sink = mixed[0:number_of // 2 * 2:2], mixed[1:number_of // 2 * 2:2]
    margin = jnp.minimum(sizes[donor] - 1, bound - sizes[sink]) // 2
    margin = jnp.where((donor == order[0]) | (sink == order[0]) | (sizes[sink] == 0), 0, jnp.maximum(margin, 0))
    shifted = jax.random.randint(jax.random.fold_in(own, 4), (number_of // 2,), 0, 1 << 20) % (margin + 1)
    sizes = sizes.at[donor].add(-shifted).at[sink].add(shifted)
    items = jnp.searchsorted(jnp.cumsum(sizes), jnp.arange(rows * top), side="right").astype(jnp.int32)
    table = items.reshape(top, rows).T
    table = table[jax.random.permutation(jax.random.fold_in(own, 1), rows)]
    offset_by = jax.random.randint(jax.random.fold_in(own, 2), (rows, 1), 0, top)
    return jnp.take_along_axis(table, (jnp.arange(top)[None, :] + offset_by) % top, axis=1)


def load_shares(count, total, bound, skew, full):
    weights = [(1 << 20) // math.isqrt(standing ** skew) + 1 for standing in range(1, count + 1)]
    largest = bound if full else min(bound, max(-(-total // count), total * weights[0] // sum(weights)))
    least = 1 if total - largest >= count - 1 else 0
    counts, rest = [largest] + [least] * (count - 1), total - largest - least * (count - 1)
    while rest > 0:
        free = [i for i in range(1, count) if counts[i] < largest] or [i for i in range(1, count) if counts[i] < bound]
        pool, remaining = sum([weights[i] for i in free]), rest
        for i in free:
            more = min(bound - counts[i], max(1, remaining * weights[i] // pool), rest)
            counts[i] = counts[i] + more
            rest = rest - more
    return np.array(counts)


def gaussian(key, shape, scale, most, cuts=(), kind=jnp.bfloat16):
    level = steps_of(key, shape, cuts, -0.22, 0.18) if cuts else 1.0
    array = jax.random.normal(key, shape, jnp.float32) * scale * level
    return jnp.minimum(jnp.maximum(array, -most), most).astype(kind)


def setup_inputs(seed: int = 0) -> dict:
    arg_keys = jax.random.split(jax.random.key(seed), 12)
    tokens = gaussian(arg_keys[0], (TOKENS, D), 1.0, 6.0, ((0, 32),))
    assignment_keys = jax.random.split(jax.random.fold_in(arg_keys[1], 1), TOKENS // TOK_DEV)
    assignment_turns = jax.random.permutation(jax.random.fold_in(arg_keys[1], 3), TOKENS // TOK_DEV)
    assignment = jax.vmap(lambda own, number: assign_block(jax.random.fold_in(arg_keys[1], 2), own, number, TOK_DEV, EXPERTS, 1, CAP, 0))(assignment_keys, assignment_turns).reshape((TOKENS, 1))
    lengths = set_ends(jax.random.randint(arg_keys[2], (SEQS,), SEQ // 32, SEQ + 1), jax.random.fold_in(arg_keys[2], 1), SEQ // 32, SEQ).astype(jnp.int32)
    centroids = gaussian(arg_keys[3], (EXPERTS, D), (2 * D) ** -0.5, 0.125, ((0, 8), (1, 4)))
    ln_gain = jnp.clip(1.0 + 0.1 * jax.random.normal(arg_keys[4], (EXPERTS, D), jnp.float32), 0.5, 1.5)
    ln_bias = gaussian(arg_keys[5], (EXPERTS, D), 0.15, 2.0, ((0, 8), (1, 4)), jnp.float32)
    w_in = gaussian(arg_keys[6], (EXPERTS, D, FF), D ** -0.5, 0.1875, ((0, 8), (2, 4)))
    b_in = gaussian(arg_keys[7], (EXPERTS, FF), 0.15, 2.0, ((0, 8), (1, 4)), jnp.float32)
    w_out = gaussian(arg_keys[8], (EXPERTS, FF, D), (FF // 4) ** -0.5, 0.1875, ((0, 8), (1, 4)))
    b_out = gaussian(arg_keys[9], (EXPERTS, D), 0.15, 2.0, ((0, 8), (1, 4)), jnp.float32)
    cotangent = gaussian(arg_keys[10], (TOKENS, D), 1.0, 6.0, ((0, 32),))
    return {"tokens": tokens, "assignment": assignment, "lengths": lengths, "centroids": centroids, "ln_gain": ln_gain, "ln_bias": ln_bias, "w_in": w_in, "b_in": b_in, "w_out": w_out, "b_out": b_out, "cotangent": cotangent}


EPS = 1e-05
HIGH = lax.Precision.HIGHEST

@jax.custom_vjp
def low(v):
    return lax.optimization_barrier(v.astype(jnp.bfloat16)).astype(jnp.float32)

@jax.custom_vjp
def low_back(v):
    return v

def low_keep(v):
    return (low(v), None)

def low_pass(kept, grad):
    return (grad,)

def back_keep(v):
    return (v, None)

def back_low(kept, grad):
    return (low(grad),)
low.defvjp(low_keep, low_pass)
low_back.defvjp(back_keep, back_low)

def normalize(rows):
    mean = lax.optimization_barrier(jnp.mean(rows, axis=-1, keepdims=True))
    centered = rows - mean
    var = lax.optimization_barrier(jnp.mean(centered * centered, axis=-1, keepdims=True))
    return centered * lax.rsqrt(var + EPS)

def expert_apply(rows, gain, shift, weight_in, bias_in, weight_out, bias_out):
    lifted = low(normalize(rows) * gain + shift)
    pre = low_back(jnp.dot(lifted, weight_in, precision=HIGH) + bias_in)
    active = low(jax.nn.gelu(pre))
    summed = jnp.dot(active, weight_out, precision=HIGH) + bias_out
    return low(low_back(summed))

def slots_of(assignment, lengths):
    devices = N_EXPERT * N_HIDDEN
    position = jnp.arange(TOKENS, dtype=jnp.int32)
    live = position % SEQ < lengths[(position // SEQ).astype(jnp.int32)]
    chosen = assignment[:, 0].astype(jnp.int32)
    onehot = ((chosen[:, None] == jnp.arange(EXPERTS, dtype=jnp.int32)[None, :]) & live[:, None]).astype(jnp.int32)
    blocks = onehot.reshape(devices, TOK_DEV, EXPERTS)
    before = jnp.cumsum(blocks, axis=1) - blocks
    rank = lax.optimization_barrier(jnp.sum(before * blocks, axis=2)).reshape(TOKENS).astype(jnp.int32)
    target = jnp.where(live, chosen * CAP + rank, EXPERTS * CAP).astype(jnp.int32)
    home = (position // TOK_DEV).astype(jnp.int32)
    return (live, chosen, onehot, home, target)

def reference(tokens, assignment, lengths, centroids, ln_gain, ln_bias, w_in, b_in, w_out, b_out, cotangent):
    devices = N_EXPERT * N_HIDDEN
    live, chosen, onehot, home, target = slots_of(assignment, lengths)
    livef = live.astype(jnp.float32)

    def forward(inputs, centres, gain, shift, weight_in, bias_in, weight_out, bias_out):
        sent = low_back(inputs)
        buffer = jnp.zeros((devices, EXPERTS * CAP, D), jnp.float32).at[home, target].add(sent, mode='drop')
        buffer = buffer.reshape(devices, EXPERTS, CAP, D).transpose(1, 0, 2, 3).reshape(EXPERTS, devices * CAP, D)

        def one_expert(packed):
            return jax.checkpoint(expert_apply)(*packed)
        results = lax.map(one_expert, (buffer, gain, shift, weight_in, bias_in, weight_out, bias_out))
        results = results.reshape(EXPERTS, devices, CAP, D).transpose(1, 0, 2, 3).reshape(devices, EXPERTS * CAP, D)
        branch = results.at[home, target].get(mode='fill', fill_value=0.0)
        score = lax.optimization_barrier(jnp.sum(inputs * centres[chosen], axis=1))
        gate = jax.nn.sigmoid(score) * livef
        return (inputs + gate[:, None] * branch, gate)
    primals = (tokens.astype(jnp.float32), centroids.astype(jnp.float32), ln_gain, ln_bias, w_in.astype(jnp.float32), b_in, w_out.astype(jnp.float32), b_out)
    mixed, pullback, gate = jax.vjp(forward, *primals, has_aux=True)
    grads = pullback(cotangent.astype(jnp.float32))
    hot = onehot.astype(jnp.float32)
    gate_sum = lax.optimization_barrier(jnp.sum(hot * gate[:, None], axis=0))
    count = lax.optimization_barrier(jnp.sum(hot, axis=0))
    mean_gate = gate_sum / jnp.maximum(count, 1.0)
    return (mixed.astype(jnp.bfloat16), grads[0].astype(jnp.bfloat16), grads[1], grads[2], grads[3], grads[4], grads[5], grads[6], grads[7], mean_gate)
```

```python
import functools

import jax
import jax.numpy as jnp
from jax import lax
from jax.experimental import pallas as pl
from jax.experimental.pallas import tpu as pltpu
from jax.sharding import PartitionSpec as P

EPS = 1e-05
MESH = pl.DeviceIdType.MESH
F32 = jnp.float32
BF16 = jnp.bfloat16
TILE = 256
HALVES = 2
GELU_A = 0.7978845608028654
GELU_B = 0.044715


def contract(a, b, dims):
    return lax.dot_general(a, b, (dims, ((), ())), preferred_element_type=F32)


def iota(shape, axis):
    return lax.broadcasted_iota(jnp.int32, shape, axis)


def exchange_kernel(
    dims,
    tok, cot, asg, lens, cent, gain, bias, bout, bin_, win, wout,
    o_gat, o_act, o_pg, o_ret, o_slot, o_small, o_bg, o_mean,
    vwin, vwout, gat, act, pg, sbuf, rbuf, snd, rcv, rsnd, xg, pick, par, stats, zs, mg, grads, gbuf, fin,
    w_sem, par_s, par_r, zs_s, zs_r, mg_s, mg_r, gb_s, gb_r,
    disp_s, disp_r, ret_s, ret_r, gat_s, gat_r, red_s, red_r, out_sem,
):
    G, H, J, S, MSG, R, T, D, F, PW, seq_len = dims
    e, z = lax.axis_index("expert"), lax.axis_index("hidden")
    dtiles, ftiles = D // TILE, F // TILE
    DH = D // HALVES

    def cols(t, size=TILE):
        return pl.ds(pl.multiple_of(t * size, size), size)

    load_in = pltpu.make_async_copy(win, vwin, w_sem.at[0])
    load_out = pltpu.make_async_copy(wout, vwout, w_sem.at[1])
    load_in.start()
    load_out.start()

    barrier = pltpu.get_barrier_semaphore()
    for d in range(1, H):
        pl.semaphore_signal(barrier, inc=1, device_id=(e, (z + d) % H), device_id_type=MESH)
    for d in range(1, G):
        pl.semaphore_signal(barrier, inc=1, device_id=((e + d) % G, z), device_id_type=MESH)

    own_cols = cols(z, PW)
    par[pl.ds(0, J), own_cols] = gain[...]
    par[pl.ds(J, J), own_cols] = bias[...]
    par[pl.ds(2 * J, J), own_cols] = cent[...].astype(F32)
    par[pl.ds(3 * J, J), own_cols] = bout[...]

    expert = asg[...]
    place = (e * H + z) * T
    length = lens[place // seq_len]
    live = (place % seq_len + iota((T, 1), 0)) < length
    lane = iota((T, 128), 1)
    hot = ((expert == lane) & live).astype(F32)
    hot16 = hot.astype(BF16)
    earlier = (iota((T, T), 1) < iota((T, T), 0)).astype(F32).astype(BF16)
    before = contract(earlier, hot16, ((1,), (0,)))
    row_e = iota((1, 128), 1)
    group = lax.div(row_e, jnp.int32(J))
    inner = row_e - group * J
    base = (inner * (G * MSG) + group * MSG).astype(F32)
    slot = jnp.sum(hot * (before + base), axis=1, keepdims=True)
    slot = jnp.where(live, slot, -1.0)
    count_at = jnp.where(live, jnp.sum(hot * (base + 2.0 * S), axis=1, keepdims=True), -1.0)
    o_slot[...] = jnp.broadcast_to(slot, (T, 128))
    slot_i = slot.astype(jnp.int32)
    count_i = count_at.astype(jnp.int32)

    r = iota((R, G * MSG), 0)
    rk = jnp.floor((r.astype(F32) + 0.5) * (1.0 / S)).astype(jnp.int32)
    at = r + rk * (MSG - S)
    c = iota((R, G * MSG), 1)
    pick[pl.ds(0, R), :] = (c == at).astype(F32).astype(BF16)
    pick[pl.ds(R, R), :] = (c == at + S).astype(F32).astype(BF16)

    pl.semaphore_wait(barrier, (H - 1) + (G - 1))

    def par_copy(d, source):
        return pltpu.make_async_remote_copy(
            src_ref=par.at[:, cols(source, PW)], dst_ref=par.at[:, cols(source, PW)],
            send_sem=par_s.at[d], recv_sem=par_r.at[d],
            device_id=(e, (z + d) % H), device_id_type=MESH)

    for d in range(1, H):
        par_copy(d, z).start()

    def msg(k):
        return pl.ds(pl.multiple_of(k * MSG, MSG), MSG)

    def disp_copy(j, d, target):
        return pltpu.make_async_remote_copy(
            src_ref=snd.at[j, msg(target)], dst_ref=rcv.at[j, msg(e)],
            send_sem=disp_s.at[j, d], recv_sem=disp_r.at[j, d],
            device_id=(target, z), device_id_type=MESH)

    def disp_in(j, d):
        k = (e - d + G) % G
        return pltpu.make_async_remote_copy(
            src_ref=snd.at[j, msg(k)], dst_ref=rcv.at[j, msg(k)],
            send_sem=disp_s.at[j, d], recv_sem=disp_r.at[j, d],
            device_id=((e + d) % G, z), device_id_type=MESH)

    for j in range(J):
        m = iota((T, G * MSG), 1) + j * (G * MSG)
        to_tok = (slot_i == m).astype(F32).astype(BF16)
        to_cot = ((slot_i + S == m) & (slot_i >= 0)).astype(F32).astype(BF16)
        to_count = (count_i == m).astype(F32).astype(BF16)

        def fill(t, _, j=j, to_tok=to_tok, to_cot=to_cot):
            v = contract(to_tok, tok[:, cols(t)], ((0,), (0,)))
            v = v + contract(to_cot, cot[:, cols(t)], ((0,), (0,)))
            snd[j, :, cols(t)] = v.astype(BF16)
            return 0

        lax.fori_loop(0, dtiles, fill, 0)
        counts = contract(to_count, jnp.ones((T, 128), BF16), ((0,), (0,)))
        snd[j, :, pl.ds(0, 128)] = (snd[j, :, pl.ds(0, 128)].astype(F32) + counts).astype(BF16)
        for d in range(1, G):
            disp_copy(j, d, (e + d) % G).start()
        rcv[j, msg(e), :] = snd[j, msg(e), :]

    for d in range(1, H):
        par_copy(d, (z - d + H) % H).wait_recv()

    def gat_copy(a, j, chunk, up):
        return pltpu.make_async_remote_copy(
            src_ref=gat.at[a, j, chunk], dst_ref=gat.at[a, j, chunk],
            send_sem=gat_s.at[up, a, j, chunk], recv_sem=gat_r.at[a, j, chunk],
            device_id=(e, jnp.clip(z + 2 * up - 1, 0, H - 1)), device_id_type=MESH)

    def send_gat(a, j, chunk, up):
        @pl.when(jnp.where(up == 1, z < H - 1, z > 0))
        def _():
            gat_copy(a, j, chunk, up).start()

    def red_copy(a, j, half, home, up):
        slot_to = jnp.where(jnp.logical_and(up == 1, home == z + 1), H, home)
        return pltpu.make_async_remote_copy(
            src_ref=sbuf.at[a, j, home, :, pl.ds(half * DH, DH)],
            dst_ref=rbuf.at[a, j, slot_to, :, pl.ds(half * DH, DH)],
            send_sem=red_s.at[a, j, half, home], recv_sem=red_r.at[a, j, half, slot_to],
            device_id=(e, jnp.clip(z + 2 * up - 1, 0, H - 1)), device_id_type=MESH)

    def red_in(a, j, half, slot_at):
        return pltpu.make_async_remote_copy(
            src_ref=sbuf.at[a, j, 0, :, pl.ds(half * DH, DH)],
            dst_ref=rbuf.at[a, j, slot_at, :, pl.ds(half * DH, DH)],
            send_sem=red_s.at[a, j, half, 0], recv_sem=red_r.at[a, j, half, slot_at],
            device_id=(e, jnp.clip(z + 1, 0, H - 1)), device_id_type=MESH)

    gate_sums = jnp.zeros((8, 128), F32)
    live_counts = jnp.zeros((8, 128), F32)
    lane8 = iota((8, 128), 1)
    for j in range(J):
        for d in range(1, G):
            disp_in(j, d).wait_recv()

        def unpack(t, _, j=j):
            xg[j, :, cols(t)] = contract(pick[...], rcv[j, :, cols(t)], ((1,), (0,))).astype(BF16)
            return 0

        lax.fori_loop(0, dtiles, unpack, 0)
        rr = iota((R, G * MSG), 0)
        rrk = jnp.floor((rr.astype(F32) + 0.5) * (1.0 / S)).astype(jnp.int32)
        pick_count = (iota((R, G * MSG), 1) == rrk * MSG + 2 * S).astype(F32).astype(BF16)
        count = contract(pick_count, rcv[j, :, pl.ds(0, 128)], ((1,), (0,)))[:, 0:1]
        r1 = iota((R, 1), 0).astype(F32)
        rank = r1 - S * jnp.floor((r1 + 0.5) * (1.0 / S))
        filled = rank < count

        x = xg[j, pl.ds(0, R), :].astype(F32)
        score = jnp.sum(x * par[pl.ds(2 * J + j, 1), :], axis=1, keepdims=True)
        gate = jax.nn.sigmoid(score)
        mean = jnp.mean(x, axis=1, keepdims=True)
        centered = x - mean
        var = jnp.mean(centered * centered, axis=1, keepdims=True)
        factor = lax.rsqrt(var + EPS)
        lifted = centered * factor * par[pl.ds(j, 1), :] + par[pl.ds(J + j, 1), :]
        gat[0, j, z] = lifted.astype(BF16)
        send_gat(0, j, z, 1)
        send_gat(0, j, z, 0)
        gat[1, j, z] = (gate * xg[j, pl.ds(R, R), :].astype(F32)).astype(BF16)
        send_gat(1, j, z, 1)
        send_gat(1, j, z, 0)
        stats[0, j] = gate
        stats[1, j] = mean
        stats[2, j] = factor
        kept = jnp.where(filled, gate, 0.0)
        total = jnp.sum(kept, axis=0, keepdims=True)
        number = jnp.sum(filled.astype(F32), axis=0, keepdims=True)
        gate_sums = gate_sums + jnp.where(lane8 == j, total, 0.0)
        live_counts = live_counts + jnp.where(lane8 == j, number, 0.0)

    zs[z, pl.ds(0, 8), :] = gate_sums
    zs[z, pl.ds(8, 8), :] = live_counts

    def zs_copy(d, source):
        return pltpu.make_async_remote_copy(
            src_ref=zs.at[source], dst_ref=zs.at[source],
            send_sem=zs_s.at[d], recv_sem=zs_r.at[d],
            device_id=(e, (z + d) % H), device_id_type=MESH)

    for d in range(1, H):
        zs_copy(d, z).start()

    load_in.wait()
    load_out.wait()
    o_bg[...] = jnp.zeros_like(o_bg)

    def compute(chunk, j):
        def first(t, _):
            lifted = gat[0, j, chunk]
            pre = contract(lifted, vwin[j, :, cols(t)], ((1,), (0,))) + bin_[pl.ds(j, 1), cols(t)]
            sq = pre * pre
            th = jnp.tanh(pre * (GELU_A + (GELU_A * GELU_B) * sq))
            cdf = 0.5 + 0.5 * th
            slope = cdf + pre * (0.5 - 0.5 * th * th) * (GELU_A + (3.0 * GELU_A * GELU_B) * sq)
            act[j, chunk, :, cols(t)] = (pre * cdf).astype(BF16)
            act_grad = contract(gat[1, j, chunk], vwout[j, cols(t), :], ((1,), (1,)))
            pre_grad = (act_grad * slope).astype(BF16)
            pg[j, chunk, :, cols(t)] = pre_grad
            o_bg[pl.ds(j, 1), cols(t)] += jnp.sum(pre_grad.astype(F32), axis=0, keepdims=True)
            return 0

        lax.fori_loop(0, ftiles, first, 0)

        def second(t, _):
            v = contract(act[j, chunk], vwout[j, :, cols(t)], ((1,), (0,)))
            sbuf[0, j, chunk, :, cols(t)] = v.astype(BF16)
            w = contract(pg[j, chunk], vwin[j, cols(t), :], ((1,), (1,)))
            sbuf[1, j, chunk, :, cols(t)] = w.astype(BF16)
            return 0

        lax.fori_loop(0, dtiles, second, 0)

    def item(q, _):
        s, j = q // J, q % J
        for up in (1, 0):
            chunk = z - s if up else z + s
            there = (chunk >= 0) if up else (chunk < H)

            @pl.when(jnp.logical_and(s > 0, there))
            def _(chunk=chunk, up=up):
                for a in range(2):
                    gat_copy(a, j, chunk, up).wait_recv()
                    send_gat(a, j, chunk, up)

        def side(d, _):
            chunk = jnp.where(d == 0, z - s, z + s)
            there = jnp.logical_and(jnp.logical_and(chunk >= 0, chunk < H), jnp.logical_or(s > 0, d == 0))

            @pl.when(there)
            def _():
                compute(jnp.clip(chunk, 0, H - 1), j)

                @pl.when(jnp.logical_and(s > 0, jnp.where(d == 0, z == H - 1, z == 0)))
                def _():
                    for a in range(2):
                        for half in range(HALVES):
                            red_copy(a, j, half, jnp.clip(chunk, 0, H - 1), d).start()

            return 0

        lax.fori_loop(0, 2, side, 0)

        @pl.when(s > 0)
        def _():
            for a in range(2):
                for half in range(HALVES):
                    for k in range(2):
                        up = (k + jnp.where(z >= H // 2, 0, 1)) % 2
                        home = jnp.where(up == 1, s, H - 1 - s)
                        passes = jnp.where(up == 1, jnp.logical_and(z > 0, z < home), jnp.logical_and(z < H - 1, z > home))

                        @pl.when(passes)
                        def _(a=a, half=half, up=up, home=home):
                            red_in(a, j, half, home).wait_recv()
                            at = (a, j, home, slice(None), pl.ds(half * DH, DH))
                            sbuf[at] = (sbuf[at].astype(F32) + rbuf[at].astype(F32)).astype(BF16)
                            red_copy(a, j, half, home, up).start()

        return 0

    lax.fori_loop(0, J, item, 0)

    for d in range(1, H):
        zs_copy(d, (z - d + H) % H).wait_recv()
    both = zs[0]
    for h in range(1, H):
        both = both + zs[h]
    mg[e] = both[0:8] / jnp.maximum(both[8:16], 1.0)

    def mg_copy(d, source):
        return pltpu.make_async_remote_copy(
            src_ref=mg.at[source], dst_ref=mg.at[source],
            send_sem=mg_s.at[d], recv_sem=mg_r.at[d],
            device_id=((e + d) % G, z), device_id_type=MESH)

    for d in range(1, G):
        mg_copy(d, e).start()

    lax.fori_loop(J, H * J, item, 0)

    outs = [
        pltpu.make_async_copy(gat, o_gat, out_sem.at[0]),
        pltpu.make_async_copy(act, o_act, out_sem.at[1]),
        pltpu.make_async_copy(pg, o_pg, out_sem.at[2]),
    ]
    for copy in outs:
        copy.start()

    def ret_copy(j, d, target):
        return pltpu.make_async_remote_copy(
            src_ref=rsnd.at[j, msg(target)], dst_ref=o_ret.at[j, msg(e)],
            send_sem=ret_s.at[j, d], recv_sem=ret_r.at[j, d],
            device_id=(target, z), device_id_type=MESH)

    def ret_in(j, d):
        k = (e - d + G) % G
        return pltpu.make_async_remote_copy(
            src_ref=rsnd.at[j, msg(k)], dst_ref=o_ret.at[j, msg(k)],
            send_sem=ret_s.at[j, d], recv_sem=ret_r.at[j, d],
            device_id=((e + d) % G, z), device_id_type=MESH)

    def ret_own(j):
        return pltpu.make_async_copy(rsnd.at[j, msg(e)], o_ret.at[j, msg(e)], out_sem.at[3 + j])

    for j in range(J):
        for half in range(HALVES):
            for a in range(2):
                at = (a, j, z, slice(None), pl.ds(half * DH, DH))
                low = (a, j, H, slice(None), pl.ds(half * DH, DH))
                to = (a, slice(None), pl.ds(half * DH, DH))
                fin[to] = sbuf[at].astype(F32)

                @pl.when(z < H - 1)
                def _(a=a, half=half, at=at, to=to):
                    red_in(a, j, half, z).wait_recv()
                    fin[to] += rbuf[at].astype(F32)

                @pl.when(z > 0)
                def _(a=a, half=half, low=low, to=to):
                    red_in(a, j, half, H).wait_recv()
                    fin[to] += rbuf[low].astype(F32)

        gate, mean, factor = stats[0, j], stats[1, j], stats[2, j]
        x = xg[j, pl.ds(0, R), :].astype(F32)
        g = xg[j, pl.ds(R, R), :].astype(F32)
        branch = (fin[0] + par[pl.ds(3 * J + j, 1), :]).astype(BF16).astype(F32)
        score_grad = jnp.sum(g * branch, axis=1, keepdims=True) * gate * (1.0 - gate)
        grads[pl.ds(2 * J + j, 1), :] = jnp.sum(score_grad * x, axis=0, keepdims=True)
        grads[pl.ds(3 * J + j, 1), :] = jnp.sum(gat[1, j, z].astype(F32), axis=0, keepdims=True)
        mixed = (x + gate * branch).astype(BF16)
        lifted_grad = fin[1]
        normed = (x - mean) * factor
        grads[pl.ds(j, 1), :] = jnp.sum(lifted_grad * normed, axis=0, keepdims=True)
        grads[pl.ds(J + j, 1), :] = jnp.sum(lifted_grad, axis=0, keepdims=True)
        n_grad = lifted_grad * par[pl.ds(j, 1), :]
        rows_grad = factor * (
            n_grad
            - jnp.mean(n_grad, axis=1, keepdims=True)
            - normed * jnp.mean(n_grad * normed, axis=1, keepdims=True)
        )
        rows_grad = rows_grad.astype(BF16).astype(F32)
        xg[j, pl.ds(0, R), :] = mixed
        xg[j, pl.ds(R, R), :] = (g + score_grad * par[pl.ds(2 * J + j, 1), :] + rows_grad).astype(BF16)

        def repack(t, _, j=j):
            rsnd[j, :, cols(t)] = contract(pick[...], xg[j, :, cols(t)], ((0,), (0,))).astype(BF16)
            return 0

        lax.fori_loop(0, dtiles, repack, 0)
        for d in range(1, G):
            ret_copy(j, d, (e + d) % G).start()
        ret_own(j).start()

    def gb_copy(d, source, target):
        return pltpu.make_async_remote_copy(
            src_ref=grads.at[:, cols(target, PW)], dst_ref=gbuf.at[source],
            send_sem=gb_s.at[d], recv_sem=gb_r.at[d],
            device_id=(e, (z + d) % H), device_id_type=MESH)

    for d in range(1, H):
        gb_copy(d, z, (z + d) % H).start()
    gbuf[z] = grads[:, own_cols]

    for d in range(1, G):
        mg_copy(d, (e - d + G) % G).wait_recv()
    means = jnp.zeros((8, 128), F32)
    for k in range(G):
        v = mg[k] if k == 0 else pltpu.roll(mg[k], k * J, 1)
        means = jnp.where((lane8 >= k * J) & (lane8 < k * J + J), v, means)
    o_mean[...] = means

    for d in range(1, H):
        gb_copy(d, (z - d + H) % H, z).wait_recv()
    small = gbuf[0]
    for h in range(1, H):
        small = small + gbuf[h]
    o_small[...] = small

    for j in range(J):
        for d in range(1, G):
            ret_in(j, d).wait_recv()
        ret_own(j).wait()
    for copy in outs:
        copy.wait()

    for d in range(1, H):
        par_copy(d, z).wait_send()
        zs_copy(d, z).wait_send()
        gb_copy(d, z, (z + d) % H).wait_send()
    for d in range(1, G):
        mg_copy(d, e).wait_send()
        for j in range(J):
            disp_copy(j, d, (e + d) % G).wait_send()
            ret_copy(j, d, (e + d) % G).wait_send()
    for a in range(2):
        for j in range(J):
            for h in range(H):

                @pl.when(jnp.logical_and(z < H - 1, h <= z))
                def _(a=a, j=j, h=h):
                    gat_copy(a, j, h, 1).wait_send()

                @pl.when(jnp.logical_and(z > 0, h >= z))
                def _(a=a, j=j, h=h):
                    gat_copy(a, j, h, 0).wait_send()

                @pl.when(h != z)
                def _(a=a, j=j, h=h):
                    for half in range(HALVES):
                        red_copy(a, j, half, h, jnp.where(h > z, 1, 0)).wait_send()


def local_kernel(
    dims,
    lift, pg, act, grad, ret, slot, tok, cot, small, bg, mean,
    o_mixed, o_tg, o_cent, o_gain, o_bias, o_win, o_bin, o_wout, o_bout, o_mean,
):
    G, H, J, S, MSG, R, T, D, F, PW, seq_len = dims
    o_win[0] = contract(lift[0, 0], pg[0], ((0,), (0,)))
    o_wout[0] = contract(act[0], grad[0, 0], ((0,), (0,)))

    first = jnp.logical_and(pl.program_id(0) == 0, pl.program_id(1) == 0)

    @pl.when(first)
    def _():
        o_gain[...] = small[pl.ds(0, J), :]
        o_bias[...] = small[pl.ds(J, J), :]
        o_cent[...] = small[pl.ds(2 * J, J), :]
        o_bout[...] = small[pl.ds(3 * J, J), :]
        o_bin[...] = bg[...]
        o_mean[...] = mean[pl.ds(0, 1), pl.ds(0, G * J)]
        spot = slot[:, 0:1].astype(jnp.int32)
        n = J * G * MSG
        m = iota((T, n), 1)
        live = spot >= 0
        to_mixed = (spot == m).astype(F32).astype(BF16)
        to_grad = ((spot + S == m) & live).astype(F32).astype(BF16)

        def place(t, _):
            at = pl.ds(pl.multiple_of(t * TILE, TILE), TILE)
            v = contract(to_mixed, ret[:, at], ((1,), (0,)))
            o_mixed[:, at] = jnp.where(live, v, tok[:, at].astype(F32)).astype(BF16)
            w = contract(to_grad, ret[:, at], ((1,), (0,)))
            o_tg[:, at] = jnp.where(live, w, cot[:, at].astype(F32)).astype(BF16)
            return 0

        lax.fori_loop(0, D // TILE, place, 0)


def on_device(
    tokens, assignment, lengths, centroids, ln_gain, ln_bias, w_in, b_in, w_out, b_out, cotangent
):
    T, D = tokens.shape
    G, H = lax.axis_size("expert"), lax.axis_size("hidden")
    J, F = w_in.shape[0], w_in.shape[2]
    PW = centroids.shape[1]
    S = max(2, 9 * T // (8 * J * G))
    MSG = -(-(2 * S + 1) // 16) * 16
    R = G * S
    seq_len = min(2048, H * T)
    dims = (G, H, J, S, MSG, R, T, D, F, PW, seq_len)
    vm = pl.BlockSpec(memory_space=pltpu.VMEM)
    hbm = pl.BlockSpec(memory_space=pl.ANY)
    sm = pl.BlockSpec(memory_space=pltpu.SMEM)
    dma = pltpu.SemaphoreType.DMA
    shape = jax.ShapeDtypeStruct
    gat, act, pg, ret, slot, small, bg, mean = pl.pallas_call(
        functools.partial(exchange_kernel, dims),
        name="exchange",
        out_shape=[
            shape((2, J, H, R, D), BF16),
            shape((J, H, R, F), BF16),
            shape((J, H, R, F), BF16),
            shape((J, G * MSG, D), BF16),
            shape((T, 128), F32),
            shape((4 * J, PW), F32),
            shape((J, F), F32),
            shape((8, 128), F32),
        ],
        in_specs=[vm, vm, vm, sm, vm, vm, vm, vm, vm, hbm, hbm],
        out_specs=[hbm, hbm, hbm, hbm, vm, vm, vm, vm],
        scratch_shapes=[
            pltpu.VMEM((J, D, F), BF16),
            pltpu.VMEM((J, F, D), BF16),
            pltpu.VMEM((2, J, H, R, D), BF16),
            pltpu.VMEM((J, H, R, F), BF16),
            pltpu.VMEM((J, H, R, F), BF16),
            pltpu.VMEM((2, J, H, R, D), BF16),
            pltpu.VMEM((2, J, H + 1, R, D), BF16),
            pltpu.VMEM((J, G * MSG, D), BF16),
            pltpu.VMEM((J, G * MSG, D), BF16),
            pltpu.VMEM((J, G * MSG, D), BF16),
            pltpu.VMEM((J, 2 * R, D), BF16),
            pltpu.VMEM((2 * R, G * MSG), BF16),
            pltpu.VMEM((4 * J, D), F32),
            pltpu.VMEM((3, J, R, 1), F32),
            pltpu.VMEM((H, 16, 128), F32),
            pltpu.VMEM((G, 8, 128), F32),
            pltpu.VMEM((4 * J, D), F32),
            pltpu.VMEM((H, 4 * J, PW), F32),
            pltpu.VMEM((2, R, D), F32),
            dma((2,)),
            dma((H,)), dma((H,)),
            dma((H,)), dma((H,)),
            dma((G,)), dma((G,)),
            dma((H,)), dma((H,)),
            dma((J, G)), dma((J, G)),
            dma((J, G)), dma((J, G)),
            dma((2, 2, J, H)), dma((2, J, H)),
            dma((2, J, HALVES, H)), dma((2, J, HALVES, H + 1)),
            dma((3 + J,)),
        ],
        compiler_params=pltpu.CompilerParams(
            collective_id=0, has_side_effects=True, vmem_limit_bytes=56 * 2**20
        ),
        cost_estimate=pl.CostEstimate(
            flops=16 * J * H * R * D * F // 2, bytes_accessed=30 * 2**20, transcendentals=J * H * R * F
        ),
    )(tokens, cotangent, assignment, lengths, centroids, ln_gain, ln_bias, b_out, b_in, w_in, w_out)

    N = H * R
    both = gat.reshape(2, J, N, D)
    full = lambda *shape: pl.BlockSpec(shape, lambda j, t: (0,) * len(shape))
    outs = pl.pallas_call(
        functools.partial(local_kernel, dims),
        name="gradients",
        grid=(J, F // TILE),
        out_shape=[
            shape((T, D), BF16),
            shape((T, D), BF16),
            shape((J, PW), F32),
            shape((J, PW), F32),
            shape((J, PW), F32),
            shape((J, D, F), F32),
            shape((J, F), F32),
            shape((J, F, D), F32),
            shape((J, PW), F32),
            shape((1, G * J), F32),
        ],
        in_specs=[
            pl.BlockSpec((1, 1, N, D), lambda j, t: (0, j, 0, 0)),
            pl.BlockSpec((1, N, TILE), lambda j, t: (j, 0, t)),
            pl.BlockSpec((1, N, TILE), lambda j, t: (j, 0, t)),
            pl.BlockSpec((1, 1, N, D), lambda j, t: (1, j, 0, 0)),
            full(J * G * MSG, D),
            full(T, 128),
            full(T, D),
            full(T, D),
            full(4 * J, PW),
            full(J, F),
            full(8, 128),
        ],
        out_specs=[
            full(T, D),
            full(T, D),
            full(J, PW),
            full(J, PW),
            full(J, PW),
            pl.BlockSpec((1, D, TILE), lambda j, t: (j, 0, t)),
            full(J, F),
            pl.BlockSpec((1, TILE, D), lambda j, t: (j, t, 0)),
            full(J, PW),
            full(1, G * J),
        ],
        compiler_params=pltpu.CompilerParams(
            dimension_semantics=("arbitrary", "arbitrary"), vmem_limit_bytes=48 * 2**20
        ),
        cost_estimate=pl.CostEstimate(
            flops=4 * J * N * D * F, bytes_accessed=28 * 2**20, transcendentals=0
        ),
    )(both, pg.reshape(J, N, F), act.reshape(J, N, F), both, ret.reshape(J * G * MSG, D), slot, tokens, cotangent, small, bg, mean)
    return (*outs[:9], outs[9].reshape(G * J))


def solution(mesh):
    tok = P(("expert", "hidden"), None)
    par = P("expert", "hidden")
    win = P("expert", None, "hidden")
    wout = P("expert", "hidden", None)
    return jax.shard_map(
        on_device,
        mesh=mesh,
        in_specs=(tok, tok, P(), par, par, par, win, par, wout, par, tok),
        out_specs=(tok, tok, par, par, par, win, par, wout, par, P()),
        check_vma=False,
    )
```

```python
import functools

import jax
import jax.numpy as jnp
from jax import lax
from jax.experimental import pallas as pl
from jax.experimental.pallas import tpu as pltpu
from jax.sharding import PartitionSpec as P

EPS = 1e-05
MESH = pl.DeviceIdType.MESH
F32 = jnp.float32
BF16 = jnp.bfloat16
TILE = 256
HALVES = 2
GELU_A = 0.7978845608028654
GELU_B = 0.044715
SHAPES = ((8, 8, 8, 8), (8, 7, 5, 4),)


def contract(a, b, dims=((1,), (0,))):
    return lax.dot_general(a, b, (dims, ((), ())), preferred_element_type=F32)


def iota(shape, axis):
    return lax.broadcasted_iota(jnp.int32, shape, axis)


def ones_where(mask):
    return mask.astype(F32).astype(BF16)


def per(index, size, count):
    return jnp.floor((index.astype(F32) + 0.5) * (1.0 / size)).astype(jnp.int32)


def exchange_kernel(
    dims, sizes,
    asg, lens, cent, gain, bias, bout, bin_, tok_in, cot_in, win, wout,
    o_gat, o_act, o_pg, o_ret, o_slot, o_small, o_bg, o_mean,
    tok, cot, vwin, vwout, gat, act, pg, sbuf, rbuf, snd, rcv, rsnd, xg, spread, pick, unpick, pick_count,
    par, stats, zs, mg, grads, gbuf, scores,
    w_sem, par_s, par_r, zs_s, zs_r, mg_s, mg_r, gb_s, gb_r,
    disp_s, disp_r, ret_s, ret_r, gat_s, gat_r, red_s, red_r, out_sem,
):
    G, H, J, S, MSG, R, T, D, F, PW, seq_len = dims
    e, z = lax.axis_index("expert"), lax.axis_index("hidden")
    E = G * J
    GM = G * MSG
    parts, ftiles = D // TILE, F // TILE
    DH = D // HALVES

    def cols(t, size=TILE):
        return pl.ds(pl.multiple_of(t * size, size), size)

    barrier = pltpu.get_barrier_semaphore()
    for d in range(1, H):
        pl.semaphore_signal(barrier, inc=1, device_id=(e, (z + d) % H), device_id_type=MESH)
    for d in range(1, G):
        pl.semaphore_signal(barrier, inc=1, device_id=((e + d) % G, z), device_id_type=MESH)

    loads = [
        pltpu.make_async_copy(a, b, w_sem.at[i])
        for i, (a, b) in enumerate(((tok_in, tok), (cot_in, cot), (win, vwin), (wout, vwout)))
    ]
    for copy in loads:
        copy.start()

    own_cols = cols(z, PW)
    par[pl.ds(0, J), own_cols] = gain[...]
    par[pl.ds(J, J), own_cols] = bias[...]
    par[pl.ds(2 * J, J), own_cols] = cent[...].astype(F32)
    par[pl.ds(3 * J, J), own_cols] = bout[...]

    expert = asg[...]
    place = (e * H + z) * T
    length = lens[place // seq_len]
    live = (place % seq_len + iota((1, T), 1)) < length
    sub_e = iota((E, 1), 0)
    hot = ((expert == sub_e) & live).astype(F32)
    earlier = ones_where(iota((T, T), 0) < iota((T, T), 1))
    before = contract(hot.astype(BF16), earlier)
    group = per(sub_e, J, G)
    inner = sub_e - group * J
    rank = jnp.sum(hot * before, axis=0, keepdims=True).astype(jnp.int32)
    to_group = jnp.sum(hot * group.astype(F32), axis=0, keepdims=True).astype(jnp.int32)
    to_inner = jnp.sum(hot * inner.astype(F32), axis=0, keepdims=True).astype(jnp.int32)
    to_inner = jnp.where(live, to_inner, -1)
    message = to_group * MSG
    o_slot[...] = jnp.broadcast_to(jnp.where(live, to_inner * GM + message + rank, -D * D), (8, T))

    pl.semaphore_wait(barrier, (H - 1) + (G - 1))

    def par_copy(d, source):
        return pltpu.make_async_remote_copy(
            src_ref=par.at[:, cols(source, PW)], dst_ref=par.at[:, cols(source, PW)],
            send_sem=par_s.at[d], recv_sem=par_r.at[d],
            device_id=(e, (z + d) % H), device_id_type=MESH)

    for d in range(1, H):
        par_copy(d, z).start()

    def msg(k):
        return pl.ds(pl.multiple_of(k * MSG, MSG), MSG)

    def disp_copy(j, a, d, target):
        return pltpu.make_async_remote_copy(
            src_ref=snd.at[j, a, msg(target)], dst_ref=rcv.at[j, a, msg(e)],
            send_sem=disp_s.at[j, a, d], recv_sem=disp_r.at[j, a, d],
            device_id=(target, z), device_id_type=MESH)

    def disp_in(j, a, d):
        k = (e - d + G) % G
        return pltpu.make_async_remote_copy(
            src_ref=snd.at[j, a, msg(k)], dst_ref=rcv.at[j, a, msg(k)],
            send_sem=disp_s.at[j, a, d], recv_sem=disp_r.at[j, a, d],
            device_id=((e + d) % G, z), device_id_type=MESH)

    for j in range(J):
        mine = to_inner == j
        at = jnp.where(mine, message + rank, -D * D)
        row = iota((GM, T), 0)
        for part in range(parts):
            spread[part] = ones_where(at + part * S == row)
        for a, source in enumerate((tok, cot)):
            if j == 0:
                loads[a].wait()
            v = contract(spread[0], source[:, pl.ds(0, TILE)])
            for part in range(1, parts):
                v = v + contract(spread[part], source[:, pl.ds(part * TILE, TILE)])
            if a == 0:
                to_count = ones_where(jnp.where(mine, message + parts * S, -1) == row)
                v = v + contract(to_count, jnp.ones((T, TILE), BF16))
            snd[j, a] = v.astype(BF16)
            for d in range(1, G):
                disp_copy(j, a, d, (e + d) % G).start()
            rcv[j, a, msg(e), :] = snd[j, a, msg(e), :]

    def row_of(c):
        k = per(c, MSG, G)
        start = jnp.full(c.shape, -D * D, jnp.int32)
        filled_before = jnp.int32(0)
        for i in range(G):
            first = (i * H + z) * T
            some = lens[first // seq_len] > first % seq_len
            start = jnp.where((k == i) & some, filled_before * S, start)
            filled_before = filled_before + some.astype(jnp.int32)
        return start, c - k * MSG

    start, within = row_of(iota((1, GM), 1))
    down = iota((R, GM), 0)
    for part in range(parts):
        i = within - part * S
        pick[part] = ones_where(jnp.where((i >= 0) & (i < S), start + i, -1) == down)
    counts_at = jnp.where(within == parts * S, start, -D * D)
    pick_count[...] = ones_where((down >= counts_at) & (down < counts_at + S))
    start, within = row_of(iota((GM, 1), 0))
    across = iota((GM, R), 1)
    for part in range(parts):
        i = within - part * S
        unpick[part] = ones_where(jnp.where((i >= 0) & (i < S), start + i, -1) == across)

    for h in range(H):
        if sizes[h] < R:
            gat[:, :, h, pl.ds(sizes[h], R - sizes[h]), :] = jnp.zeros((2, J, R - sizes[h], D), BF16)

    @pl.when(z == 0)
    def _():
        rbuf[:, :, H] = jnp.zeros((2, J, R, D), BF16)

    @pl.when(z == H - 1)
    def _():
        rbuf[:, :, H - 1] = jnp.zeros((2, J, R, D), BF16)

    o_bg[...] = jnp.zeros_like(o_bg)

    for d in range(1, H):
        par_copy(d, (z - d + H) % H).wait_recv()

    def with_rows(chunk, body):
        for size in sorted(set(sizes)):
            planes = [h for h in range(H) if sizes[h] == size]
            if len(planes) == H:
                body(size)
            else:
                hit = chunk == planes[0]
                for h in planes[1:]:
                    hit = jnp.logical_or(hit, chunk == h)
                pl.when(hit)(functools.partial(body, size))

    def gat_copy(a, j, chunk, up, size):
        return pltpu.make_async_remote_copy(
            src_ref=gat.at[a, j, chunk, pl.ds(0, size)], dst_ref=gat.at[a, j, chunk, pl.ds(0, size)],
            send_sem=gat_s.at[up, a, j, chunk], recv_sem=gat_r.at[a, j, chunk],
            device_id=(e, jnp.clip(z + 2 * up - 1, 0, H - 1)), device_id_type=MESH)

    def send_gat(a, j, chunk, up, size):
        @pl.when(jnp.where(up == 1, z < H - 1, z > 0))
        def _():
            gat_copy(a, j, chunk, up, size).start()

    def send_own(a, j):
        def both(size):
            send_gat(a, j, z, 1, size)
            send_gat(a, j, z, 0, size)

        with_rows(z, both)

    def red_copy(a, j, half, home, up, size):
        slot_to = jnp.where(jnp.logical_and(up == 1, home == z + 1), H, home)
        at = (pl.ds(0, size), pl.ds(half * DH, DH))
        return pltpu.make_async_remote_copy(
            src_ref=sbuf.at[(a, j, home, *at)], dst_ref=rbuf.at[(a, j, slot_to, *at)],
            send_sem=red_s.at[a, j, half, home], recv_sem=red_r.at[a, j, half, slot_to],
            device_id=(e, jnp.clip(z + 2 * up - 1, 0, H - 1)), device_id_type=MESH)

    def red_in(a, j, half, slot_at, size):
        at = (pl.ds(0, size), pl.ds(half * DH, DH))
        return pltpu.make_async_remote_copy(
            src_ref=sbuf.at[(a, j, 0, *at)], dst_ref=rbuf.at[(a, j, slot_at, *at)],
            send_sem=red_s.at[a, j, half, 0], recv_sem=red_r.at[a, j, half, slot_at],
            device_id=(e, jnp.clip(z + 1, 0, H - 1)), device_id_type=MESH)

    gate_sums = jnp.zeros((8, 128), F32)
    live_counts = jnp.zeros((8, 128), F32)
    lane8 = iota((8, 128), 1)
    r1 = iota((R, 1), 0)
    rank_in = r1 - S * per(r1, S, G)
    for j in range(J):
        for d in range(1, G):
            disp_in(j, 0, d).wait_recv()
        for part in range(parts):
            xg[j, 0, :, pl.ds(part * TILE, TILE)] = contract(pick[part], rcv[j, 0]).astype(BF16)
        count = contract(pick_count[...], rcv[j, 0, :, pl.ds(0, 128)])[:, 0:1]
        filled = rank_in.astype(F32) < count

        x = xg[j, 0].astype(F32)
        mean = jnp.mean(x, axis=1, keepdims=True)
        centered = x - mean
        var = jnp.mean(centered * centered, axis=1, keepdims=True)
        factor = lax.rsqrt(var + EPS)
        lifted = centered * factor * par[pl.ds(j, 1), :] + par[pl.ds(J + j, 1), :]
        gat[0, j, z] = lifted.astype(BF16)
        send_own(0, j)

        score = jnp.sum(x * par[pl.ds(2 * J + j, 1), :], axis=1, keepdims=True)
        gate = jax.nn.sigmoid(score)
        for d in range(1, G):
            disp_in(j, 1, d).wait_recv()
        for part in range(parts):
            at = pl.ds(part * TILE, TILE)
            g = contract(pick[part], rcv[j, 1])
            xg[j, 1, :, at] = g.astype(BF16)
            gat[1, j, z, :, at] = (gate * g).astype(BF16)
        send_own(1, j)
        stats[0, j] = gate
        stats[1, j] = mean
        stats[2, j] = factor
        stats[3, j] = filled.astype(F32)
        total = jnp.sum(jnp.where(filled, gate, 0.0), axis=0, keepdims=True)
        number = jnp.sum(filled.astype(F32), axis=0, keepdims=True)
        gate_sums = gate_sums + jnp.where(lane8 == j, total, 0.0)
        live_counts = live_counts + jnp.where(lane8 == j, number, 0.0)

    zs[z, pl.ds(0, 8), :] = gate_sums
    zs[z, pl.ds(8, 8), :] = live_counts

    def zs_copy(d, source):
        return pltpu.make_async_remote_copy(
            src_ref=zs.at[source], dst_ref=zs.at[source],
            send_sem=zs_s.at[d], recv_sem=zs_r.at[d],
            device_id=(e, (z + d) % H), device_id_type=MESH)

    for d in range(1, H):
        zs_copy(d, z).start()

    loads[2].wait()
    loads[3].wait()

    def compute(chunk, j):
        def first(t, _):
            pre = contract(gat[0, j, chunk], vwin[j, :, cols(t)]) + bin_[pl.ds(j, 1), cols(t)]
            sq = pre * pre
            th = jnp.tanh(pre * (GELU_A + (GELU_A * GELU_B) * sq))
            cdf = 0.5 + 0.5 * th
            slope = cdf + pre * (0.5 - 0.5 * th * th) * (GELU_A + (3.0 * GELU_A * GELU_B) * sq)
            act[j, chunk, :, cols(t)] = (pre * cdf).astype(BF16)
            act_grad = contract(gat[1, j, chunk], vwout[j, cols(t), :], ((1,), (1,)))
            pre_grad = (act_grad * slope).astype(BF16)
            pg[j, chunk, :, cols(t)] = pre_grad
            o_bg[pl.ds(j, 1), cols(t)] += jnp.sum(pre_grad.astype(F32), axis=0, keepdims=True)
            return 0

        lax.fori_loop(0, ftiles, first, 0)

        def second(t, _):
            v = contract(act[j, chunk], vwout[j, :, cols(t)])
            sbuf[0, j, chunk, :, cols(t)] = v.astype(BF16)
            w = contract(pg[j, chunk], vwin[j, cols(t), :], ((1,), (1,)))
            sbuf[1, j, chunk, :, cols(t)] = w.astype(BF16)
            return 0

        lax.fori_loop(0, parts, second, 0)

    def mg_copy(d, source):
        return pltpu.make_async_remote_copy(
            src_ref=mg.at[source], dst_ref=mg.at[source],
            send_sem=mg_s.at[d], recv_sem=mg_r.at[d],
            device_id=((e + d) % G, z), device_id_type=MESH)

    def gb_copy(d, source, target):
        return pltpu.make_async_remote_copy(
            src_ref=grads.at[:, cols(target, PW)], dst_ref=gbuf.at[source],
            send_sem=gb_s.at[d], recv_sem=gb_r.at[d],
            device_id=(e, (z + d) % H), device_id_type=MESH)

    outs = [
        pltpu.make_async_copy(gat, o_gat, out_sem.at[0]),
        pltpu.make_async_copy(act, o_act, out_sem.at[1]),
        pltpu.make_async_copy(pg, o_pg, out_sem.at[2]),
    ]

    def ret_copy(j, a, d, target):
        return pltpu.make_async_remote_copy(
            src_ref=rsnd.at[a, j, msg(target)], dst_ref=o_ret.at[a, j, msg(e)],
            send_sem=ret_s.at[j, a, d], recv_sem=ret_r.at[j, a, d],
            device_id=(target, z), device_id_type=MESH)

    def ret_in(j, a, d):
        k = (e - d + G) % G
        return pltpu.make_async_remote_copy(
            src_ref=rsnd.at[a, j, msg(k)], dst_ref=o_ret.at[a, j, msg(k)],
            send_sem=ret_s.at[j, a, d], recv_sem=ret_r.at[j, a, d],
            device_id=((e + d) % G, z), device_id_type=MESH)

    def ret_own(j, a):
        return pltpu.make_async_copy(rsnd.at[a, j, msg(e)], o_ret.at[a, j, msg(e)], out_sem.at[3 + 2 * j + a])

    def summed(a, j):
        for half in range(HALVES):
            @pl.when(z < H - 1)
            def _(half=half):
                with_rows(z, lambda size: red_in(a, j, half, z, size).wait_recv())

            @pl.when(z > 0)
            def _(half=half):
                with_rows(z, lambda size: red_in(a, j, half, H, size).wait_recv())

        v = sbuf[a, j, z].astype(F32) + rbuf[a, j, z].astype(F32) + rbuf[a, j, H].astype(F32)
        return jnp.where(stats[3, j] > 0.5, v, 0.0)

    def send_home(a, j):
        v = contract(unpick[0], xg[j, a, :, pl.ds(0, TILE)])
        for part in range(1, parts):
            v = v + contract(unpick[part], xg[j, a, :, pl.ds(part * TILE, TILE)])
        rsnd[a, j] = v.astype(BF16)
        for d in range(1, G):
            ret_copy(j, a, d, (e + d) % G).start()
        ret_own(j, a).start()

    def finish(j, _):
        gate, mean, factor = stats[0, j], stats[1, j], stats[2, j]
        branch = (summed(0, j) + par[pl.ds(3 * J + j, 1), :]).astype(BF16).astype(F32)
        x = xg[j, 0].astype(F32)
        score_grad = jnp.sum(xg[j, 1].astype(F32) * branch, axis=1, keepdims=True) * gate * (1.0 - gate)
        grads[pl.ds(2 * J + j, 1), :] = jnp.sum(score_grad * x, axis=0, keepdims=True)
        grads[pl.ds(3 * J + j, 1), :] = jnp.sum(gat[1, j, z].astype(F32), axis=0, keepdims=True)
        scores[j] = ((x - mean) * factor).astype(F32)
        xg[j, 0] = (x + gate * branch).astype(BF16)
        send_home(0, j)
        lifted_grad = summed(1, j)
        normed = scores[j]
        grads[pl.ds(j, 1), :] = jnp.sum(lifted_grad * normed, axis=0, keepdims=True)
        grads[pl.ds(J + j, 1), :] = jnp.sum(lifted_grad, axis=0, keepdims=True)
        n_grad = lifted_grad * par[pl.ds(j, 1), :]
        rows_grad = factor * (
            n_grad
            - jnp.mean(n_grad, axis=1, keepdims=True)
            - normed * jnp.mean(n_grad * normed, axis=1, keepdims=True)
        )
        rows_grad = rows_grad.astype(BF16).astype(F32)
        xg[j, 1] = (xg[j, 1].astype(F32) + score_grad * par[pl.ds(2 * J + j, 1), :] + rows_grad).astype(BF16)
        send_home(1, j)
        return 0

    last = jnp.maximum(z, H - 1 - z)

    def item(q, _):
        s, j = q // J, q % J
        for up in (1, 0):
            chunk = z - s if up else z + s
            there = (chunk >= 0) if up else (chunk < H)

            @pl.when(jnp.logical_and(s > 0, there))
            def _(chunk=chunk, up=up):
                for a in range(2):
                    def pass_on(size, a=a):
                        gat_copy(a, j, chunk, up, size).wait_recv()
                        send_gat(a, j, chunk, up, size)

                    with_rows(chunk, pass_on)

        def side(d, _):
            chunk = jnp.where(d == 0, z - s, z + s)
            there = jnp.logical_and(jnp.logical_and(chunk >= 0, chunk < H), jnp.logical_or(s > 0, d == 0))

            @pl.when(there)
            def _():
                home = jnp.clip(chunk, 0, H - 1)
                compute(home, j)

                @pl.when(jnp.logical_and(s > 0, jnp.where(d == 0, z == H - 1, z == 0)))
                def _():
                    def begin(size):
                        for a in range(2):
                            for half in range(HALVES):
                                red_copy(a, j, half, home, d, size).start()

                    with_rows(home, begin)

            return 0

        lax.fori_loop(0, 2, side, 0)

        @pl.when(s > 0)
        def _():
            for a in range(2):
                for half in range(HALVES):

                    def through(k, _, a=a, half=half):
                        up = (k + jnp.where(z >= H // 2, 0, 1)) % 2
                        home = jnp.where(up == 1, s, H - 1 - s)
                        passes = jnp.where(
                            up == 1, jnp.logical_and(z > 0, z < home), jnp.logical_and(z < H - 1, z > home)
                        )

                        @pl.when(passes)
                        def _():
                            def add(size):
                                red_in(a, j, half, home, size).wait_recv()
                                at = (a, j, home, pl.ds(0, size), pl.ds(half * DH, DH))
                                sbuf[at] = (sbuf[at].astype(F32) + rbuf[at].astype(F32)).astype(BF16)
                                red_copy(a, j, half, home, up, size).start()

                            with_rows(home, add)

                        return 0

                    lax.fori_loop(0, 2, through, 0)

        @pl.when(q == J - 1)
        def _():
            for d in range(1, H):
                zs_copy(d, (z - d + H) % H).wait_recv()
            both = zs[0]
            for h in range(1, H):
                both = both + zs[h]
            mg[e] = both[0:8] / jnp.maximum(both[8:16], 1.0)
            for d in range(1, G):
                mg_copy(d, e).start()

        @pl.when(jnp.logical_and(s == last, j == J - 1))
        def _():
            for copy in outs:
                copy.start()
            lax.fori_loop(0, J, finish, 0)
            for d in range(1, H):
                gb_copy(d, z, (z + d) % H).start()

        return 0

    lax.fori_loop(0, H * J, item, 0)

    gbuf[z] = grads[:, own_cols]
    for d in range(1, G):
        mg_copy(d, (e - d + G) % G).wait_recv()
    means = jnp.zeros((8, 128), F32)
    for k in range(G):
        v = mg[k] if k == 0 else pltpu.roll(mg[k], k * J, 1)
        means = jnp.where((lane8 >= k * J) & (lane8 < k * J + J), v, means)
    o_mean[...] = means

    for d in range(1, H):
        gb_copy(d, (z - d + H) % H, z).wait_recv()
    small = gbuf[0]
    for h in range(1, H):
        small = small + gbuf[h]
    o_small[...] = small

    for d in range(1, H):
        par_copy(d, z).wait_send()
        zs_copy(d, z).wait_send()
        gb_copy(d, z, (z + d) % H).wait_send()
    for d in range(1, G):
        mg_copy(d, e).wait_send()
        for j in range(J):
            for a in range(2):
                disp_copy(j, a, d, (e + d) % G).wait_send()

    def drain(i, _):
        a, j, h = i // (J * H), i // H % J, i % H

        def wait(size):
            @pl.when(jnp.logical_and(z < H - 1, h <= z))
            def _():
                gat_copy(a, j, h, 1, size).wait_send()

            @pl.when(jnp.logical_and(z > 0, h >= z))
            def _():
                gat_copy(a, j, h, 0, size).wait_send()

            @pl.when(h != z)
            def _():
                for half in range(HALVES):
                    red_copy(a, j, half, h, jnp.where(h > z, 1, 0), size).wait_send()

        with_rows(h, wait)
        return 0

    lax.fori_loop(0, 2 * J * H, drain, 0)
    for copy in outs:
        copy.wait()
    for j in range(J):
        for a in range(2):
            ret_own(j, a).wait()
            for d in range(1, G):
                ret_copy(j, a, d, (e + d) % G).wait_send()
                ret_in(j, a, d).wait_recv()


def local_kernel(
    dims,
    gat, pg, act, ret, slot, tok, cot, small, bg, mean,
    o_mixed, o_tg, o_cent, o_gain, o_bias, o_win, o_bin, o_wout, o_bout, o_mean,
    v_gat, v_pg, v_act, v_ret, v_tok, v_cot, turned, v_win, v_wout, v_mixed, v_tg, in_sem, out_sem,
):
    G, H, J, S, MSG, R, T, D, F, PW, seq_len = dims
    parts = D // TILE
    n = J * G * MSG
    loads = {}
    for j in range(J):
        for name, a, b in (
            ("lift", gat.at[0, j], v_gat.at[0, j]), ("pg", pg.at[j], v_pg.at[j]),
            ("act", act.at[j], v_act.at[j]), ("grad", gat.at[1, j], v_gat.at[1, j]),
        ):
            loads[name, j] = pltpu.make_async_copy(a, b, in_sem.at[len(loads)])
    for name, a, b in (("ret", ret, v_ret), ("tok", tok, v_tok), ("cot", cot, v_cot)):
        loads[name] = pltpu.make_async_copy(a, b, in_sem.at[len(loads)])
    for copy in loads.values():
        copy.start()

    o_gain[...] = small[pl.ds(0, J), :]
    o_bias[...] = small[pl.ds(J, J), :]
    o_cent[...] = small[pl.ds(2 * J, J), :]
    o_bout[...] = small[pl.ds(3 * J, J), :]
    o_bin[...] = bg[...]
    o_mean[...] = mean[pl.ds(0, 1), pl.ds(0, G * J)]

    stores = []

    def outer(left, right, where, to, width):
        turned[pl.ds(0, left.shape[1]), :] = jnp.transpose(left)

        def tile(t, _):
            at = pl.ds(pl.multiple_of(t * TILE, TILE), TILE)
            where[:, at] = contract(turned[pl.ds(0, left.shape[1]), :], right[:, at])
            return 0

        lax.fori_loop(0, width // TILE, tile, 0)
        stores.append(pltpu.make_async_copy(where, to, out_sem.at[len(stores)]))
        stores[-1].start()

    for j in range(J):
        loads["lift", j].wait()
        loads["pg", j].wait()
        outer(v_gat[0, j], v_pg.at[j], v_win.at[j], o_win.at[j], F)
        loads["act", j].wait()
        loads["grad", j].wait()
        outer(v_act[j], v_gat.at[1, j], v_wout.at[j], o_wout.at[j], D)

    for name in ("ret", "tok", "cot"):
        loads[name].wait()
    turned_slot = jnp.transpose(jnp.broadcast_to(slot[pl.ds(0, 1), :].astype(F32), (128, T)))
    spot = turned_slot[:, 0:1].astype(jnp.int32)
    live = spot >= 0
    m = iota((T, n), 1)
    for part in range(parts):
        at = pl.ds(part * TILE, TILE)
        take = ones_where(spot + part * S == m)
        v = contract(take, v_ret[0])
        v_mixed[:, at] = jnp.where(live, v, v_tok[:, at].astype(F32)).astype(BF16)
        w = contract(take, v_ret[1])
        v_tg[:, at] = jnp.where(live, w, v_cot[:, at].astype(F32)).astype(BF16)
    for a, b in ((v_mixed, o_mixed), (v_tg, o_tg)):
        stores.append(pltpu.make_async_copy(a, b, out_sem.at[len(stores)]))
        stores[-1].start()
    for copy in stores:
        copy.wait()


def on_device(
    tokens, assignment, lengths, centroids, ln_gain, ln_bias, w_in, b_in, w_out, b_out, cotangent
):
    T, D = tokens.shape
    G, H = lax.axis_size("expert"), lax.axis_size("hidden")
    J, F = w_in.shape[0], w_in.shape[2]
    PW = centroids.shape[1]
    S = max(2, 9 * T // (8 * J * G))
    parts = D // TILE
    MSG = -(-(parts * S + 1) // 16) * 16
    R, GM = G * S, G * MSG
    seq_len = min(2048, H * T)
    dims = (G, H, J, S, MSG, R, T, D, F, PW, seq_len)
    vm = pl.BlockSpec(memory_space=pltpu.VMEM)
    hbm = pl.BlockSpec(memory_space=pl.ANY)
    sm = pl.BlockSpec(memory_space=pltpu.SMEM)
    dma = pltpu.SemaphoreType.DMA
    shape = jax.ShapeDtypeStruct

    def exchange(number, sizes, *args):
        return pl.pallas_call(
            functools.partial(exchange_kernel, dims, sizes),
            name="exchange",
            out_shape=[
                shape((2, J, H, R, D), BF16),
                shape((J, H, R, F), BF16),
                shape((J, H, R, F), BF16),
                shape((2, J, GM, TILE), BF16),
                shape((8, T), jnp.int32),
                shape((4 * J, PW), F32),
                shape((J, F), F32),
                shape((8, 128), F32),
            ],
            in_specs=[vm, sm, vm, vm, vm, vm, vm, hbm, hbm, hbm, hbm],
            out_specs=[hbm, hbm, hbm, hbm, vm, vm, vm, vm],
            scratch_shapes=[
                pltpu.VMEM((T, D), BF16),
                pltpu.VMEM((T, D), BF16),
                pltpu.VMEM((J, D, F), BF16),
                pltpu.VMEM((J, F, D), BF16),
                pltpu.VMEM((2, J, H, R, D), BF16),
                pltpu.VMEM((J, H, R, F), BF16),
                pltpu.VMEM((J, H, R, F), BF16),
                pltpu.VMEM((2, J, H, R, D), BF16),
                pltpu.VMEM((2, J, H + 1, R, D), BF16),
                pltpu.VMEM((J, 2, GM, TILE), BF16),
                pltpu.VMEM((J, 2, GM, TILE), BF16),
                pltpu.VMEM((2, J, GM, TILE), BF16),
                pltpu.VMEM((J, 2, R, D), BF16),
                pltpu.VMEM((parts, GM, T), BF16),
                pltpu.VMEM((parts, R, GM), BF16),
                pltpu.VMEM((parts, GM, R), BF16),
                pltpu.VMEM((R, GM), BF16),
                pltpu.VMEM((4 * J, D), F32),
                pltpu.VMEM((4, J, R, 1), F32),
                pltpu.VMEM((H, 16, 128), F32),
                pltpu.VMEM((G, 8, 128), F32),
                pltpu.VMEM((4 * J, D), F32),
                pltpu.VMEM((H, 4 * J, PW), F32),
                pltpu.VMEM((J, R, D), F32),
                dma((4,)),
                dma((H,)), dma((H,)),
                dma((H,)), dma((H,)),
                dma((G,)), dma((G,)),
                dma((H,)), dma((H,)),
                dma((J, 2, G)), dma((J, 2, G)),
                dma((J, 2, G)), dma((J, 2, G)),
                dma((2, 2, J, H)), dma((2, J, H)),
                dma((2, J, HALVES, H)), dma((2, J, HALVES, H + 1)),
                dma((3 + 2 * J,)),
            ],
            compiler_params=pltpu.CompilerParams(
                collective_id=number, has_side_effects=True, vmem_limit_bytes=60 * 2**20
            ),
            cost_estimate=pl.CostEstimate(
                flops=8 * J * H * R * D * F, bytes_accessed=30 * 2**20, transcendentals=J * H * R * F
            ),
        )(*args)

    args = (
        assignment.reshape(1, T), lengths, centroids, ln_gain, ln_bias, b_out, b_in, tokens, cotangent, w_in, w_out
    )
    options = []
    for shares in SHAPES:
        rows = [-(-G * shares[4 * h // H] // 8) * S for h in range(H)]
        options.append([-(-r // 16) * 16 for r in rows])
    if len(options) == 1:
        found = exchange(0, tuple(options[0]), *args)
    else:
        first = (jnp.arange(G, dtype=jnp.int32)[:, None] * H + jnp.arange(H, dtype=jnp.int32)[None, :]) * T
        needed = S * jnp.sum((lengths[first // seq_len] > first % seq_len).astype(jnp.int32), axis=0)
        fits = jnp.all(needed[None, :] <= jnp.asarray(options, jnp.int32), axis=1)
        which = jnp.max(jnp.where(fits, jnp.arange(len(options), dtype=jnp.int32), 0))
        def choose(low, high):
            if high - low == 1:
                return functools.partial(exchange, low, tuple(options[low]))
            middle = (low + high) // 2
            return lambda *args: lax.cond(which >= middle, choose(middle, high), choose(low, middle), *args)

        found = choose(0, len(options))(*args)
    gat, act, pg, ret, slot, small, bg, mean = found

    N = H * R
    outs = pl.pallas_call(
        functools.partial(local_kernel, dims),
        name="gradients",
        out_shape=[
            shape((T, D), BF16),
            shape((T, D), BF16),
            shape((J, PW), F32),
            shape((J, PW), F32),
            shape((J, PW), F32),
            shape((J, D, F), F32),
            shape((J, F), F32),
            shape((J, F, D), F32),
            shape((J, PW), F32),
            shape((1, G * J), F32),
        ],
        in_specs=[hbm, hbm, hbm, hbm, vm, hbm, hbm, vm, vm, vm],
        out_specs=[hbm, hbm, vm, vm, vm, hbm, vm, hbm, vm, vm],
        scratch_shapes=[
            pltpu.VMEM((2, J, N, D), BF16),
            pltpu.VMEM((J, N, F), BF16),
            pltpu.VMEM((J, N, F), BF16),
            pltpu.VMEM((2, J * GM, TILE), BF16),
            pltpu.VMEM((T, D), BF16),
            pltpu.VMEM((T, D), BF16),
            pltpu.VMEM((max(D, F), N), BF16),
            pltpu.VMEM((J, D, F), F32),
            pltpu.VMEM((J, F, D), F32),
            pltpu.VMEM((T, D), BF16),
            pltpu.VMEM((T, D), BF16),
            dma((4 * J + 3,)),
            dma((2 * J + 2,)),
        ],
        compiler_params=pltpu.CompilerParams(vmem_limit_bytes=60 * 2**20),
        cost_estimate=pl.CostEstimate(
            flops=4 * J * N * D * F, bytes_accessed=28 * 2**20, transcendentals=0
        ),
    )(
        gat.reshape(2, J, N, D), pg.reshape(J, N, F), act.reshape(J, N, F), ret.reshape(2, J * GM, TILE),
        slot, tokens, cotangent, small, bg, mean,
    )
    return (*outs[:9], outs[9].reshape(G * J))


def solution(mesh):
    tok = P(("expert", "hidden"), None)
    par = P("expert", "hidden")
    win = P("expert", None, "hidden")
    wout = P("expert", "hidden", None)
    return jax.shard_map(
        on_device,
        mesh=mesh,
        in_specs=(tok, tok, P(), par, par, par, win, par, wout, par, tok),
        out_specs=(tok, tok, par, par, par, win, par, wout, par, P()),
        check_vma=False,
    )
```

```python
import functools

import jax
import jax.numpy as jnp
from jax import lax
from jax.experimental import pallas as pl
from jax.experimental.pallas import tpu as pltpu
from jax.sharding import PartitionSpec as P

EPS = 1e-05
MESH = pl.DeviceIdType.MESH
F32 = jnp.float32
BF16 = jnp.bfloat16
TILE = 256
HALVES = 2
GELU_A = 0.7978845608028654
GELU_B = 0.044715
SHAPES = ((8, 8, 8, 8), (8, 7, 5, 4), (8, 6, 4, 3),)


def contract(a, b, dims=((1,), (0,))):
    return lax.dot_general(a, b, (dims, ((), ())), preferred_element_type=F32)


def iota(shape, axis):
    return lax.broadcasted_iota(jnp.int32, shape, axis)


def ones_where(mask):
    return mask.astype(F32).astype(BF16)


def per(index, size, count):
    return jnp.floor((index.astype(F32) + 0.5) * (1.0 / size)).astype(jnp.int32)


def layer_kernel(
    dims, sizes,
    asg, lens, cent, gain, bias, bout, bin_, tok_in, cot_in, win, wout,
    home, ret, o_slot, o_cent, o_gain, o_bias, o_win, o_bin, o_wout, o_bout, o_mean,
    vwin, vwout, gat, act, pg, sbuf, rbuf, snd, rcv, xg, spread, pick, unpick, pick_count,
    par, stats, zs, mg, grads, gbuf, normed_of, turned,
    w_sem, par_s, par_r, zs_s, zs_r, mg_s, mg_r, gb_s, gb_r,
    disp_s, disp_r, ret_s, ret_r, gat_s, gat_r, red_s, red_r,
):
    G, H, J, S, MSG, R, T, D, F, PW, seq_len = dims
    e, z = lax.axis_index("expert"), lax.axis_index("hidden")
    E, GM, N = G * J, G * MSG, H * R
    parts, ftiles = D // TILE, F // TILE
    BLOCK = R

    def cols(t, size=TILE):
        return pl.ds(pl.multiple_of(t * size, size), size)

    def rows(start, size):
        return pl.ds(pl.multiple_of(start, 16), size)

    def loop(count, body):
        def step(i, _):
            body(i)
            return 0

        lax.fori_loop(0, count, step, 0)

    barrier = pltpu.get_barrier_semaphore()
    for d in range(1, H):
        pl.semaphore_signal(barrier, inc=1, device_id=(e, (z + d) % H), device_id_type=MESH)
    for d in range(1, G):
        pl.semaphore_signal(barrier, inc=1, device_id=((e + d) % G, z), device_id_type=MESH)

    loads = []
    for a, source in enumerate((tok_in, cot_in)):
        for part in range(parts):
            loads.append(pltpu.make_async_copy(
                source.at[:, pl.ds(part * TILE, TILE)], home.at[a, pl.ds(part * T, T), :],
                w_sem.at[a * parts + part]))
    weights = [
        pltpu.make_async_copy(win, vwin, w_sem.at[2 * parts]),
        pltpu.make_async_copy(wout, vwout, w_sem.at[2 * parts + 1]),
    ]
    for copy in loads + weights:
        copy.start()

    own_cols = cols(z, PW)
    par[pl.ds(0, J), own_cols] = gain[...]
    par[pl.ds(J, J), own_cols] = bias[...]
    par[pl.ds(2 * J, J), own_cols] = cent[...].astype(F32)
    par[pl.ds(3 * J, J), own_cols] = bout[...]

    expert = asg[...]
    place = (e * H + z) * T
    length = lens[place // seq_len]
    live = (place % seq_len + iota((1, T), 1)) < length
    sub_e = iota((E, 1), 0)
    hot = ((expert == sub_e) & live).astype(F32)
    earlier = ones_where(iota((T, T), 0) < iota((T, T), 1))
    before = contract(hot.astype(BF16), earlier)
    group = per(sub_e, J, G)
    inner = sub_e - group * J
    rank = jnp.sum(hot * before, axis=0, keepdims=True).astype(jnp.int32)
    to_group = jnp.sum(hot * group.astype(F32), axis=0, keepdims=True).astype(jnp.int32)
    to_inner = jnp.sum(hot * inner.astype(F32), axis=0, keepdims=True).astype(jnp.int32)
    to_inner = jnp.where(live, to_inner, -1)
    message = to_group * MSG
    o_slot[...] = jnp.broadcast_to(jnp.where(live, to_inner * GM + message + rank, -D * D), (8, T))

    pl.semaphore_wait(barrier, (H - 1) + (G - 1))

    def par_copy(d, source):
        return pltpu.make_async_remote_copy(
            src_ref=par.at[:, cols(source, PW)], dst_ref=par.at[:, cols(source, PW)],
            send_sem=par_s.at[d], recv_sem=par_r.at[d],
            device_id=(e, (z + d) % H), device_id_type=MESH)

    for d in range(1, H):
        par_copy(d, z).start()

    def msg(k):
        return pl.ds(pl.multiple_of(k * MSG, MSG), MSG)

    def disp_copy(j, a, d, target):
        return pltpu.make_async_remote_copy(
            src_ref=snd.at[j, a, msg(target)], dst_ref=rcv.at[j, a, msg(e)],
            send_sem=disp_s.at[j, a, d], recv_sem=disp_r.at[j, a, d],
            device_id=(target, z), device_id_type=MESH)

    def disp_in(j, a, d):
        k = (e - d + G) % G
        return pltpu.make_async_remote_copy(
            src_ref=snd.at[j, a, msg(k)], dst_ref=rcv.at[j, a, msg(k)],
            send_sem=disp_s.at[j, a, d], recv_sem=disp_r.at[j, a, d],
            device_id=((e + d) % G, z), device_id_type=MESH)

    def dispatch(i):
        j, a = i // 2, i % 2
        row = iota((GM, T), 0)
        mine = to_inner == j

        @pl.when(a == 0)
        def _():
            at = jnp.where(mine, message + rank, -D * D)
            for part in range(parts):
                spread[:, pl.ds(part * T, T)] = ones_where(at + part * S == row)

        for b in range(2):
            @pl.when(jnp.logical_and(j == 0, a == b))
            def _(b=b):
                for copy in loads[b * parts:(b + 1) * parts]:
                    copy.wait()

        counted = jnp.where(mine & (a == 0), message + parts * S, -1)
        v = contract(spread[...], home[a]) + contract(ones_where(counted == row), jnp.ones((T, TILE), BF16))
        snd[j, a] = v.astype(BF16)
        for d in range(1, G):
            disp_copy(j, a, d, (e + d) % G).start()
        rcv[j, a, msg(e), :] = snd[j, a, msg(e), :]

    loop(2 * J, dispatch)

    def row_of(c):
        k = per(c, MSG, G)
        start = jnp.full(c.shape, -D * D, jnp.int32)
        filled_before = jnp.int32(0)
        for i in range(G):
            first = (i * H + z) * T
            some = lens[first // seq_len] > first % seq_len
            start = jnp.where((k == i) & some, filled_before * S, start)
            filled_before = filled_before + some.astype(jnp.int32)
        return start, c - k * MSG

    start, within = row_of(iota((1, GM), 1))
    down = iota((R, GM), 0)
    for part in range(parts):
        i = within - part * S
        pick[pl.ds(part * R, R), :] = ones_where(jnp.where((i >= 0) & (i < S), start + i, -1) == down)
    counts_at = jnp.where(within == parts * S, start, -D * D)
    pick_count[...] = ones_where((down >= counts_at) & (down < counts_at + S))
    start, within = row_of(iota((GM, 1), 0))
    across = iota((1, parts * R), 1)
    across_part = per(across, R, parts)
    i = within - across_part * S
    unpick[...] = ones_where((i >= 0) & (i < S) & (start + i == across - across_part * R))

    for h in range(H):
        if sizes[h] < R:
            gat[:, :, pl.ds(h * R + sizes[h], R - sizes[h]), :] = jnp.zeros((2, J, R - sizes[h], D), BF16)

    def clear(slot_at):
        def one(i):
            rbuf[i // J, i % J, slot_at] = jnp.zeros((R, D), BF16)

        loop(2 * J, one)

    pl.when(z == 0)(lambda: clear(H))
    pl.when(z == H - 1)(lambda: clear(H - 1))

    o_bin[...] = jnp.zeros_like(o_bin)

    for d in range(1, H):
        par_copy(d, (z - d + H) % H).wait_recv()

    def with_rows(chunk, body):
        for size in sorted(set(sizes)):
            planes = [h for h in range(H) if sizes[h] == size]
            if len(planes) == H:
                body(size)
            else:
                hit = chunk == planes[0]
                for h in planes[1:]:
                    hit = jnp.logical_or(hit, chunk == h)
                pl.when(hit)(functools.partial(body, size))

    def gat_copy(a, j, chunk, up, size):
        at = (a, j, rows(chunk * R, size))
        return pltpu.make_async_remote_copy(
            src_ref=gat.at[at], dst_ref=gat.at[at],
            send_sem=gat_s.at[up, a, j, chunk], recv_sem=gat_r.at[a, j, chunk],
            device_id=(e, jnp.clip(z + 2 * up - 1, 0, H - 1)), device_id_type=MESH)

    def send_gat(a, j, chunk, up, size):
        @pl.when(jnp.where(up == 1, z < H - 1, z > 0))
        def _():
            gat_copy(a, j, chunk, up, size).start()

    def send_own(a, j):
        def both(size):
            send_gat(a, j, z, 1, size)
            send_gat(a, j, z, 0, size)

        with_rows(z, both)

    def half_of(size, half):
        first = -(-size // 32) * 16
        return (0, first) if half == 0 else (first, size - first)

    def red_copy(a, j, half, to, up, size):
        slot_to = jnp.where(jnp.logical_and(up == 1, to == z + 1), H, to)
        at = pl.ds(*half_of(size, half))
        return pltpu.make_async_remote_copy(
            src_ref=sbuf.at[a, j, to, at], dst_ref=rbuf.at[a, j, slot_to, at],
            send_sem=red_s.at[a, j, half, to], recv_sem=red_r.at[a, j, half, slot_to],
            device_id=(e, jnp.clip(z + 2 * up - 1, 0, H - 1)), device_id_type=MESH)

    def red_in(a, j, half, slot_at, size):
        at = pl.ds(*half_of(size, half))
        return pltpu.make_async_remote_copy(
            src_ref=sbuf.at[a, j, 0, at], dst_ref=rbuf.at[a, j, slot_at, at],
            send_sem=red_s.at[a, j, half, 0], recv_sem=red_r.at[a, j, half, slot_at],
            device_id=(e, jnp.clip(z + 1, 0, H - 1)), device_id_type=MESH)

    def quarter(part, b):
        return pl.ds(pl.multiple_of(part * R + b * BLOCK, 16), BLOCK)

    lane8 = iota((8, 128), 1)
    r1 = iota((R, 1), 0)
    rank_in = (r1 - S * per(r1, S, G)).astype(F32)
    zs[z] = jnp.zeros((16, 128), F32)

    def take_in(j, a):
        for d in range(1, G):
            disp_in(j, a, d).wait_recv()
        xg[j, a] = contract(pick[...], rcv[j, a]).astype(BF16)

    def prepare(j):
        take_in(j, 0)
        count = contract(pick_count[...], rcv[j, 0, :, pl.ds(0, 128)])[:, 0:1]
        stats[3, j] = (rank_in < count).astype(F32)

        def block(b):
            x = [xg[j, 0, quarter(part, b), :].astype(F32) for part in range(parts)]
            mean = sum(jnp.sum(v, axis=1, keepdims=True) for v in x) * (1.0 / D)
            x_mid = [v - mean for v in x]
            var = sum(jnp.sum(v * v, axis=1, keepdims=True) for v in x_mid) * (1.0 / D)
            factor = lax.rsqrt(var + EPS)
            score = 0.0
            at = rows(b * BLOCK, BLOCK)
            for part in range(parts):
                lanes = pl.ds(part * TILE, TILE)
                normed = x_mid[part] * factor
                lifted = normed * par[pl.ds(j, 1), lanes] + par[pl.ds(J + j, 1), lanes]
                gat[0, j, rows(z * R + b * BLOCK, BLOCK), lanes] = lifted.astype(BF16)
                normed_of[j, at, lanes] = normed
                score = score + jnp.sum(x[part] * par[pl.ds(2 * J + j, 1), lanes], axis=1, keepdims=True)
            stats[0, j, at] = jax.nn.sigmoid(score)
            stats[1, j, at] = factor

        loop(R // BLOCK, block)
        send_own(0, j)
        take_in(j, 1)

        def weigh(b):
            at = rows(b * BLOCK, BLOCK)
            for part in range(parts):
                g = xg[j, 1, quarter(part, b), :].astype(F32)
                gat[1, j, rows(z * R + b * BLOCK, BLOCK), pl.ds(part * TILE, TILE)] = (stats[0, j, at] * g).astype(BF16)

        loop(R // BLOCK, weigh)
        send_own(1, j)
        total = jnp.sum(stats[3, j] * stats[0, j], axis=0, keepdims=True)
        number = jnp.sum(stats[3, j], axis=0, keepdims=True)
        zs[z, pl.ds(0, 8), :] += jnp.where(lane8 == j, total, 0.0)
        zs[z, pl.ds(8, 8), :] += jnp.where(lane8 == j, number, 0.0)

    loop(J, prepare)

    def zs_copy(d, source):
        return pltpu.make_async_remote_copy(
            src_ref=zs.at[source], dst_ref=zs.at[source],
            send_sem=zs_s.at[d], recv_sem=zs_r.at[d],
            device_id=(e, (z + d) % H), device_id_type=MESH)

    for d in range(1, H):
        zs_copy(d, z).start()

    for copy in weights:
        copy.wait()

    def compute(chunk, j):
        mine = rows(chunk * R, R)

        def first(t):
            pre = contract(gat[0, j, mine, :], vwin[j, :, cols(t)]) + bin_[pl.ds(j, 1), cols(t)]
            sq = pre * pre
            th = jnp.tanh(pre * (GELU_A + (GELU_A * GELU_B) * sq))
            cdf = 0.5 + 0.5 * th
            slope = cdf + pre * (0.5 - 0.5 * th * th) * (GELU_A + (3.0 * GELU_A * GELU_B) * sq)
            act[j, mine, cols(t)] = (pre * cdf).astype(BF16)
            act_grad = contract(gat[1, j, mine, :], vwout[j, cols(t), :], ((1,), (1,)))
            pre_grad = (act_grad * slope).astype(BF16)
            pg[j, mine, cols(t)] = pre_grad
            o_bin[pl.ds(j, 1), cols(t)] += jnp.sum(pre_grad.astype(F32), axis=0, keepdims=True)

        loop(ftiles, first)

        def second(t):
            v = contract(act[j, mine, :], vwout[j, :, cols(t)])
            sbuf[0, j, chunk, :, cols(t)] = v.astype(BF16)
            w = contract(pg[j, mine, :], vwin[j, cols(t), :], ((1,), (1,)))
            sbuf[1, j, chunk, :, cols(t)] = w.astype(BF16)

        loop(parts, second)

    def outer(left, right, to, tall, wide):
        turned[pl.ds(0, tall), :] = jnp.transpose(left)

        def tile(t):
            to[:, cols(t)] = contract(turned[pl.ds(0, tall), :], right[:, cols(t)])

        loop(wide // TILE, tile)

    def mg_copy(d, source):
        return pltpu.make_async_remote_copy(
            src_ref=mg.at[source], dst_ref=mg.at[source],
            send_sem=mg_s.at[d], recv_sem=mg_r.at[d],
            device_id=((e + d) % G, z), device_id_type=MESH)

    def gb_copy(d, source, target):
        return pltpu.make_async_remote_copy(
            src_ref=grads.at[:, cols(target, PW)], dst_ref=gbuf.at[source],
            send_sem=gb_s.at[d], recv_sem=gb_r.at[d],
            device_id=(e, (z + d) % H), device_id_type=MESH)

    def ret_copy(j, a, d, target):
        return pltpu.make_async_remote_copy(
            src_ref=snd.at[j, a, msg(target)], dst_ref=ret.at[a, rows(j * GM + e * MSG, MSG)],
            send_sem=ret_s.at[j, a, d], recv_sem=ret_r.at[j, a, d],
            device_id=(target, z), device_id_type=MESH)

    def ret_in(j, a, d):
        k = (e - d + G) % G
        return pltpu.make_async_remote_copy(
            src_ref=snd.at[j, a, msg(k)], dst_ref=ret.at[a, rows(j * GM + k * MSG, MSG)],
            send_sem=ret_s.at[j, a, d], recv_sem=ret_r.at[j, a, d],
            device_id=((e + d) % G, z), device_id_type=MESH)

    def wait_sums(a, j):
        def both(size):
            for half in range(HALVES):
                @pl.when(z < H - 1)
                def _(half=half):
                    red_in(a, j, half, z, size).wait_recv()

                @pl.when(z > 0)
                def _(half=half):
                    red_in(a, j, half, H, size).wait_recv()

        with_rows(z, both)

    def summed(a, j, b, part):
        at = (rows(b * BLOCK, BLOCK), pl.ds(part * TILE, TILE))
        v = sbuf[(a, j, z, *at)].astype(F32) + rbuf[(a, j, z, *at)].astype(F32) + rbuf[(a, j, H, *at)].astype(F32)
        return jnp.where(stats[3, j, at[0]] > 0.5, v, 0.0)

    def send_home(j, a):
        snd[j, a] = contract(unpick[...], xg[j, a]).astype(BF16)
        for d in range(1, G):
            ret_copy(j, a, d, (e + d) % G).start()
        ret[a, rows(j * GM + e * MSG, MSG), :] = snd[j, a, msg(e), :]

    def finish(j):
        wait_sums(0, j)

        def forward(b):
            at = rows(b * BLOCK, BLOCK)
            gate = stats[0, j, at]
            gate_grad = 0.0
            for part in range(parts):
                lanes = pl.ds(part * TILE, TILE)
                branch = (summed(0, j, b, part) + par[pl.ds(3 * J + j, 1), lanes]).astype(BF16).astype(F32)
                x = xg[j, 0, quarter(part, b), :].astype(F32)
                gate_grad = gate_grad + jnp.sum(
                    xg[j, 1, quarter(part, b), :].astype(F32) * branch, axis=1, keepdims=True)
                rbuf[0, j, H, at, lanes] = x.astype(BF16)
                xg[j, 0, quarter(part, b), :] = (x + gate * branch).astype(BF16)
            score_grad = gate_grad * gate * (1.0 - gate)
            stats[2, j, at] = score_grad
            for part in range(parts):
                lanes = pl.ds(part * TILE, TILE)
                x = rbuf[0, j, H, at, lanes].astype(F32)
                grads[pl.ds(2 * J + j, 1), lanes] += jnp.sum(score_grad * x, axis=0, keepdims=True)
                sent = gat[1, j, rows(z * R + b * BLOCK, BLOCK), lanes].astype(F32)
                grads[pl.ds(3 * J + j, 1), lanes] += jnp.sum(sent, axis=0, keepdims=True)

        loop(R // BLOCK, forward)
        send_home(j, 0)
        wait_sums(1, j)

        def backward(b):
            at = rows(b * BLOCK, BLOCK)
            factor, score_grad = stats[1, j, at], stats[2, j, at]
            sum_n, sum_nn = 0.0, 0.0
            n_grads = []
            for part in range(parts):
                lanes = pl.ds(part * TILE, TILE)
                lifted_grad = summed(1, j, b, part)
                normed = normed_of[j, at, lanes]
                grads[pl.ds(j, 1), lanes] += jnp.sum(lifted_grad * normed, axis=0, keepdims=True)
                grads[pl.ds(J + j, 1), lanes] += jnp.sum(lifted_grad, axis=0, keepdims=True)
                n_grad = lifted_grad * par[pl.ds(j, 1), lanes]
                sum_n = sum_n + jnp.sum(n_grad, axis=1, keepdims=True)
                sum_nn = sum_nn + jnp.sum(n_grad * normed, axis=1, keepdims=True)
                n_grads.append(n_grad)
            for part in range(parts):
                lanes = pl.ds(part * TILE, TILE)
                rows_grad = factor * (
                    n_grads[part] - sum_n * (1.0 / D) - normed_of[j, at, lanes] * (sum_nn * (1.0 / D)))
                rows_grad = rows_grad.astype(BF16).astype(F32)
                g = xg[j, 1, quarter(part, b), :].astype(F32)
                moved = g + score_grad * par[pl.ds(2 * J + j, 1), lanes] + rows_grad
                xg[j, 1, quarter(part, b), :] = moved.astype(BF16)

        loop(R // BLOCK, backward)
        send_home(j, 1)

    last = jnp.maximum(z, H - 1 - z)
    grads[...] = jnp.zeros_like(grads)

    def sent(i):
        for d in range(1, G):
            disp_copy(i // 2, i % 2, d, (e + d) % G).wait_send()

    def starts(up):
        return jnp.where(up == 1, z == 0, z == H - 1)

    def passes(up, to):
        return jnp.where(up == 1, (z > 0) & (z < to), (z < H - 1) & (z > to))

    def begin(to, j, up):
        def both(size):
            for a in range(2):
                for half in range(HALVES):
                    red_copy(a, j, half, to, up, size).start()

        with_rows(to, both)

    def pass_sum(a, j, to, up):
        def both(size):
            for half in range(HALVES):
                red_in(a, j, half, to, size).wait_recv()
                at = (a, j, to, pl.ds(*half_of(size, half)))
                sbuf[at] = (sbuf[at].astype(F32) + rbuf[at].astype(F32)).astype(BF16)
                red_copy(a, j, half, to, up, size).start()

        with_rows(to, both)

    def item(q):
        s, j = q // J, q % J

        def forwarded(i):
            up, a = 1 - i // 2, i % 2
            chunk = jnp.where(up == 1, z - s, z + s)

            @pl.when((s > 0) & (chunk >= 0) & (chunk < H))
            def _():
                def pass_on(size):
                    gat_copy(a, j, chunk, up, size).wait_recv()
                    send_gat(a, j, chunk, up, size)

                with_rows(chunk, pass_on)

        loop(4, forwarded)

        def side(d):
            chunk = jnp.where(d == 0, z - s, z + s)

            @pl.when((chunk >= 0) & (chunk < H) & ((s > 0) | (d == 0)))
            def _():
                compute(chunk, j)

                @pl.when(starts(d) & (s > 0) & ((s > 1) | (j < J - 1)))
                def _():
                    begin(chunk, j, d)

        loop(2, side)

        early = (s == last + 1) & (s < H) & (j < J - 1)
        late = (s == H) & ((last == H - 1) | (j == J - 1))

        @pl.when((s == last + 1) & (j == 0))
        def _():
            loop(2 * J, sent)

        @pl.when(early | late)
        def _():
            finish(j)

        def through(i):
            a, up = i // 2, (i + jnp.where(z >= H // 2, 0, 1)) % 2
            to = jnp.where(up == 1, s, H - 1 - s)
            near = (to == z + 2 * up - 1) & (j == J - 1) & (s < H - 1)

            @pl.when((s > 0) & (s < H) & passes(up, to) & jnp.logical_not(near))
            def _():
                pass_sum(a, j, to, up)

        loop(4, through)

        @pl.when(q == H * J - 1)
        def _():
            for up in range(2):
                to = z + 2 * up - 1

                @pl.when(starts(up) & (to >= 0) & (to < H))
                def _(up=up, to=to):
                    begin(to, J - 1, up)

                @pl.when(passes(up, to) & (jnp.where(up == 1, to, H - 1 - to) < H - 1))
                def _(up=up, to=to):
                    loop(2, lambda a: pass_sum(a, J - 1, to, up))

        @pl.when(q == J - 1)
        def _():
            for d in range(1, H):
                zs_copy(d, (z - d + H) % H).wait_recv()
            both = zs[0]
            for h in range(1, H):
                both = both + zs[h]
            mg[e] = both[0:8] / jnp.maximum(both[8:16], 1.0)
            for d in range(1, G):
                mg_copy(d, e).start()

        @pl.when(s == last)
        def _():
            outer(gat[0, j], pg.at[j], o_win.at[j], D, F)
            outer(act[j], gat.at[1, j], o_wout.at[j], F, D)

    loop((H + 1) * J, item)
    for d in range(1, H):
        gb_copy(d, z, (z + d) % H).start()

    gbuf[z] = grads[:, own_cols]
    for d in range(1, G):
        mg_copy(d, (e - d + G) % G).wait_recv()
    means = jnp.zeros((8, 128), F32)
    for k in range(G):
        v = mg[k] if k == 0 else pltpu.roll(mg[k], k * J, 1)
        means = jnp.where((lane8 >= k * J) & (lane8 < k * J + J), v, means)
    o_mean[...] = means[0:1, 0:E]

    for d in range(1, H):
        gb_copy(d, (z - d + H) % H, z).wait_recv()
    small = gbuf[0]
    for h in range(1, H):
        small = small + gbuf[h]
    o_gain[...] = small[0:J]
    o_bias[...] = small[J:2 * J]
    o_cent[...] = small[2 * J:3 * J]
    o_bout[...] = small[3 * J:4 * J]

    for d in range(1, H):
        par_copy(d, z).wait_send()
        zs_copy(d, z).wait_send()
        gb_copy(d, z, (z + d) % H).wait_send()
    for d in range(1, G):
        mg_copy(d, e).wait_send()

    def drain(i):
        a, j, h = i // (J * H), i // H % J, i % H

        def wait(size):
            @pl.when((z < H - 1) & (h <= z))
            def _():
                gat_copy(a, j, h, 1, size).wait_send()

            @pl.when((z > 0) & (h >= z))
            def _():
                gat_copy(a, j, h, 0, size).wait_send()

            @pl.when(h != z)
            def _():
                for half in range(HALVES):
                    red_copy(a, j, half, h, jnp.where(h > z, 1, 0), size).wait_send()

        with_rows(h, wait)

    loop(2 * J * H, drain)

    def arrived(i):
        j, a = i // 2, i % 2
        for d in range(1, G):
            ret_in(j, a, d).wait_recv()
            ret_copy(j, a, d, (e + d) % G).wait_send()

    loop(2 * J, arrived)


def deliver_kernel(dims, home, ret, slot, *refs):
    G, H, J, S, MSG, R, T, D, F, PW, seq_len = dims
    results, (o_mixed, o_tg, *outs), (mixed, moved, sem) = refs[:8], refs[8:18], refs[18:]
    copies = [pltpu.make_async_copy(a, b, sem.at[i]) for i, (a, b) in enumerate(zip(results, outs))]
    for i in (3, 5, 0, 1, 2, 4, 6, 7):
        copies[i].start()

    spot = jnp.transpose(jnp.broadcast_to(slot[pl.ds(0, 1), :].astype(F32), (128, T)))[:, 0:1].astype(jnp.int32)
    live_rows = spot >= 0
    m = iota((T, J * G * MSG), 1)
    for part in range(D // TILE):
        take = ones_where(spot + part * S == m)
        at = pl.ds(part * TILE, TILE)
        for a, to in enumerate((mixed, moved)):
            kept = home[a, pl.ds(part * T, T), :].astype(F32)
            to[:, at] = jnp.where(live_rows, contract(take, ret[a]), kept).astype(BF16)
    for i, (a, b) in enumerate(((mixed, o_mixed), (moved, o_tg))):
        copies.append(pltpu.make_async_copy(a, b, sem.at[8 + i]))
        copies[-1].start()
    for copy in copies:
        copy.wait()


def on_device(
    tokens, assignment, lengths, centroids, ln_gain, ln_bias, w_in, b_in, w_out, b_out, cotangent
):
    T, D = tokens.shape
    G, H = lax.axis_size("expert"), lax.axis_size("hidden")
    J, F = w_in.shape[0], w_in.shape[2]
    PW = centroids.shape[1]
    S = max(2, 9 * T // (8 * J * G))
    parts = D // TILE
    MSG = -(-(parts * S + 1) // 16) * 16
    R, GM, N = G * S, G * MSG, H * G * S
    seq_len = min(2048, H * T)
    dims = (G, H, J, S, MSG, R, T, D, F, PW, seq_len)
    vm = pl.BlockSpec(memory_space=pltpu.VMEM)
    hbm = pl.BlockSpec(memory_space=pl.ANY)
    sm = pl.BlockSpec(memory_space=pltpu.SMEM)
    dma = pltpu.SemaphoreType.DMA
    buffers = [
        ((J, D, F), BF16),
        ((J, F, D), BF16),
        ((2, J, N, D), BF16),
        ((J, N, F), BF16),
        ((J, N, F), BF16),
        ((2, J, H, R, D), BF16),
        ((2, J, H + 1, R, D), BF16),
        ((J, 2, GM, TILE), BF16),
        ((J, 2, GM, TILE), BF16),
        ((J, 2, parts * R, TILE), BF16),
        ((GM, parts * T), BF16),
        ((parts * R, GM), BF16),
        ((GM, parts * R), BF16),
        ((R, GM), BF16),
        ((4 * J, D), F32),
        ((4, J, R, 1), F32),
        ((H, 16, 128), F32),
        ((G, 8, 128), F32),
        ((4 * J, D), F32),
        ((H, 4 * J, PW), F32),
        ((J, R, D), F32),
        ((max(D, F), N), BF16),
    ]
    taken = sum(
        jnp.dtype(t).itemsize * -(-s[-1] // 128) * 128 * functools.reduce(lambda a, b: a * b, s[:-1]) for s, t in buffers
    )

    results = [(J, PW), (J, PW), (J, PW), (J, D, F), (J, F), (J, F, D), (J, PW), (1, G * J)]
    shape = jax.ShapeDtypeStruct

    def layer(number, sizes, *args):
        made = pl.pallas_call(
            functools.partial(layer_kernel, dims, sizes),
            name="layer",
            out_shape=[
                pltpu.VMEM((2, parts * T, TILE), BF16),
                pltpu.VMEM((2, J * GM, TILE), BF16),
                pltpu.VMEM((8, T), jnp.int32),
                *[pltpu.VMEM(s, F32) for s in results],
            ],
            in_specs=[vm, sm, vm, vm, vm, vm, vm, hbm, hbm, hbm, hbm],
            out_specs=[vm] * 11,
            scratch_shapes=[
                *[pltpu.VMEM(s, t) for s, t in buffers],
                dma((2 * parts + 2,)),
                dma((H,)), dma((H,)),
                dma((H,)), dma((H,)),
                dma((G,)), dma((G,)),
                dma((H,)), dma((H,)),
                dma((J, 2, G)), dma((J, 2, G)),
                dma((J, 2, G)), dma((J, 2, G)),
                dma((2, 2, J, H)), dma((2, J, H)),
                dma((2, J, HALVES, H)), dma((2, J, HALVES, H + 1)),
            ],
            compiler_params=pltpu.CompilerParams(
                collective_id=number, has_side_effects=True, vmem_limit_bytes=taken + 3 * 2**20
            ),
            cost_estimate=pl.CostEstimate(
                flops=12 * J * N * D * F, bytes_accessed=30 * 2**20, transcendentals=J * N * F
            ),
        )(*args)
        return pl.pallas_call(
            functools.partial(deliver_kernel, dims),
            name="deliver",
            out_shape=[shape((T, D), BF16), shape((T, D), BF16), *[shape(s, F32) for s in results]],
            in_specs=[vm] * 11,
            out_specs=[hbm] * 10,
            scratch_shapes=[pltpu.VMEM((T, D), BF16), pltpu.VMEM((T, D), BF16), dma((10,))],
            compiler_params=pltpu.CompilerParams(vmem_limit_bytes=8 * 2**20),
        )(*made)

    args = (
        assignment.reshape(1, T), lengths, centroids, ln_gain, ln_bias, b_out, b_in, tokens, cotangent, w_in, w_out
    )
    options = []
    for shares in SHAPES:
        needed = [-(-G * shares[4 * h // H] // 8) * S for h in range(H)]
        options.append(tuple(-(-r // 16) * 16 for r in needed))
    if len(options) > 1:
        first = (jnp.arange(G, dtype=jnp.int32)[:, None] * H + jnp.arange(H, dtype=jnp.int32)[None, :]) * T
        if seq_len == H * T:
            lengths_of = lengths[:, None]
        else:
            lengths_of = lengths[first // seq_len]
        needed = S * jnp.sum((lengths_of > first % seq_len).astype(jnp.int32), axis=0)
        fits = jnp.all(needed[None, :] <= jnp.asarray(options, jnp.int32), axis=1)
        which = jnp.max(jnp.where(fits, jnp.arange(len(options), dtype=jnp.int32), 0))

    def choose(low, high):
        if high - low == 1:
            return functools.partial(layer, low, options[low])
        middle = (low + high) // 2
        return lambda *args: lax.cond(which >= middle, choose(middle, high), choose(low, middle), *args)

    outs = choose(0, len(options))(*args)
    return (*outs[:9], outs[9].reshape(G * J))


def solution(mesh):
    tok = P(("expert", "hidden"), None)
    par = P("expert", "hidden")
    win = P("expert", None, "hidden")
    wout = P("expert", "hidden", None)
    return jax.shard_map(
        on_device,
        mesh=mesh,
        in_specs=(tok, tok, P(), par, par, par, win, par, wout, par, tok),
        out_specs=(tok, tok, par, par, par, win, par, wout, par, P()),
        check_vma=False,
    )
```

```python
import functools

import jax
import jax.numpy as jnp
from jax import lax
from jax.experimental import pallas as pl
from jax.experimental.pallas import tpu as pltpu
from jax.sharding import PartitionSpec as P

EPS = 1e-05
MESH = pl.DeviceIdType.MESH
F32 = jnp.float32
BF16 = jnp.bfloat16
TILE = 256
HALVES = 2
GELU_A = 0.7978845608028654
GELU_B = 0.044715
SHAPES = ((8, 8, 8, 8), (8, 7, 5, 4), (8, 6, 4, 3),)


def contract(a, b, dims=((1,), (0,))):
    return lax.dot_general(a, b, (dims, ((), ())), preferred_element_type=F32)


def iota(shape, axis):
    return lax.broadcasted_iota(jnp.int32, shape, axis)


def ones_where(mask):
    return mask.astype(F32).astype(BF16)


def per(index, size, count):
    return jnp.floor((index.astype(F32) + 0.5) * (1.0 / size)).astype(jnp.int32)


def layer_kernel(
    dims, sizes,
    asg, lens, cent, gain, bias, bout, bin_, tok_in, cot_in, win, wout,
    home, ret, o_slot, o_cent, o_gain, o_bias, o_win, o_bin, o_wout, o_bout, o_mean,
    vwin, vwout, gat, act, pg, sbuf, rbuf, snd, rcv, xg, spread, pick, unpick, pick_count,
    par, stats, zs, mg, grads, gbuf, normed_of, turned,
    w_sem, par_s, par_r, zs_s, zs_r, mg_s, mg_r, gb_s, gb_r,
    disp_s, disp_r, ret_s, ret_r, gat_s, gat_r, red_s, red_r,
):
    G, H, J, S, MSG, R, T, D, F, PW, seq_len = dims
    e, z = lax.axis_index("expert"), lax.axis_index("hidden")
    E, GM, N = G * J, G * MSG, H * R
    parts, ftiles = D // TILE, F // TILE
    BLOCK = R

    def cols(t, size=TILE):
        return pl.ds(pl.multiple_of(t * size, size), size)

    def rows(start, size):
        return pl.ds(pl.multiple_of(start, 16), size)

    def loop(count, body):
        def step(i, _):
            body(i)
            return 0

        lax.fori_loop(0, count, step, 0)

    barrier = pltpu.get_barrier_semaphore()
    for d in range(1, H):
        pl.semaphore_signal(barrier, inc=1, device_id=(e, (z + d) % H), device_id_type=MESH)
    for d in range(1, G):
        pl.semaphore_signal(barrier, inc=1, device_id=((e + d) % G, z), device_id_type=MESH)

    loads = []
    for a, source in enumerate((tok_in, cot_in)):
        for part in range(parts):
            loads.append(pltpu.make_async_copy(
                source.at[:, pl.ds(part * TILE, TILE)], home.at[a, pl.ds(part * T, T), :],
                w_sem.at[a * parts + part]))
    weights = [
        pltpu.make_async_copy(win, vwin, w_sem.at[2 * parts]),
        pltpu.make_async_copy(wout, vwout, w_sem.at[2 * parts + 1]),
    ]
    for copy in loads + weights:
        copy.start()

    own_cols = cols(z, PW)
    par[pl.ds(0, J), own_cols] = gain[...]
    par[pl.ds(J, J), own_cols] = bias[...]
    par[pl.ds(2 * J, J), own_cols] = cent[...].astype(F32)
    par[pl.ds(3 * J, J), own_cols] = bout[...]

    expert = asg[...]
    place = (e * H + z) * T
    length = lens[place // seq_len]
    live = (place % seq_len + iota((1, T), 1)) < length
    sub_e = iota((E, 1), 0)
    hot = ((expert == sub_e) & live).astype(F32)
    earlier = ones_where(iota((T, T), 0) < iota((T, T), 1))
    before = contract(hot.astype(BF16), earlier)
    group = per(sub_e, J, G)
    inner = sub_e - group * J
    rank = jnp.sum(hot * before, axis=0, keepdims=True).astype(jnp.int32)
    to_group = jnp.sum(hot * group.astype(F32), axis=0, keepdims=True).astype(jnp.int32)
    to_inner = jnp.sum(hot * inner.astype(F32), axis=0, keepdims=True).astype(jnp.int32)
    to_inner = jnp.where(live, to_inner, -1)
    message = to_group * MSG
    o_slot[...] = jnp.broadcast_to(jnp.where(live, to_inner * GM + message + rank, -D * D), (8, T))

    pl.semaphore_wait(barrier, (H - 1) + (G - 1))

    def par_copy(d, source):
        return pltpu.make_async_remote_copy(
            src_ref=par.at[:, cols(source, PW)], dst_ref=par.at[:, cols(source, PW)],
            send_sem=par_s.at[d], recv_sem=par_r.at[d],
            device_id=(e, (z + d) % H), device_id_type=MESH)

    for d in range(1, H):
        par_copy(d, z).start()

    def msg(k):
        return pl.ds(pl.multiple_of(k * MSG, MSG), MSG)

    def disp_copy(j, a, d, target):
        return pltpu.make_async_remote_copy(
            src_ref=snd.at[j, a, msg(target)], dst_ref=rcv.at[j, a, msg(e)],
            send_sem=disp_s.at[j, a, d], recv_sem=disp_r.at[j, a, d],
            device_id=(target, z), device_id_type=MESH)

    def disp_in(j, a, d):
        k = (e - d + G) % G
        return pltpu.make_async_remote_copy(
            src_ref=snd.at[j, a, msg(k)], dst_ref=rcv.at[j, a, msg(k)],
            send_sem=disp_s.at[j, a, d], recv_sem=disp_r.at[j, a, d],
            device_id=((e + d) % G, z), device_id_type=MESH)

    def dispatch(i):
        j, a = i // 2, i % 2
        row = iota((GM, T), 0)
        mine = to_inner == j

        @pl.when(a == 0)
        def _():
            at = jnp.where(mine, message + rank, -D * D)
            for part in range(parts):
                spread[:, pl.ds(part * T, T)] = ones_where(at + part * S == row)

        for b in range(2):
            @pl.when(jnp.logical_and(j == 0, a == b))
            def _(b=b):
                for copy in loads[b * parts:(b + 1) * parts]:
                    copy.wait()

        counted = jnp.where(mine & (a == 0), message + parts * S, -1)
        v = contract(spread[...], home[a]) + contract(ones_where(counted == row), jnp.ones((T, TILE), BF16))
        snd[j, a] = v.astype(BF16)
        for d in range(1, G):
            disp_copy(j, a, d, (e + d) % G).start()
        rcv[j, a, msg(e), :] = snd[j, a, msg(e), :]

    loop(2 * J, dispatch)

    def row_of(c):
        k = per(c, MSG, G)
        start = jnp.full(c.shape, -D * D, jnp.int32)
        filled_before = jnp.int32(0)
        for i in range(G):
            first = (i * H + z) * T
            some = lens[first // seq_len] > first % seq_len
            start = jnp.where((k == i) & some, filled_before * S, start)
            filled_before = filled_before + some.astype(jnp.int32)
        return start, c - k * MSG

    start, within = row_of(iota((1, GM), 1))
    down = iota((R, GM), 0)
    for part in range(parts):
        i = within - part * S
        pick[pl.ds(part * R, R), :] = ones_where(jnp.where((i >= 0) & (i < S), start + i, -1) == down)
    counts_at = jnp.where(within == parts * S, start, -D * D)
    pick_count[...] = ones_where((down >= counts_at) & (down < counts_at + S))
    start, within = row_of(iota((GM, 1), 0))
    across = iota((1, parts * R), 1)
    across_part = per(across, R, parts)
    i = within - across_part * S
    unpick[...] = ones_where((i >= 0) & (i < S) & (start + i == across - across_part * R))

    for h in range(H):
        if sizes[h] < R:
            gat[:, :, pl.ds(h * R + sizes[h], R - sizes[h]), :] = jnp.zeros((2, J, R - sizes[h], D), BF16)

    def clear(slot_at):
        def one(i):
            rbuf[i // J, i % J, slot_at] = jnp.zeros((R, D), BF16)

        loop(2 * J, one)

    pl.when(z == 0)(lambda: clear(H))
    pl.when(z == H - 1)(lambda: clear(H - 1))

    o_bin[...] = jnp.zeros_like(o_bin)

    for d in range(1, H):
        par_copy(d, (z - d + H) % H).wait_recv()

    def with_rows(chunk, body):
        for size in sorted(set(sizes)):
            planes = [h for h in range(H) if sizes[h] == size]
            if len(planes) == H:
                body(size)
            else:
                hit = chunk == planes[0]
                for h in planes[1:]:
                    hit = jnp.logical_or(hit, chunk == h)
                pl.when(hit)(functools.partial(body, size))

    def gat_copy(a, j, chunk, up, size):
        at = (a, j, rows(chunk * R, size))
        return pltpu.make_async_remote_copy(
            src_ref=gat.at[at], dst_ref=gat.at[at],
            send_sem=gat_s.at[up, a, j, chunk], recv_sem=gat_r.at[a, j, chunk],
            device_id=(e, jnp.clip(z + 2 * up - 1, 0, H - 1)), device_id_type=MESH)

    def send_gat(a, j, chunk, up, size):
        @pl.when(jnp.where(up == 1, z < H - 1, z > 0))
        def _():
            gat_copy(a, j, chunk, up, size).start()

    def send_own(a, j):
        def both(size):
            send_gat(a, j, z, 1, size)
            send_gat(a, j, z, 0, size)

        with_rows(z, both)

    def half_of(size, half):
        first = -(-size // 32) * 16
        return (0, first) if half == 0 else (first, size - first)

    def red_copy(a, j, half, to, up, size):
        slot_to = jnp.where(jnp.logical_and(up == 1, to == z + 1), H, to)
        at = pl.ds(*half_of(size, half))
        return pltpu.make_async_remote_copy(
            src_ref=sbuf.at[a, j, to, at], dst_ref=rbuf.at[a, j, slot_to, at],
            send_sem=red_s.at[a, j, half, to], recv_sem=red_r.at[a, j, half, slot_to],
            device_id=(e, jnp.clip(z + 2 * up - 1, 0, H - 1)), device_id_type=MESH)

    def red_in(a, j, half, slot_at, size):
        at = pl.ds(*half_of(size, half))
        return pltpu.make_async_remote_copy(
            src_ref=sbuf.at[a, j, 0, at], dst_ref=rbuf.at[a, j, slot_at, at],
            send_sem=red_s.at[a, j, half, 0], recv_sem=red_r.at[a, j, half, slot_at],
            device_id=(e, jnp.clip(z + 1, 0, H - 1)), device_id_type=MESH)

    def quarter(part, b):
        return pl.ds(pl.multiple_of(part * R + b * BLOCK, 16), BLOCK)

    lane8 = iota((8, 128), 1)
    r1 = iota((R, 1), 0)
    rank_in = (r1 - S * per(r1, S, G)).astype(F32)
    zs[z] = jnp.zeros((16, 128), F32)

    def take_in(j, a):
        for d in range(1, G):
            disp_in(j, a, d).wait_recv()
        xg[j, a] = contract(pick[...], rcv[j, a]).astype(BF16)

    def prepare(j):
        take_in(j, 0)
        count = contract(pick_count[...], rcv[j, 0, :, pl.ds(0, 128)])[:, 0:1]
        stats[3, j] = (rank_in < count).astype(F32)

        def block(b):
            x = [xg[j, 0, quarter(part, b), :].astype(F32) for part in range(parts)]
            mean = sum(jnp.sum(v, axis=1, keepdims=True) for v in x) * (1.0 / D)
            x_mid = [v - mean for v in x]
            var = sum(jnp.sum(v * v, axis=1, keepdims=True) for v in x_mid) * (1.0 / D)
            factor = lax.rsqrt(var + EPS)
            score = 0.0
            at = rows(b * BLOCK, BLOCK)
            for part in range(parts):
                lanes = pl.ds(part * TILE, TILE)
                normed = x_mid[part] * factor
                lifted = normed * par[pl.ds(j, 1), lanes] + par[pl.ds(J + j, 1), lanes]
                gat[0, j, rows(z * R + b * BLOCK, BLOCK), lanes] = lifted.astype(BF16)
                normed_of[j, at, lanes] = normed
                score = score + jnp.sum(x[part] * par[pl.ds(2 * J + j, 1), lanes], axis=1, keepdims=True)
            stats[0, j, at] = jax.nn.sigmoid(score)
            stats[1, j, at] = factor

        loop(R // BLOCK, block)
        send_own(0, j)
        take_in(j, 1)

        def weigh(b):
            at = rows(b * BLOCK, BLOCK)
            for part in range(parts):
                g = xg[j, 1, quarter(part, b), :].astype(F32)
                gat[1, j, rows(z * R + b * BLOCK, BLOCK), pl.ds(part * TILE, TILE)] = (stats[0, j, at] * g).astype(BF16)

        loop(R // BLOCK, weigh)
        send_own(1, j)
        total = jnp.sum(stats[3, j] * stats[0, j], axis=0, keepdims=True)
        number = jnp.sum(stats[3, j], axis=0, keepdims=True)
        zs[z, pl.ds(0, 8), :] += jnp.where(lane8 == j, total, 0.0)
        zs[z, pl.ds(8, 8), :] += jnp.where(lane8 == j, number, 0.0)

    loop(J, prepare)

    def zs_copy(d, source):
        return pltpu.make_async_remote_copy(
            src_ref=zs.at[source], dst_ref=zs.at[source],
            send_sem=zs_s.at[d], recv_sem=zs_r.at[d],
            device_id=(e, (z + d) % H), device_id_type=MESH)

    for d in range(1, H):
        zs_copy(d, z).start()

    for copy in weights:
        copy.wait()

    def compute(chunk, j):
        mine = rows(chunk * R, R)

        def first(t):
            pre = contract(gat[0, j, mine, :], vwin[j, :, cols(t)]) + bin_[pl.ds(j, 1), cols(t)]
            sq = pre * pre
            th = jnp.tanh(pre * (GELU_A + (GELU_A * GELU_B) * sq))
            cdf = 0.5 + 0.5 * th
            slope = cdf + pre * (0.5 - 0.5 * th * th) * (GELU_A + (3.0 * GELU_A * GELU_B) * sq)
            act[j, mine, cols(t)] = (pre * cdf).astype(BF16)
            act_grad = contract(gat[1, j, mine, :], vwout[j, cols(t), :], ((1,), (1,)))
            pre_grad = (act_grad * slope).astype(BF16)
            pg[j, mine, cols(t)] = pre_grad
            o_bin[pl.ds(j, 1), cols(t)] += jnp.sum(pre_grad.astype(F32), axis=0, keepdims=True)

        loop(ftiles, first)

        def second(t):
            v = contract(act[j, mine, :], vwout[j, :, cols(t)])
            sbuf[0, j, chunk, :, cols(t)] = v.astype(BF16)
            w = contract(pg[j, mine, :], vwin[j, cols(t), :], ((1,), (1,)))
            sbuf[1, j, chunk, :, cols(t)] = w.astype(BF16)

        loop(parts, second)

    def outer(left, right, to, tall, wide):
        turned[pl.ds(0, tall), :] = jnp.transpose(left)

        def tile(t):
            to[:, cols(t)] = contract(turned[pl.ds(0, tall), :], right[:, cols(t)])

        loop(wide // TILE, tile)

    def mg_copy(d, source):
        return pltpu.make_async_remote_copy(
            src_ref=mg.at[source], dst_ref=mg.at[source],
            send_sem=mg_s.at[d], recv_sem=mg_r.at[d],
            device_id=((e + d) % G, z), device_id_type=MESH)

    def gb_copy(d, source, target):
        return pltpu.make_async_remote_copy(
            src_ref=grads.at[:, cols(target, PW)], dst_ref=gbuf.at[source],
            send_sem=gb_s.at[d], recv_sem=gb_r.at[d],
            device_id=(e, (z + d) % H), device_id_type=MESH)

    def ret_copy(j, a, d, target):
        return pltpu.make_async_remote_copy(
            src_ref=snd.at[j, a, msg(target)], dst_ref=ret.at[a, rows(j * GM + e * MSG, MSG)],
            send_sem=ret_s.at[j, a, d], recv_sem=ret_r.at[j, a, d],
            device_id=(target, z), device_id_type=MESH)

    def ret_in(j, a, d):
        k = (e - d + G) % G
        return pltpu.make_async_remote_copy(
            src_ref=snd.at[j, a, msg(k)], dst_ref=ret.at[a, rows(j * GM + k * MSG, MSG)],
            send_sem=ret_s.at[j, a, d], recv_sem=ret_r.at[j, a, d],
            device_id=((e + d) % G, z), device_id_type=MESH)

    def wait_sums(a, j):
        def both(size):
            for half in range(HALVES):
                @pl.when(z < H - 1)
                def _(half=half):
                    red_in(a, j, half, z, size).wait_recv()

                @pl.when(z > 0)
                def _(half=half):
                    red_in(a, j, half, H, size).wait_recv()

        with_rows(z, both)

    def summed(a, j, b, part):
        at = (rows(b * BLOCK, BLOCK), pl.ds(part * TILE, TILE))
        v = sbuf[(a, j, z, *at)].astype(F32) + rbuf[(a, j, z, *at)].astype(F32) + rbuf[(a, j, H, *at)].astype(F32)
        return jnp.where(stats[3, j, at[0]] > 0.5, v, 0.0)

    def send_home(j, a):
        snd[j, a] = contract(unpick[...], xg[j, a]).astype(BF16)
        for d in range(1, G):
            ret_copy(j, a, d, (e + d) % G).start()
        ret[a, rows(j * GM + e * MSG, MSG), :] = snd[j, a, msg(e), :]

    def finish(j):
        wait_sums(0, j)

        def forward(b):
            at = rows(b * BLOCK, BLOCK)
            gate = stats[0, j, at]
            gate_grad = 0.0
            for part in range(parts):
                lanes = pl.ds(part * TILE, TILE)
                branch = (summed(0, j, b, part) + par[pl.ds(3 * J + j, 1), lanes]).astype(BF16).astype(F32)
                x = xg[j, 0, quarter(part, b), :].astype(F32)
                gate_grad = gate_grad + jnp.sum(
                    xg[j, 1, quarter(part, b), :].astype(F32) * branch, axis=1, keepdims=True)
                rbuf[0, j, H, at, lanes] = x.astype(BF16)
                xg[j, 0, quarter(part, b), :] = (x + gate * branch).astype(BF16)
            score_grad = gate_grad * gate * (1.0 - gate)
            stats[2, j, at] = score_grad
            for part in range(parts):
                lanes = pl.ds(part * TILE, TILE)
                x = rbuf[0, j, H, at, lanes].astype(F32)
                grads[pl.ds(2 * J + j, 1), lanes] += jnp.sum(score_grad * x, axis=0, keepdims=True)
                sent = gat[1, j, rows(z * R + b * BLOCK, BLOCK), lanes].astype(F32)
                grads[pl.ds(3 * J + j, 1), lanes] += jnp.sum(sent, axis=0, keepdims=True)

        loop(R // BLOCK, forward)
        send_home(j, 0)
        wait_sums(1, j)

        def backward(b):
            at = rows(b * BLOCK, BLOCK)
            factor, score_grad = stats[1, j, at], stats[2, j, at]
            sum_n, sum_nn = 0.0, 0.0
            n_grads = []
            for part in range(parts):
                lanes = pl.ds(part * TILE, TILE)
                lifted_grad = summed(1, j, b, part)
                normed = normed_of[j, at, lanes]
                grads[pl.ds(j, 1), lanes] += jnp.sum(lifted_grad * normed, axis=0, keepdims=True)
                grads[pl.ds(J + j, 1), lanes] += jnp.sum(lifted_grad, axis=0, keepdims=True)
                n_grad = lifted_grad * par[pl.ds(j, 1), lanes]
                sum_n = sum_n + jnp.sum(n_grad, axis=1, keepdims=True)
                sum_nn = sum_nn + jnp.sum(n_grad * normed, axis=1, keepdims=True)
                n_grads.append(n_grad)
            for part in range(parts):
                lanes = pl.ds(part * TILE, TILE)
                rows_grad = factor * (
                    n_grads[part] - sum_n * (1.0 / D) - normed_of[j, at, lanes] * (sum_nn * (1.0 / D)))
                rows_grad = rows_grad.astype(BF16).astype(F32)
                g = xg[j, 1, quarter(part, b), :].astype(F32)
                moved = g + score_grad * par[pl.ds(2 * J + j, 1), lanes] + rows_grad
                xg[j, 1, quarter(part, b), :] = moved.astype(BF16)

        loop(R // BLOCK, backward)
        send_home(j, 1)

    last = jnp.maximum(z, H - 1 - z)
    grads[...] = jnp.zeros_like(grads)

    def sent(i):
        for d in range(1, G):
            disp_copy(i // 2, i % 2, d, (e + d) % G).wait_send()

    def starts(up):
        return jnp.where(up == 1, z == 0, z == H - 1)

    def passes(up, to):
        return jnp.where(up == 1, (z > 0) & (z < to), (z < H - 1) & (z > to))

    def begin(to, j, up):
        def both(size):
            for a in range(2):
                for half in range(HALVES):
                    red_copy(a, j, half, to, up, size).start()

        with_rows(to, both)

    def pass_sum(a, j, to, up):
        def both(size):
            for half in range(HALVES):
                red_in(a, j, half, to, size).wait_recv()
                at = (a, j, to, pl.ds(*half_of(size, half)))
                sbuf[at] = (sbuf[at].astype(F32) + rbuf[at].astype(F32)).astype(BF16)
                red_copy(a, j, half, to, up, size).start()

        with_rows(to, both)

    def item(q):
        s, j = q // J, q % J

        def forwarded(i):
            up, a = 1 - i // 2, i % 2
            chunk = jnp.where(up == 1, z - s, z + s)

            @pl.when((s > 0) & (chunk >= 0) & (chunk < H))
            def _():
                def pass_on(size):
                    gat_copy(a, j, chunk, up, size).wait_recv()
                    send_gat(a, j, chunk, up, size)

                with_rows(chunk, pass_on)

        loop(4, forwarded)

        def side(d):
            chunk = jnp.where(d == 0, z - s, z + s)

            @pl.when((chunk >= 0) & (chunk < H) & ((s > 0) | (d == 0)))
            def _():
                compute(chunk, j)

                @pl.when(starts(d) & (s > 0) & ((s > 1) | (j < J - 1)))
                def _():
                    begin(chunk, j, d)

        loop(2, side)

        early = (s == last + 1) & (s < H) & (j < J - 1)
        late = (s == H) & ((last == H - 1) | (j == J - 1))

        @pl.when((s == last + 1) & (j == 0))
        def _():
            loop(2 * J, sent)

        @pl.when(early | late)
        def _():
            finish(j)

        def through(i):
            a, up = i // 2, (i + jnp.where(z >= H // 2, 0, 1)) % 2
            to = jnp.where(up == 1, s, H - 1 - s)
            near = (to == z + 2 * up - 1) & (j == J - 1) & (s < H - 1)

            @pl.when((s > 0) & (s < H) & passes(up, to) & jnp.logical_not(near))
            def _():
                pass_sum(a, j, to, up)

        loop(4, through)

        @pl.when(q == H * J - 1)
        def _():
            for up in range(2):
                to = z + 2 * up - 1

                @pl.when(starts(up) & (to >= 0) & (to < H))
                def _(up=up, to=to):
                    begin(to, J - 1, up)

                @pl.when(passes(up, to) & (jnp.where(up == 1, to, H - 1 - to) < H - 1))
                def _(up=up, to=to):
                    loop(2, lambda a: pass_sum(a, J - 1, to, up))

        @pl.when((s == last) & (j == 0))
        def _():
            for d in range(1, H):
                zs_copy(d, (z - d + H) % H).wait_recv()
            both = zs[0]
            for h in range(1, H):
                both = both + zs[h]
            mg[e] = both[0:8] / jnp.maximum(both[8:16], 1.0)
            for d in range(1, G):
                mg_copy(d, e).start()

        @pl.when(s == last)
        def _():
            outer(gat[0, j], pg.at[j], o_win.at[j], D, F)
            outer(act[j], gat.at[1, j], o_wout.at[j], F, D)

    loop((H + 1) * J, item)
    for d in range(1, H):
        gb_copy(d, z, (z + d) % H).start()

    gbuf[z] = grads[:, own_cols]
    for d in range(1, G):
        mg_copy(d, (e - d + G) % G).wait_recv()
    means = jnp.zeros((8, 128), F32)
    for k in range(G):
        v = mg[k] if k == 0 else pltpu.roll(mg[k], k * J, 1)
        means = jnp.where((lane8 >= k * J) & (lane8 < k * J + J), v, means)
    o_mean[...] = means[0:1, 0:E]

    for d in range(1, H):
        gb_copy(d, (z - d + H) % H, z).wait_recv()
    small = gbuf[0]
    for h in range(1, H):
        small = small + gbuf[h]
    o_gain[...] = small[0:J]
    o_bias[...] = small[J:2 * J]
    o_cent[...] = small[2 * J:3 * J]
    o_bout[...] = small[3 * J:4 * J]

    for d in range(1, H):
        par_copy(d, z).wait_send()
        zs_copy(d, z).wait_send()
        gb_copy(d, z, (z + d) % H).wait_send()
    for d in range(1, G):
        mg_copy(d, e).wait_send()

    def drain(i):
        a, j, h = i // (J * H), i // H % J, i % H

        def wait(size):
            @pl.when((z < H - 1) & (h <= z))
            def _():
                gat_copy(a, j, h, 1, size).wait_send()

            @pl.when((z > 0) & (h >= z))
            def _():
                gat_copy(a, j, h, 0, size).wait_send()

            @pl.when(h != z)
            def _():
                for half in range(HALVES):
                    red_copy(a, j, half, h, jnp.where(h > z, 1, 0), size).wait_send()

        with_rows(h, wait)

    loop(2 * J * H, drain)

    def arrived(i):
        j, a = i // 2, i % 2
        for d in range(1, G):
            ret_in(j, a, d).wait_recv()
            ret_copy(j, a, d, (e + d) % G).wait_send()

    loop(2 * J, arrived)


def deliver_kernel(dims, home, ret, slot, *refs):
    G, H, J, S, MSG, R, T, D, F, PW, seq_len = dims
    results, (o_mixed, o_tg, *outs), (mixed, moved, sem) = refs[:8], refs[8:18], refs[18:]
    copies = [pltpu.make_async_copy(a, b, sem.at[i]) for i, (a, b) in enumerate(zip(results, outs))]
    for i in (3, 5, 0, 1, 2, 4, 6, 7):
        copies[i].start()

    spot = jnp.transpose(jnp.broadcast_to(slot[pl.ds(0, 1), :].astype(F32), (128, T)))[:, 0:1].astype(jnp.int32)
    live_rows = spot >= 0
    m = iota((T, J * G * MSG), 1)
    for part in range(D // TILE):
        take = ones_where(spot + part * S == m)
        at = pl.ds(part * TILE, TILE)
        for a, to in enumerate((mixed, moved)):
            kept = home[a, pl.ds(part * T, T), :].astype(F32)
            to[:, at] = jnp.where(live_rows, contract(take, ret[a]), kept).astype(BF16)
    for i, (a, b) in enumerate(((mixed, o_mixed), (moved, o_tg))):
        copies.append(pltpu.make_async_copy(a, b, sem.at[8 + i]))
        copies[-1].start()
    for copy in copies:
        copy.wait()


def on_device(
    tokens, assignment, lengths, centroids, ln_gain, ln_bias, w_in, b_in, w_out, b_out, cotangent
):
    T, D = tokens.shape
    G, H = lax.axis_size("expert"), lax.axis_size("hidden")
    J, F = w_in.shape[0], w_in.shape[2]
    PW = centroids.shape[1]
    S = max(2, 9 * T // (8 * J * G))
    parts = D // TILE
    MSG = -(-(parts * S + 1) // 16) * 16
    R, GM, N = G * S, G * MSG, H * G * S
    seq_len = min(2048, H * T)
    dims = (G, H, J, S, MSG, R, T, D, F, PW, seq_len)
    vm = pl.BlockSpec(memory_space=pltpu.VMEM)
    hbm = pl.BlockSpec(memory_space=pl.ANY)
    sm = pl.BlockSpec(memory_space=pltpu.SMEM)
    dma = pltpu.SemaphoreType.DMA
    buffers = [
        ((J, D, F), BF16),
        ((J, F, D), BF16),
        ((2, J, N, D), BF16),
        ((J, N, F), BF16),
        ((J, N, F), BF16),
        ((2, J, H, R, D), BF16),
        ((2, J, H + 1, R, D), BF16),
        ((J, 2, GM, TILE), BF16),
        ((J, 2, GM, TILE), BF16),
        ((J, 2, parts * R, TILE), BF16),
        ((GM, parts * T), BF16),
        ((parts * R, GM), BF16),
        ((GM, parts * R), BF16),
        ((R, GM), BF16),
        ((4 * J, D), F32),
        ((4, J, R, 1), F32),
        ((H, 16, 128), F32),
        ((G, 8, 128), F32),
        ((4 * J, D), F32),
        ((H, 4 * J, PW), F32),
        ((J, R, D), F32),
        ((max(D, F), N), BF16),
    ]
    taken = sum(
        jnp.dtype(t).itemsize * -(-s[-1] // 128) * 128 * functools.reduce(lambda a, b: a * b, s[:-1]) for s, t in buffers
    )

    results = [(J, PW), (J, PW), (J, PW), (J, D, F), (J, F), (J, F, D), (J, PW), (1, G * J)]
    shape = jax.ShapeDtypeStruct

    def layer(number, sizes, *args):
        made = pl.pallas_call(
            functools.partial(layer_kernel, dims, sizes),
            name="layer",
            out_shape=[
                pltpu.VMEM((2, parts * T, TILE), BF16),
                pltpu.VMEM((2, J * GM, TILE), BF16),
                pltpu.VMEM((8, T), jnp.int32),
                *[pltpu.VMEM(s, F32) for s in results],
            ],
            in_specs=[vm, sm, vm, vm, vm, vm, vm, hbm, hbm, hbm, hbm],
            out_specs=[vm] * 11,
            scratch_shapes=[
                *[pltpu.VMEM(s, t) for s, t in buffers],
                dma((2 * parts + 2,)),
                dma((H,)), dma((H,)),
                dma((H,)), dma((H,)),
                dma((G,)), dma((G,)),
                dma((H,)), dma((H,)),
                dma((J, 2, G)), dma((J, 2, G)),
                dma((J, 2, G)), dma((J, 2, G)),
                dma((2, 2, J, H)), dma((2, J, H)),
                dma((2, J, HALVES, H)), dma((2, J, HALVES, H + 1)),
            ],
            compiler_params=pltpu.CompilerParams(
                collective_id=number, has_side_effects=True, vmem_limit_bytes=taken + 3 * 2**20
            ),
            cost_estimate=pl.CostEstimate(
                flops=12 * J * N * D * F, bytes_accessed=30 * 2**20, transcendentals=J * N * F
            ),
        )(*args)
        return pl.pallas_call(
            functools.partial(deliver_kernel, dims),
            name="deliver",
            out_shape=[shape((T, D), BF16), shape((T, D), BF16), *[shape(s, F32) for s in results]],
            in_specs=[vm] * 11,
            out_specs=[hbm] * 10,
            scratch_shapes=[pltpu.VMEM((T, D), BF16), pltpu.VMEM((T, D), BF16), dma((10,))],
            compiler_params=pltpu.CompilerParams(vmem_limit_bytes=8 * 2**20),
        )(*made)

    args = (
        assignment.reshape(1, T), lengths, centroids, ln_gain, ln_bias, b_out, b_in, tokens, cotangent, w_in, w_out
    )
    options = []
    for shares in SHAPES:
        needed = [-(-G * shares[4 * h // H] // 8) * S for h in range(H)]
        options.append(tuple(-(-r // 16) * 16 for r in needed))
    if len(options) > 1:
        first = (jnp.arange(G, dtype=jnp.int32)[:, None] * H + jnp.arange(H, dtype=jnp.int32)[None, :]) * T
        if seq_len == H * T:
            lengths_of = lengths[:, None]
        else:
            lengths_of = lengths[first // seq_len]
        needed = S * jnp.sum((lengths_of > first % seq_len).astype(jnp.int32), axis=0)
        fits = jnp.all(needed[None, :] <= jnp.asarray(options, jnp.int32), axis=1)
        which = jnp.max(jnp.where(fits, jnp.arange(len(options), dtype=jnp.int32), 0))

    def choose(low, high):
        if high - low == 1:
            return functools.partial(layer, low, options[low])
        middle = (low + high) // 2
        return lambda *args: lax.cond(which >= middle, choose(middle, high), choose(low, middle), *args)

    outs = choose(0, len(options))(*args)
    return (*outs[:9], outs[9].reshape(G * J))


def solution(mesh):
    tok = P(("expert", "hidden"), None)
    par = P("expert", "hidden")
    win = P("expert", None, "hidden")
    wout = P("expert", "hidden", None)
    return jax.shard_map(
        on_device,
        mesh=mesh,
        in_specs=(tok, tok, P(), par, par, par, win, par, wout, par, tok),
        out_specs=(tok, tok, par, par, par, win, par, wout, par, P()),
        check_vma=False,
    )
```

```python
import functools

import jax
import jax.numpy as jnp
from jax import lax
from jax.experimental import pallas as pl
from jax.experimental.pallas import tpu as pltpu
from jax.sharding import PartitionSpec as P

EPS = 1e-05
MESH = pl.DeviceIdType.MESH
F32 = jnp.float32
BF16 = jnp.bfloat16
TILE = 256
PIECES = 3
GELU_A = 0.7978845608028654
GELU_B = 0.044715
SHAPES = ((8, 8, 8, 8), (8, 7, 6, 5), (8, 6, 4, 3),)


def contract(a, b, dims=((1,), (0,))):
    return lax.dot_general(a, b, (dims, ((), ())), preferred_element_type=F32)


def iota(shape, axis):
    return lax.broadcasted_iota(jnp.int32, shape, axis)


def ones_where(mask):
    return mask.astype(F32).astype(BF16)


def per(index, size, count):
    return jnp.floor((index.astype(F32) + 0.5) * (1.0 / size)).astype(jnp.int32)


def layer_kernel(
    dims, sizes,
    asg, lens, cent, gain, bias, bout, bin_, tok_in, cot_in, win, wout,
    home, ret, o_slot, o_cent, o_gain, o_bias, o_win, o_bin, o_wout, o_bout, o_mean,
    vwin, vwout, gat, act, pg, sbuf, rbuf, snd, rcv, xg, spread, pick, unpick, pick_count,
    par, stats, zs, mg, grads, gbuf, normed_of, turned,
    w_sem, par_s, par_r, zs_s, zs_r, mg_s, mg_r, gb_s, gb_r,
    disp_s, disp_r, ret_s, ret_r, gat_s, gat_r, red_s, red_r,
):
    G, H, J, S, MSG, R, T, D, F, PW, seq_len = dims
    e, z = lax.axis_index("expert"), lax.axis_index("hidden")
    E, GM, N = G * J, G * MSG, H * R
    parts = D // TILE
    BLOCK = R

    def cols(t, size=TILE):
        return pl.ds(pl.multiple_of(t * size, size), size)

    def rows(start, size):
        return pl.ds(pl.multiple_of(start, 16), size)

    def loop(count, body):
        def step(i, _):
            body(i)
            return 0

        lax.fori_loop(0, count, step, 0)

    barrier = pltpu.get_barrier_semaphore()
    for d in range(1, H):
        pl.semaphore_signal(barrier, inc=1, device_id=(e, (z + d) % H), device_id_type=MESH)
    for d in range(1, G):
        pl.semaphore_signal(barrier, inc=1, device_id=((e + d) % G, z), device_id_type=MESH)

    loads = []
    for a, source in enumerate((tok_in, cot_in)):
        for part in range(parts):
            loads.append(pltpu.make_async_copy(
                source.at[:, pl.ds(part * TILE, TILE)], home.at[a, pl.ds(part * T, T), :],
                w_sem.at[a * parts + part]))
    weights = [
        pltpu.make_async_copy(win, vwin, w_sem.at[2 * parts]),
        pltpu.make_async_copy(wout, vwout, w_sem.at[2 * parts + 1]),
    ]
    for copy in loads + weights:
        copy.start()

    own_cols = cols(z, PW)
    par[pl.ds(0, J), own_cols] = gain[...]
    par[pl.ds(J, J), own_cols] = bias[...]
    par[pl.ds(2 * J, J), own_cols] = cent[...].astype(F32)
    par[pl.ds(3 * J, J), own_cols] = bout[...]

    expert = asg[...]
    place = (e * H + z) * T
    length = lens[place // seq_len]
    live = (place % seq_len + iota((1, T), 1)) < length
    sub_e = iota((E, 1), 0)
    hot = ((expert == sub_e) & live).astype(F32)
    earlier = ones_where(iota((T, T), 0) < iota((T, T), 1))
    before = contract(hot.astype(BF16), earlier)
    group = per(sub_e, J, G)
    inner = sub_e - group * J
    rank = jnp.sum(hot * before, axis=0, keepdims=True).astype(jnp.int32)
    to_group = jnp.sum(hot * group.astype(F32), axis=0, keepdims=True).astype(jnp.int32)
    to_inner = jnp.sum(hot * inner.astype(F32), axis=0, keepdims=True).astype(jnp.int32)
    to_inner = jnp.where(live, to_inner, -1)
    message = to_group * MSG
    o_slot[...] = jnp.broadcast_to(jnp.where(live, to_inner * GM + message + rank, -D * D), (8, T))

    pl.semaphore_wait(barrier, (H - 1) + (G - 1))

    def par_copy(d, source):
        return pltpu.make_async_remote_copy(
            src_ref=par.at[:, cols(source, PW)], dst_ref=par.at[:, cols(source, PW)],
            send_sem=par_s.at[d], recv_sem=par_r.at[d],
            device_id=(e, (z + d) % H), device_id_type=MESH)

    for d in range(1, H):
        par_copy(d, z).start()

    def msg(k):
        return pl.ds(pl.multiple_of(k * MSG, MSG), MSG)

    def disp_copy(j, a, d, target):
        return pltpu.make_async_remote_copy(
            src_ref=snd.at[j, a, msg(target)], dst_ref=rcv.at[j, a, msg(e)],
            send_sem=disp_s.at[j, a, d], recv_sem=disp_r.at[j, a, d],
            device_id=(target, z), device_id_type=MESH)

    def disp_in(j, a, d):
        k = (e - d + G) % G
        return pltpu.make_async_remote_copy(
            src_ref=snd.at[j, a, msg(k)], dst_ref=rcv.at[j, a, msg(k)],
            send_sem=disp_s.at[j, a, d], recv_sem=disp_r.at[j, a, d],
            device_id=((e + d) % G, z), device_id_type=MESH)

    def dispatch(i):
        j, a = i // 2, i % 2
        row = iota((GM, T), 0)
        mine = to_inner == j

        @pl.when(a == 0)
        def _():
            at = jnp.where(mine, message + rank, -D * D)
            for part in range(parts):
                spread[:, pl.ds(part * T, T)] = ones_where(at + part * S == row)

        for b in range(2):
            @pl.when(jnp.logical_and(j == 0, a == b))
            def _(b=b):
                for copy in loads[b * parts:(b + 1) * parts]:
                    copy.wait()

        counted = jnp.where(mine & (a == 0), message + parts * S, -1)
        v = contract(spread[...], home[a]) + contract(ones_where(counted == row), jnp.ones((T, TILE), BF16))
        snd[j, a] = v.astype(BF16)
        for d in range(1, G):
            disp_copy(j, a, d, (e + d) % G).start()
        rcv[j, a, msg(e), :] = snd[j, a, msg(e), :]

    loop(2 * J, dispatch)

    def row_of(c):
        k = per(c, MSG, G)
        start = jnp.full(c.shape, -D * D, jnp.int32)
        filled_before = jnp.int32(0)
        for i in range(G):
            first = (i * H + z) * T
            some = lens[first // seq_len] > first % seq_len
            start = jnp.where((k == i) & some, filled_before * S, start)
            filled_before = filled_before + some.astype(jnp.int32)
        return start, c - k * MSG

    start, within = row_of(iota((1, GM), 1))
    down = iota((R, GM), 0)
    for part in range(parts):
        i = within - part * S
        pick[pl.ds(part * R, R), :] = ones_where(jnp.where((i >= 0) & (i < S), start + i, -1) == down)
    counts_at = jnp.where(within == parts * S, start, -D * D)
    pick_count[...] = ones_where((down >= counts_at) & (down < counts_at + S))
    start, within = row_of(iota((GM, 1), 0))
    across = iota((1, parts * R), 1)
    across_part = per(across, R, parts)
    i = within - across_part * S
    unpick[...] = ones_where((i >= 0) & (i < S) & (start + i == across - across_part * R))

    for h in range(H):
        if sizes[h] < R:
            gat[:, :, pl.ds(h * R + sizes[h], R - sizes[h]), :] = jnp.zeros((2, J, R - sizes[h], D), BF16)

    def clear(slot_at):
        def one(i):
            rbuf[i // J, i % J, slot_at] = jnp.zeros((R, D), BF16)

        loop(2 * J, one)

    pl.when(z == 0)(lambda: clear(H))
    pl.when(z == H - 1)(lambda: clear(H - 1))

    o_bin[...] = jnp.zeros_like(o_bin)

    for d in range(1, H):
        par_copy(d, (z - d + H) % H).wait_recv()

    def with_rows(chunk, body):
        for size in sorted(set(sizes)):
            planes = [h for h in range(H) if sizes[h] == size]
            if len(planes) == H:
                body(size)
            else:
                hit = chunk == planes[0]
                for h in planes[1:]:
                    hit = jnp.logical_or(hit, chunk == h)
                pl.when(hit)(functools.partial(body, size))

    def gat_copy(a, j, chunk, up, size):
        at = (a, j, rows(chunk * R, size))
        return pltpu.make_async_remote_copy(
            src_ref=gat.at[at], dst_ref=gat.at[at],
            send_sem=gat_s.at[up, a, j, chunk], recv_sem=gat_r.at[a, j, chunk],
            device_id=(e, jnp.clip(z + 2 * up - 1, 0, H - 1)), device_id_type=MESH)

    def send_gat(a, j, chunk, up, size):
        @pl.when(jnp.where(up == 1, z < H - 1, z > 0))
        def _():
            gat_copy(a, j, chunk, up, size).start()

    def send_own(a, j):
        def both(size):
            send_gat(a, j, z, 1, size)
            send_gat(a, j, z, 0, size)

        with_rows(z, both)

    def piece_of(size, piece):
        start = 0
        for i in range(piece + 1):
            count = -(-(size - start) // (16 * (PIECES - i))) * 16
            start = start + count
        return start - count, count

    def red_copy(a, j, piece, to, up, size):
        slot_to = jnp.where(jnp.logical_and(up == 1, to == z + 1), H, to)
        at = pl.ds(*piece_of(size, piece))
        return pltpu.make_async_remote_copy(
            src_ref=sbuf.at[a, j, to, at], dst_ref=rbuf.at[a, j, slot_to, at],
            send_sem=red_s.at[a, j, piece, to], recv_sem=red_r.at[a, j, piece, slot_to],
            device_id=(e, jnp.clip(z + 2 * up - 1, 0, H - 1)), device_id_type=MESH)

    def red_in(a, j, piece, slot_at, size):
        at = pl.ds(*piece_of(size, piece))
        return pltpu.make_async_remote_copy(
            src_ref=sbuf.at[a, j, 0, at], dst_ref=rbuf.at[a, j, slot_at, at],
            send_sem=red_s.at[a, j, piece, 0], recv_sem=red_r.at[a, j, piece, slot_at],
            device_id=(e, jnp.clip(z + 1, 0, H - 1)), device_id_type=MESH)

    def quarter(part, b):
        return pl.ds(pl.multiple_of(part * R + b * BLOCK, 16), BLOCK)

    lane8 = iota((8, 128), 1)
    r1 = iota((R, 1), 0)
    rank_in = (r1 - S * per(r1, S, G)).astype(F32)
    zs[z] = jnp.zeros((16, 128), F32)

    def take_in(j, a):
        for d in range(1, G):
            disp_in(j, a, d).wait_recv()
        xg[j, a] = contract(pick[...], rcv[j, a]).astype(BF16)

    def prepare(j):
        take_in(j, 0)
        count = contract(pick_count[...], rcv[j, 0, :, pl.ds(0, 128)])[:, 0:1]
        stats[3, j] = (rank_in < count).astype(F32)

        def block(b):
            x = [xg[j, 0, quarter(part, b), :].astype(F32) for part in range(parts)]
            mean = sum(jnp.sum(v, axis=1, keepdims=True) for v in x) * (1.0 / D)
            x_mid = [v - mean for v in x]
            var = sum(jnp.sum(v * v, axis=1, keepdims=True) for v in x_mid) * (1.0 / D)
            factor = lax.rsqrt(var + EPS)
            score = 0.0
            at = rows(b * BLOCK, BLOCK)
            for part in range(parts):
                lanes = pl.ds(part * TILE, TILE)
                normed = x_mid[part] * factor
                lifted = normed * par[pl.ds(j, 1), lanes] + par[pl.ds(J + j, 1), lanes]
                gat[0, j, rows(z * R + b * BLOCK, BLOCK), lanes] = lifted.astype(BF16)
                normed_of[j, at, lanes] = normed
                score = score + jnp.sum(x[part] * par[pl.ds(2 * J + j, 1), lanes], axis=1, keepdims=True)
            stats[0, j, at] = jax.nn.sigmoid(score)
            stats[1, j, at] = factor

        loop(R // BLOCK, block)
        send_own(0, j)
        take_in(j, 1)

        def weigh(b):
            at = rows(b * BLOCK, BLOCK)
            for part in range(parts):
                g = xg[j, 1, quarter(part, b), :].astype(F32)
                gat[1, j, rows(z * R + b * BLOCK, BLOCK), pl.ds(part * TILE, TILE)] = (stats[0, j, at] * g).astype(BF16)

        loop(R // BLOCK, weigh)
        send_own(1, j)
        total = jnp.sum(stats[3, j] * stats[0, j], axis=0, keepdims=True)
        number = jnp.sum(stats[3, j], axis=0, keepdims=True)
        zs[z, pl.ds(0, 8), :] += jnp.where(lane8 == j, total, 0.0)
        zs[z, pl.ds(8, 8), :] += jnp.where(lane8 == j, number, 0.0)

    loop(J, prepare)

    def zs_copy(d, source):
        return pltpu.make_async_remote_copy(
            src_ref=zs.at[source], dst_ref=zs.at[source],
            send_sem=zs_s.at[d], recv_sem=zs_r.at[d],
            device_id=(e, (z + d) % H), device_id_type=MESH)

    for d in range(1, H):
        zs_copy(d, z).start()

    for copy in weights:
        copy.wait()

    wide = 2 * TILE

    def compute(chunk, j):
        mine = rows(chunk * R, R)

        def first(t):
            pre = contract(gat[0, j, mine, :], vwin[j, :, cols(t, wide)]) + bin_[pl.ds(j, 1), cols(t, wide)]
            sq = pre * pre
            th = jnp.tanh(pre * (GELU_A + (GELU_A * GELU_B) * sq))
            cdf = 0.5 + 0.5 * th
            slope = cdf + pre * (0.5 - 0.5 * th * th) * (GELU_A + (3.0 * GELU_A * GELU_B) * sq)
            act[j, mine, cols(t, wide)] = (pre * cdf).astype(BF16)
            act_grad = contract(gat[1, j, mine, :], vwout[j, cols(t, wide), :], ((1,), (1,)))
            pre_grad = (act_grad * slope).astype(BF16)
            pg[j, mine, cols(t, wide)] = pre_grad
            o_bin[pl.ds(j, 1), cols(t, wide)] += jnp.sum(pre_grad.astype(F32), axis=0, keepdims=True)

        loop(F // wide, first)

        def second(t):
            v = contract(act[j, mine, :], vwout[j, :, cols(t, wide)])
            sbuf[0, j, chunk, :, cols(t, wide)] = v.astype(BF16)
            w = contract(pg[j, mine, :], vwin[j, cols(t, wide), :], ((1,), (1,)))
            sbuf[1, j, chunk, :, cols(t, wide)] = w.astype(BF16)

        loop(D // wide, second)

    def outer(left, right, to, tall, wide):
        turned[pl.ds(0, tall), :] = jnp.transpose(left)

        def tile(t):
            to[:, cols(t)] = contract(turned[pl.ds(0, tall), :], right[:, cols(t)])

        loop(wide // TILE, tile)

    def mg_copy(d, source):
        return pltpu.make_async_remote_copy(
            src_ref=mg.at[source], dst_ref=mg.at[source],
            send_sem=mg_s.at[d], recv_sem=mg_r.at[d],
            device_id=((e + d) % G, z), device_id_type=MESH)

    def gb_copy(d, source, target):
        return pltpu.make_async_remote_copy(
            src_ref=grads.at[:, cols(target, PW)], dst_ref=gbuf.at[source],
            send_sem=gb_s.at[d], recv_sem=gb_r.at[d],
            device_id=(e, (z + d) % H), device_id_type=MESH)

    def ret_copy(j, a, d, target):
        return pltpu.make_async_remote_copy(
            src_ref=snd.at[j, a, msg(target)], dst_ref=ret.at[a, rows(j * GM + e * MSG, MSG)],
            send_sem=ret_s.at[j, a, d], recv_sem=ret_r.at[j, a, d],
            device_id=(target, z), device_id_type=MESH)

    def ret_in(j, a, d):
        k = (e - d + G) % G
        return pltpu.make_async_remote_copy(
            src_ref=snd.at[j, a, msg(k)], dst_ref=ret.at[a, rows(j * GM + k * MSG, MSG)],
            send_sem=ret_s.at[j, a, d], recv_sem=ret_r.at[j, a, d],
            device_id=((e + d) % G, z), device_id_type=MESH)

    def wait_sums(a, j):
        def both(size):
            for piece in range(PIECES):
                @pl.when(z < H - 1)
                def _(piece=piece):
                    red_in(a, j, piece, z, size).wait_recv()

                @pl.when(z > 0)
                def _(piece=piece):
                    red_in(a, j, piece, H, size).wait_recv()

        with_rows(z, both)

    def summed(a, j, b, part):
        at = (rows(b * BLOCK, BLOCK), pl.ds(part * TILE, TILE))
        v = sbuf[(a, j, z, *at)].astype(F32) + rbuf[(a, j, z, *at)].astype(F32) + rbuf[(a, j, H, *at)].astype(F32)
        return jnp.where(stats[3, j, at[0]] > 0.5, v, 0.0)

    def send_home(j, a):
        snd[j, a] = contract(unpick[...], xg[j, a]).astype(BF16)
        for d in range(1, G):
            ret_copy(j, a, d, (e + d) % G).start()
        ret[a, rows(j * GM + e * MSG, MSG), :] = snd[j, a, msg(e), :]

    def finish(j):
        wait_sums(0, j)

        def forward(b):
            at = rows(b * BLOCK, BLOCK)
            gate = stats[0, j, at]
            gate_grad = 0.0
            for part in range(parts):
                lanes = pl.ds(part * TILE, TILE)
                branch = (summed(0, j, b, part) + par[pl.ds(3 * J + j, 1), lanes]).astype(BF16).astype(F32)
                x = xg[j, 0, quarter(part, b), :].astype(F32)
                gate_grad = gate_grad + jnp.sum(
                    xg[j, 1, quarter(part, b), :].astype(F32) * branch, axis=1, keepdims=True)
                rbuf[0, j, H, at, lanes] = x.astype(BF16)
                xg[j, 0, quarter(part, b), :] = (x + gate * branch).astype(BF16)
            score_grad = gate_grad * gate * (1.0 - gate)
            stats[2, j, at] = score_grad
            for part in range(parts):
                lanes = pl.ds(part * TILE, TILE)
                x = rbuf[0, j, H, at, lanes].astype(F32)
                grads[pl.ds(2 * J + j, 1), lanes] += jnp.sum(score_grad * x, axis=0, keepdims=True)
                sent = gat[1, j, rows(z * R + b * BLOCK, BLOCK), lanes].astype(F32)
                grads[pl.ds(3 * J + j, 1), lanes] += jnp.sum(sent, axis=0, keepdims=True)

        loop(R // BLOCK, forward)
        send_home(j, 0)
        wait_sums(1, j)

        def backward(b):
            at = rows(b * BLOCK, BLOCK)
            factor, score_grad = stats[1, j, at], stats[2, j, at]
            sum_n, sum_nn = 0.0, 0.0
            n_grads = []
            for part in range(parts):
                lanes = pl.ds(part * TILE, TILE)
                lifted_grad = summed(1, j, b, part)
                normed = normed_of[j, at, lanes]
                grads[pl.ds(j, 1), lanes] += jnp.sum(lifted_grad * normed, axis=0, keepdims=True)
                grads[pl.ds(J + j, 1), lanes] += jnp.sum(lifted_grad, axis=0, keepdims=True)
                n_grad = lifted_grad * par[pl.ds(j, 1), lanes]
                sum_n = sum_n + jnp.sum(n_grad, axis=1, keepdims=True)
                sum_nn = sum_nn + jnp.sum(n_grad * normed, axis=1, keepdims=True)
                n_grads.append(n_grad)
            for part in range(parts):
                lanes = pl.ds(part * TILE, TILE)
                rows_grad = factor * (
                    n_grads[part] - sum_n * (1.0 / D) - normed_of[j, at, lanes] * (sum_nn * (1.0 / D)))
                rows_grad = rows_grad.astype(BF16).astype(F32)
                g = xg[j, 1, quarter(part, b), :].astype(F32)
                moved = g + score_grad * par[pl.ds(2 * J + j, 1), lanes] + rows_grad
                xg[j, 1, quarter(part, b), :] = moved.astype(BF16)

        loop(R // BLOCK, backward)
        send_home(j, 1)

    last = jnp.maximum(z, H - 1 - z)
    grads[...] = jnp.zeros_like(grads)

    def sent(i):
        for d in range(1, G):
            disp_copy(i // 2, i % 2, d, (e + d) % G).wait_send()

    def starts(up):
        return jnp.where(up == 1, z == 0, z == H - 1)

    def passes(up, to):
        return jnp.where(up == 1, (z > 0) & (z < to), (z < H - 1) & (z > to))

    def begin(to, j, up):
        def both(size):
            for a in range(2):
                for piece in range(PIECES):
                    red_copy(a, j, piece, to, up, size).start()

        with_rows(to, both)

    def pass_sum(a, j, to, up):
        def both(size):
            for piece in range(PIECES):
                red_in(a, j, piece, to, size).wait_recv()
                at = (a, j, to, pl.ds(*piece_of(size, piece)))
                sbuf[at] = (sbuf[at].astype(F32) + rbuf[at].astype(F32)).astype(BF16)
                red_copy(a, j, piece, to, up, size).start()

        with_rows(to, both)

    def item(q):
        s, j = q // J, q % J

        def forwarded(i):
            up, a = 1 - i // 2, i % 2
            chunk = jnp.where(up == 1, z - s, z + s)

            @pl.when((s > 0) & (chunk >= 0) & (chunk < H))
            def _():
                def pass_on(size):
                    gat_copy(a, j, chunk, up, size).wait_recv()
                    send_gat(a, j, chunk, up, size)

                with_rows(chunk, pass_on)

        loop(4, forwarded)

        def side(d):
            chunk = jnp.where(d == 0, z - s, z + s)

            @pl.when((chunk >= 0) & (chunk < H) & ((s > 0) | (d == 0)))
            def _():
                compute(chunk, j)

                @pl.when(starts(d) & (s > 0) & ((s > 1) | (j < J - 1)))
                def _():
                    begin(chunk, j, d)

        loop(2, side)

        def through(i):
            a, up = i // 2, (i + jnp.where(z >= H // 2, 0, 1)) % 2
            to = jnp.where(up == 1, s, H - 1 - s)
            near = (to == z + 2 * up - 1) & (j == J - 1) & (s < H - 1)

            @pl.when((s > 0) & passes(up, to) & jnp.logical_not(near))
            def _():
                pass_sum(a, j, to, up)

        loop(4, through)

        @pl.when(q == H * J - 1)
        def _():
            for up in range(2):
                to = z + 2 * up - 1

                @pl.when(starts(up) & (to >= 0) & (to < H))
                def _(up=up, to=to):
                    begin(to, J - 1, up)

                @pl.when(passes(up, to) & (jnp.where(up == 1, to, H - 1 - to) < H - 1))
                def _(up=up, to=to):
                    loop(2, lambda a: pass_sum(a, J - 1, to, up))

        @pl.when((s == last) & (j == 0))
        def _():
            for d in range(1, H):
                zs_copy(d, (z - d + H) % H).wait_recv()
            both = zs[0]
            for h in range(1, H):
                both = both + zs[h]
            mg[e] = both[0:8] / jnp.maximum(both[8:16], 1.0)
            for d in range(1, G):
                mg_copy(d, e).start()

        @pl.when(s == last)
        def _():
            outer(gat[0, j], pg.at[j], o_win.at[j], D, F)
            outer(act[j], gat.at[1, j], o_wout.at[j], F, D)

    loop(H * J, item)
    loop(2 * J, sent)
    loop(J, finish)
    for d in range(1, H):
        gb_copy(d, z, (z + d) % H).start()

    gbuf[z] = grads[:, own_cols]
    for d in range(1, G):
        mg_copy(d, (e - d + G) % G).wait_recv()
    means = jnp.zeros((8, 128), F32)
    for k in range(G):
        v = mg[k] if k == 0 else pltpu.roll(mg[k], k * J, 1)
        means = jnp.where((lane8 >= k * J) & (lane8 < k * J + J), v, means)
    o_mean[...] = means[0:1, 0:E]

    for d in range(1, H):
        gb_copy(d, (z - d + H) % H, z).wait_recv()
    small = gbuf[0]
    for h in range(1, H):
        small = small + gbuf[h]
    o_gain[...] = small[0:J]
    o_bias[...] = small[J:2 * J]
    o_cent[...] = small[2 * J:3 * J]
    o_bout[...] = small[3 * J:4 * J]

    for d in range(1, H):
        par_copy(d, z).wait_send()
        zs_copy(d, z).wait_send()
        gb_copy(d, z, (z + d) % H).wait_send()
    for d in range(1, G):
        mg_copy(d, e).wait_send()

    def drain(i):
        a, j, h = i // (J * H), i // H % J, i % H

        def wait(size):
            @pl.when((z < H - 1) & (h <= z))
            def _():
                gat_copy(a, j, h, 1, size).wait_send()

            @pl.when((z > 0) & (h >= z))
            def _():
                gat_copy(a, j, h, 0, size).wait_send()

            @pl.when(h != z)
            def _():
                for piece in range(PIECES):
                    red_copy(a, j, piece, h, jnp.where(h > z, 1, 0), size).wait_send()

        with_rows(h, wait)

    loop(2 * J * H, drain)

    def arrived(i):
        j, a = i // 2, i % 2
        for d in range(1, G):
            ret_in(j, a, d).wait_recv()
            ret_copy(j, a, d, (e + d) % G).wait_send()

    loop(2 * J, arrived)


def deliver_kernel(dims, home, ret, slot, *refs):
    G, H, J, S, MSG, R, T, D, F, PW, seq_len = dims
    results, (o_mixed, o_tg, *outs), (mixed, moved, sem) = refs[:8], refs[8:18], refs[18:]
    copies = [pltpu.make_async_copy(a, b, sem.at[i]) for i, (a, b) in enumerate(zip(results, outs))]
    for i in (3, 5, 0, 1, 2, 4, 6, 7):
        copies[i].start()

    spot = jnp.transpose(jnp.broadcast_to(slot[pl.ds(0, 1), :].astype(F32), (128, T)))[:, 0:1].astype(jnp.int32)
    live_rows = spot >= 0
    m = iota((T, J * G * MSG), 1)
    for part in range(D // TILE):
        take = ones_where(spot + part * S == m)
        at = pl.ds(part * TILE, TILE)
        for a, to in enumerate((mixed, moved)):
            kept = home[a, pl.ds(part * T, T), :].astype(F32)
            to[:, at] = jnp.where(live_rows, contract(take, ret[a]), kept).astype(BF16)
    for i, (a, b) in enumerate(((mixed, o_mixed), (moved, o_tg))):
        copies.append(pltpu.make_async_copy(a, b, sem.at[8 + i]))
        copies[-1].start()
    for copy in copies:
        copy.wait()


def on_device(
    tokens, assignment, lengths, centroids, ln_gain, ln_bias, w_in, b_in, w_out, b_out, cotangent
):
    T, D = tokens.shape
    G, H = lax.axis_size("expert"), lax.axis_size("hidden")
    J, F = w_in.shape[0], w_in.shape[2]
    PW = centroids.shape[1]
    S = max(2, 9 * T // (8 * J * G))
    parts = D // TILE
    MSG = -(-(parts * S + 1) // 16) * 16
    R, GM, N = G * S, G * MSG, H * G * S
    seq_len = min(2048, H * T)
    dims = (G, H, J, S, MSG, R, T, D, F, PW, seq_len)
    vm = pl.BlockSpec(memory_space=pltpu.VMEM)
    hbm = pl.BlockSpec(memory_space=pl.ANY)
    sm = pl.BlockSpec(memory_space=pltpu.SMEM)
    dma = pltpu.SemaphoreType.DMA
    buffers = [
        ((J, D, F), BF16),
        ((J, F, D), BF16),
        ((2, J, N, D), BF16),
        ((J, N, F), BF16),
        ((J, N, F), BF16),
        ((2, J, H, R, D), BF16),
        ((2, J, H + 1, R, D), BF16),
        ((J, 2, GM, TILE), BF16),
        ((J, 2, GM, TILE), BF16),
        ((J, 2, parts * R, TILE), BF16),
        ((GM, parts * T), BF16),
        ((parts * R, GM), BF16),
        ((GM, parts * R), BF16),
        ((R, GM), BF16),
        ((4 * J, D), F32),
        ((4, J, R, 1), F32),
        ((H, 16, 128), F32),
        ((G, 8, 128), F32),
        ((4 * J, D), F32),
        ((H, 4 * J, PW), F32),
        ((J, R, D), F32),
        ((max(D, F), N), BF16),
    ]
    taken = sum(
        jnp.dtype(t).itemsize * -(-s[-1] // 128) * 128 * functools.reduce(lambda a, b: a * b, s[:-1]) for s, t in buffers
    )

    results = [(J, PW), (J, PW), (J, PW), (J, D, F), (J, F), (J, F, D), (J, PW), (1, G * J)]
    shape = jax.ShapeDtypeStruct

    def layer(number, sizes, *args):
        made = pl.pallas_call(
            functools.partial(layer_kernel, dims, sizes),
            name="layer",
            out_shape=[
                pltpu.VMEM((2, parts * T, TILE), BF16),
                pltpu.VMEM((2, J * GM, TILE), BF16),
                pltpu.VMEM((8, T), jnp.int32),
                *[pltpu.VMEM(s, F32) for s in results],
            ],
            in_specs=[vm, sm, vm, vm, vm, vm, vm, hbm, hbm, hbm, hbm],
            out_specs=[vm] * 11,
            scratch_shapes=[
                *[pltpu.VMEM(s, t) for s, t in buffers],
                dma((2 * parts + 2,)),
                dma((H,)), dma((H,)),
                dma((H,)), dma((H,)),
                dma((G,)), dma((G,)),
                dma((H,)), dma((H,)),
                dma((J, 2, G)), dma((J, 2, G)),
                dma((J, 2, G)), dma((J, 2, G)),
                dma((2, 2, J, H)), dma((2, J, H)),
                dma((2, J, PIECES, H)), dma((2, J, PIECES, H + 1)),
            ],
            compiler_params=pltpu.CompilerParams(
                collective_id=number, has_side_effects=True, vmem_limit_bytes=taken + 3 * 2**20
            ),
            cost_estimate=pl.CostEstimate(
                flops=12 * J * N * D * F, bytes_accessed=30 * 2**20, transcendentals=J * N * F
            ),
        )(*args)
        return pl.pallas_call(
            functools.partial(deliver_kernel, dims),
            name="deliver",
            out_shape=[shape((T, D), BF16), shape((T, D), BF16), *[shape(s, F32) for s in results]],
            in_specs=[vm] * 11,
            out_specs=[hbm] * 10,
            scratch_shapes=[pltpu.VMEM((T, D), BF16), pltpu.VMEM((T, D), BF16), dma((10,))],
            compiler_params=pltpu.CompilerParams(vmem_limit_bytes=8 * 2**20),
        )(*made)

    args = (
        assignment.reshape(1, T), lengths, centroids, ln_gain, ln_bias, b_out, b_in, tokens, cotangent, w_in, w_out
    )
    options = []
    for shares in SHAPES:
        needed = [-(-G * shares[4 * h // H] // 8) * S for h in range(H)]
        options.append(tuple(-(-r // 16) * 16 for r in needed))
    bits = G.bit_length()
    if len(options) > 1 and seq_len == H * T and bits * H < 32:
        alive = lengths[:, None] > jnp.asarray([h * T for h in range(H)], jnp.int32)
        packed = jnp.sum(jnp.where(alive, jnp.asarray([1 << bits * h for h in range(H)], jnp.int32), 0))
        which = jnp.int32(0)
        for i, rows in enumerate(options[1:]):
            fits = True
            for h in range(H):
                fits = fits & ((packed >> (bits * h)) % (1 << bits) * S <= rows[h])
            which = jnp.where(fits, i + 1, which)
    elif len(options) > 1:
        first = (jnp.arange(G, dtype=jnp.int32)[:, None] * H + jnp.arange(H, dtype=jnp.int32)[None, :]) * T
        needed = S * jnp.sum((lengths[first // seq_len] > first % seq_len).astype(jnp.int32), axis=0)
        fits = jnp.all(needed[None, :] <= jnp.asarray(options, jnp.int32), axis=1)
        which = jnp.max(jnp.where(fits, jnp.arange(len(options), dtype=jnp.int32), 0))

    def choose(low, high):
        if high - low == 1:
            return functools.partial(layer, low, options[low])
        middle = (low + high) // 2
        return lambda *args: lax.cond(which >= middle, choose(middle, high), choose(low, middle), *args)

    outs = choose(0, len(options))(*args)
    return (*outs[:9], outs[9].reshape(G * J))


def solution(mesh):
    tok = P(("expert", "hidden"), None)
    par = P("expert", "hidden")
    win = P("expert", None, "hidden")
    wout = P("expert", "hidden", None)
    return jax.shard_map(
        on_device,
        mesh=mesh,
        in_specs=(tok, tok, P(), par, par, par, win, par, wout, par, tok),
        out_specs=(tok, tok, par, par, par, win, par, wout, par, P()),
        check_vma=False,
    )
```

```python
import functools

import jax
import jax.numpy as jnp
from jax import lax
from jax.experimental import pallas as pl
from jax.experimental.pallas import tpu as pltpu
from jax.sharding import PartitionSpec as P

EPS = 1e-05
MESH = pl.DeviceIdType.MESH
F32 = jnp.float32
BF16 = jnp.bfloat16
TILE = 256
PIECES = 3
GELU_A = 0.7978845608028654
GELU_B = 0.044715
SHAPES = ((8, 8, 8, 8), (8, 7, 6, 5), (8, 6, 4, 3),)


def contract(a, b, dims=((1,), (0,))):
    return lax.dot_general(a, b, (dims, ((), ())), preferred_element_type=F32)


def iota(shape, axis):
    return lax.broadcasted_iota(jnp.int32, shape, axis)


def ones_where(mask):
    return mask.astype(F32).astype(BF16)


def per(index, size, count):
    return jnp.floor((index.astype(F32) + 0.5) * (1.0 / size)).astype(jnp.int32)


def layer_kernel(
    dims, sizes,
    asg, lens, cent, gain, bias, bout, bin_, tok_in, cot_in, win, wout,
    home, ret, o_slot, o_cent, o_gain, o_bias, o_win, o_bin, o_wout, o_bout, o_mean,
    vwin, vwout, gat, act, pg, sbuf, rbuf, snd, rcv, xg, spread, pick, unpick, pick_count,
    par, stats, zs, mg, grads, gbuf, normed_of, turned,
    w_sem, par_s, par_r, zs_s, zs_r, mg_s, mg_r, gb_s, gb_r,
    disp_s, disp_r, ret_s, ret_r, gat_s, gat_r, red_s, red_r,
):
    G, H, J, S, MSG, R, T, D, F, PW, seq_len = dims
    e, z = lax.axis_index("expert"), lax.axis_index("hidden")
    E, GM, N = G * J, G * MSG, H * R
    parts = D // TILE
    BLOCK = R

    def cols(t, size=TILE):
        return pl.ds(pl.multiple_of(t * size, size), size)

    def rows(start, size):
        return pl.ds(pl.multiple_of(start, 16), size)

    def loop(count, body):
        def step(i, _):
            body(i)
            return 0

        lax.fori_loop(0, count, step, 0)

    barrier = pltpu.get_barrier_semaphore()
    for d in range(1, H):
        pl.semaphore_signal(barrier, inc=1, device_id=(e, (z + d) % H), device_id_type=MESH)
    for d in range(1, G):
        pl.semaphore_signal(barrier, inc=1, device_id=((e + d) % G, z), device_id_type=MESH)

    loads = []
    for a, source in enumerate((tok_in, cot_in)):
        for part in range(parts):
            loads.append(pltpu.make_async_copy(
                source.at[:, pl.ds(part * TILE, TILE)], home.at[a, pl.ds(part * T, T), :],
                w_sem.at[a * parts + part]))
    weights = [
        pltpu.make_async_copy(win, vwin, w_sem.at[2 * parts]),
        pltpu.make_async_copy(wout, vwout, w_sem.at[2 * parts + 1]),
    ]
    for copy in loads + weights:
        copy.start()

    own_cols = cols(z, PW)
    par[pl.ds(0, J), own_cols] = gain[...]
    par[pl.ds(J, J), own_cols] = bias[...]
    par[pl.ds(2 * J, J), own_cols] = cent[...].astype(F32)
    par[pl.ds(3 * J, J), own_cols] = bout[...]

    expert = asg[...]
    place = (e * H + z) * T
    length = lens[place // seq_len]
    live = (place % seq_len + iota((1, T), 1)) < length
    sub_e = iota((E, 1), 0)
    hot = ((expert == sub_e) & live).astype(F32)
    earlier = ones_where(iota((T, T), 0) < iota((T, T), 1))
    before = contract(hot.astype(BF16), earlier)
    group = per(sub_e, J, G)
    inner = sub_e - group * J
    rank = jnp.sum(hot * before, axis=0, keepdims=True).astype(jnp.int32)
    to_group = jnp.sum(hot * group.astype(F32), axis=0, keepdims=True).astype(jnp.int32)
    to_inner = jnp.sum(hot * inner.astype(F32), axis=0, keepdims=True).astype(jnp.int32)
    to_inner = jnp.where(live, to_inner, -1)
    message = to_group * MSG
    o_slot[...] = jnp.broadcast_to(jnp.where(live, to_inner * GM + message + rank, -D * D), (8, T))

    pl.semaphore_wait(barrier, (H - 1) + (G - 1))

    def par_copy(d, source):
        return pltpu.make_async_remote_copy(
            src_ref=par.at[:, cols(source, PW)], dst_ref=par.at[:, cols(source, PW)],
            send_sem=par_s.at[d], recv_sem=par_r.at[d],
            device_id=(e, (z + d) % H), device_id_type=MESH)

    for d in range(1, H):
        par_copy(d, z).start()

    def msg(k):
        return pl.ds(pl.multiple_of(k * MSG, MSG), MSG)

    def disp_copy(j, a, d, target):
        return pltpu.make_async_remote_copy(
            src_ref=snd.at[j, a, msg(target)], dst_ref=rcv.at[j, a, msg(e)],
            send_sem=disp_s.at[j, a, d], recv_sem=disp_r.at[j, a, d],
            device_id=(target, z), device_id_type=MESH)

    def disp_in(j, a, d):
        k = (e - d + G) % G
        return pltpu.make_async_remote_copy(
            src_ref=snd.at[j, a, msg(k)], dst_ref=rcv.at[j, a, msg(k)],
            send_sem=disp_s.at[j, a, d], recv_sem=disp_r.at[j, a, d],
            device_id=((e + d) % G, z), device_id_type=MESH)

    def dispatch(i):
        j, a = i // 2, i % 2
        row = iota((GM, T), 0)
        mine = to_inner == j

        @pl.when(a == 0)
        def _():
            at = jnp.where(mine, message + rank, -D * D)
            for part in range(parts):
                spread[:, pl.ds(part * T, T)] = ones_where(at + part * S == row)

        for b in range(2):
            @pl.when(jnp.logical_and(j == 0, a == b))
            def _(b=b):
                for copy in loads[b * parts:(b + 1) * parts]:
                    copy.wait()

        counted = jnp.where(mine & (a == 0), message + parts * S, -1)
        v = contract(spread[...], home[a]) + contract(ones_where(counted == row), jnp.ones((T, TILE), BF16))
        snd[j, a] = v.astype(BF16)
        for d in range(1, G):
            disp_copy(j, a, d, (e + d) % G).start()
        rcv[j, a, msg(e), :] = snd[j, a, msg(e), :]

    loop(2 * J, dispatch)

    def row_of(c):
        k = per(c, MSG, G)
        start = jnp.full(c.shape, -D * D, jnp.int32)
        filled_before = jnp.int32(0)
        for i in range(G):
            first = (i * H + z) * T
            some = lens[first // seq_len] > first % seq_len
            start = jnp.where((k == i) & some, filled_before * S, start)
            filled_before = filled_before + some.astype(jnp.int32)
        return start, c - k * MSG

    start, within = row_of(iota((1, GM), 1))
    down = iota((R, GM), 0)
    for part in range(parts):
        i = within - part * S
        pick[pl.ds(part * R, R), :] = ones_where(jnp.where((i >= 0) & (i < S), start + i, -1) == down)
    counts_at = jnp.where(within == parts * S, start, -D * D)
    pick_count[...] = ones_where((down >= counts_at) & (down < counts_at + S))
    start, within = row_of(iota((GM, 1), 0))
    across = iota((1, parts * R), 1)
    across_part = per(across, R, parts)
    i = within - across_part * S
    unpick[...] = ones_where((i >= 0) & (i < S) & (start + i == across - across_part * R))

    for h in range(H):
        if sizes[h] < R:
            gat[:, :, pl.ds(h * R + sizes[h], R - sizes[h]), :] = jnp.zeros((2, J, R - sizes[h], D), BF16)

    def clear(slot_at):
        def one(i):
            rbuf[i // J, i % J, slot_at] = jnp.zeros((R, D), BF16)

        loop(2 * J, one)

    pl.when(z == 0)(lambda: clear(H))
    pl.when(z == H - 1)(lambda: clear(H - 1))

    o_bin[...] = jnp.zeros_like(o_bin)

    for d in range(1, H):
        par_copy(d, (z - d + H) % H).wait_recv()

    def with_rows(chunk, body):
        for size in sorted(set(sizes)):
            planes = [h for h in range(H) if sizes[h] == size]
            if len(planes) == H:
                body(size)
            else:
                hit = chunk == planes[0]
                for h in planes[1:]:
                    hit = jnp.logical_or(hit, chunk == h)
                pl.when(hit)(functools.partial(body, size))

    def gat_copy(a, j, chunk, up, size):
        at = (a, j, rows(chunk * R, size))
        return pltpu.make_async_remote_copy(
            src_ref=gat.at[at], dst_ref=gat.at[at],
            send_sem=gat_s.at[up, a, j, chunk], recv_sem=gat_r.at[a, j, chunk],
            device_id=(e, jnp.clip(z + 2 * up - 1, 0, H - 1)), device_id_type=MESH)

    def send_gat(a, j, chunk, up, size):
        @pl.when(jnp.where(up == 1, z < H - 1, z > 0))
        def _():
            gat_copy(a, j, chunk, up, size).start()

    def send_own(a, j):
        def both(size):
            send_gat(a, j, z, 1, size)
            send_gat(a, j, z, 0, size)

        with_rows(z, both)

    def piece_of(size, piece):
        start = 0
        for i in range(piece + 1):
            count = -(-(size - start) // (16 * (PIECES - i))) * 16
            start = start + count
        return start - count, count

    def red_copy(a, j, piece, to, up, size):
        slot_to = jnp.where(jnp.logical_and(up == 1, to == z + 1), H, to)
        at = pl.ds(*piece_of(size, piece))
        return pltpu.make_async_remote_copy(
            src_ref=sbuf.at[a, j, to, at], dst_ref=rbuf.at[a, j, slot_to, at],
            send_sem=red_s.at[a, j, piece, to], recv_sem=red_r.at[a, j, piece, slot_to],
            device_id=(e, jnp.clip(z + 2 * up - 1, 0, H - 1)), device_id_type=MESH)

    def red_in(a, j, piece, slot_at, size):
        at = pl.ds(*piece_of(size, piece))
        return pltpu.make_async_remote_copy(
            src_ref=sbuf.at[a, j, 0, at], dst_ref=rbuf.at[a, j, slot_at, at],
            send_sem=red_s.at[a, j, piece, 0], recv_sem=red_r.at[a, j, piece, slot_at],
            device_id=(e, jnp.clip(z + 1, 0, H - 1)), device_id_type=MESH)

    def quarter(part, b):
        return pl.ds(pl.multiple_of(part * R + b * BLOCK, 16), BLOCK)

    lane8 = iota((8, 128), 1)
    r1 = iota((R, 1), 0)
    rank_in = (r1 - S * per(r1, S, G)).astype(F32)
    zs[z] = jnp.zeros((16, 128), F32)

    def take_in(j, a):
        for d in range(1, G):
            disp_in(j, a, d).wait_recv()
        xg[j, a] = contract(pick[...], rcv[j, a]).astype(BF16)

    def prepare(j):
        take_in(j, 0)
        count = contract(pick_count[...], rcv[j, 0, :, pl.ds(0, 128)])[:, 0:1]
        stats[3, j] = (rank_in < count).astype(F32)

        def block(b):
            x = [xg[j, 0, quarter(part, b), :].astype(F32) for part in range(parts)]
            mean = sum(jnp.sum(v, axis=1, keepdims=True) for v in x) * (1.0 / D)
            x_mid = [v - mean for v in x]
            var = sum(jnp.sum(v * v, axis=1, keepdims=True) for v in x_mid) * (1.0 / D)
            factor = lax.rsqrt(var + EPS)
            score = 0.0
            at = rows(b * BLOCK, BLOCK)
            for part in range(parts):
                lanes = pl.ds(part * TILE, TILE)
                normed = x_mid[part] * factor
                lifted = normed * par[pl.ds(j, 1), lanes] + par[pl.ds(J + j, 1), lanes]
                gat[0, j, rows(z * R + b * BLOCK, BLOCK), lanes] = lifted.astype(BF16)
                normed_of[j, at, lanes] = normed
                score = score + jnp.sum(x[part] * par[pl.ds(2 * J + j, 1), lanes], axis=1, keepdims=True)
            stats[0, j, at] = jax.nn.sigmoid(score)
            stats[1, j, at] = factor

        loop(R // BLOCK, block)
        send_own(0, j)
        take_in(j, 1)

        def weigh(b):
            at = rows(b * BLOCK, BLOCK)
            for part in range(parts):
                g = xg[j, 1, quarter(part, b), :].astype(F32)
                gat[1, j, rows(z * R + b * BLOCK, BLOCK), pl.ds(part * TILE, TILE)] = (stats[0, j, at] * g).astype(BF16)

        loop(R // BLOCK, weigh)
        send_own(1, j)
        total = jnp.sum(stats[3, j] * stats[0, j], axis=0, keepdims=True)
        number = jnp.sum(stats[3, j], axis=0, keepdims=True)
        zs[z, pl.ds(0, 8), :] += jnp.where(lane8 == j, total, 0.0)
        zs[z, pl.ds(8, 8), :] += jnp.where(lane8 == j, number, 0.0)

    loop(J, prepare)

    def zs_copy(d, source):
        return pltpu.make_async_remote_copy(
            src_ref=zs.at[source], dst_ref=zs.at[source],
            send_sem=zs_s.at[d], recv_sem=zs_r.at[d],
            device_id=(e, (z + d) % H), device_id_type=MESH)

    for d in range(1, H):
        zs_copy(d, z).start()

    for copy in weights:
        copy.wait()

    wide = 2 * TILE

    def compute(chunk, j):
        mine = rows(chunk * R, R)

        def first(t):
            pre = contract(gat[0, j, mine, :], vwin[j, :, cols(t, wide)]) + bin_[pl.ds(j, 1), cols(t, wide)]
            sq = pre * pre
            th = jnp.tanh(pre * (GELU_A + (GELU_A * GELU_B) * sq))
            cdf = 0.5 + 0.5 * th
            slope = cdf + pre * (0.5 - 0.5 * th * th) * (GELU_A + (3.0 * GELU_A * GELU_B) * sq)
            act[j, mine, cols(t, wide)] = (pre * cdf).astype(BF16)
            act_grad = contract(gat[1, j, mine, :], vwout[j, cols(t, wide), :], ((1,), (1,)))
            pre_grad = (act_grad * slope).astype(BF16)
            pg[j, mine, cols(t, wide)] = pre_grad
            o_bin[pl.ds(j, 1), cols(t, wide)] += jnp.sum(pre_grad.astype(F32), axis=0, keepdims=True)

        loop(F // wide, first)

        def second(t):
            v = contract(act[j, mine, :], vwout[j, :, cols(t, wide)])
            sbuf[0, j, chunk, :, cols(t, wide)] = v.astype(BF16)
            w = contract(pg[j, mine, :], vwin[j, cols(t, wide), :], ((1,), (1,)))
            sbuf[1, j, chunk, :, cols(t, wide)] = w.astype(BF16)

        loop(D // wide, second)

    def outer(left, right, to, tall, wide):
        turned[pl.ds(0, tall), :] = jnp.transpose(left)

        def tile(t):
            to[:, cols(t)] = contract(turned[pl.ds(0, tall), :], right[:, cols(t)])

        loop(wide // TILE, tile)

    def mg_copy(d, source):
        return pltpu.make_async_remote_copy(
            src_ref=mg.at[source], dst_ref=mg.at[source],
            send_sem=mg_s.at[d], recv_sem=mg_r.at[d],
            device_id=((e + d) % G, z), device_id_type=MESH)

    def gb_copy(d, source, target):
        return pltpu.make_async_remote_copy(
            src_ref=grads.at[:, cols(target, PW)], dst_ref=gbuf.at[source],
            send_sem=gb_s.at[d], recv_sem=gb_r.at[d],
            device_id=(e, (z + d) % H), device_id_type=MESH)

    def ret_copy(j, a, d, target):
        return pltpu.make_async_remote_copy(
            src_ref=snd.at[j, a, msg(target)], dst_ref=ret.at[a, rows(j * GM + e * MSG, MSG)],
            send_sem=ret_s.at[j, a, d], recv_sem=ret_r.at[j, a, d],
            device_id=(target, z), device_id_type=MESH)

    def ret_in(j, a, d):
        k = (e - d + G) % G
        return pltpu.make_async_remote_copy(
            src_ref=snd.at[j, a, msg(k)], dst_ref=ret.at[a, rows(j * GM + k * MSG, MSG)],
            send_sem=ret_s.at[j, a, d], recv_sem=ret_r.at[j, a, d],
            device_id=((e + d) % G, z), device_id_type=MESH)

    def wait_sums(a, j):
        def both(size):
            for piece in range(PIECES):
                @pl.when(z < H - 1)
                def _(piece=piece):
                    red_in(a, j, piece, z, size).wait_recv()

                @pl.when(z > 0)
                def _(piece=piece):
                    red_in(a, j, piece, H, size).wait_recv()

        with_rows(z, both)

    def summed(a, j, b, part):
        at = (rows(b * BLOCK, BLOCK), pl.ds(part * TILE, TILE))
        v = sbuf[(a, j, z, *at)].astype(F32) + rbuf[(a, j, z, *at)].astype(F32) + rbuf[(a, j, H, *at)].astype(F32)
        return jnp.where(stats[3, j, at[0]] > 0.5, v, 0.0)

    def send_home(j, a):
        snd[j, a] = contract(unpick[...], xg[j, a]).astype(BF16)
        for d in range(1, G):
            ret_copy(j, a, d, (e + d) % G).start()
        ret[a, rows(j * GM + e * MSG, MSG), :] = snd[j, a, msg(e), :]

    def finish(j):
        wait_sums(0, j)

        def forward(b):
            at = rows(b * BLOCK, BLOCK)
            gate = stats[0, j, at]
            gate_grad = 0.0
            for part in range(parts):
                lanes = pl.ds(part * TILE, TILE)
                branch = (summed(0, j, b, part) + par[pl.ds(3 * J + j, 1), lanes]).astype(BF16).astype(F32)
                x = xg[j, 0, quarter(part, b), :].astype(F32)
                gate_grad = gate_grad + jnp.sum(
                    xg[j, 1, quarter(part, b), :].astype(F32) * branch, axis=1, keepdims=True)
                rbuf[0, j, H, at, lanes] = x.astype(BF16)
                xg[j, 0, quarter(part, b), :] = (x + gate * branch).astype(BF16)
            score_grad = gate_grad * gate * (1.0 - gate)
            stats[2, j, at] = score_grad
            for part in range(parts):
                lanes = pl.ds(part * TILE, TILE)
                x = rbuf[0, j, H, at, lanes].astype(F32)
                grads[pl.ds(2 * J + j, 1), lanes] += jnp.sum(score_grad * x, axis=0, keepdims=True)
                sent = gat[1, j, rows(z * R + b * BLOCK, BLOCK), lanes].astype(F32)
                grads[pl.ds(3 * J + j, 1), lanes] += jnp.sum(sent, axis=0, keepdims=True)

        loop(R // BLOCK, forward)
        send_home(j, 0)
        wait_sums(1, j)

        def backward(b):
            at = rows(b * BLOCK, BLOCK)
            factor, score_grad = stats[1, j, at], stats[2, j, at]
            sum_n, sum_nn = 0.0, 0.0
            n_grads = []
            for part in range(parts):
                lanes = pl.ds(part * TILE, TILE)
                lifted_grad = summed(1, j, b, part)
                normed = normed_of[j, at, lanes]
                grads[pl.ds(j, 1), lanes] += jnp.sum(lifted_grad * normed, axis=0, keepdims=True)
                grads[pl.ds(J + j, 1), lanes] += jnp.sum(lifted_grad, axis=0, keepdims=True)
                n_grad = lifted_grad * par[pl.ds(j, 1), lanes]
                sum_n = sum_n + jnp.sum(n_grad, axis=1, keepdims=True)
                sum_nn = sum_nn + jnp.sum(n_grad * normed, axis=1, keepdims=True)
                n_grads.append(n_grad)
            for part in range(parts):
                lanes = pl.ds(part * TILE, TILE)
                rows_grad = factor * (
                    n_grads[part] - sum_n * (1.0 / D) - normed_of[j, at, lanes] * (sum_nn * (1.0 / D)))
                rows_grad = rows_grad.astype(BF16).astype(F32)
                g = xg[j, 1, quarter(part, b), :].astype(F32)
                moved = g + score_grad * par[pl.ds(2 * J + j, 1), lanes] + rows_grad
                xg[j, 1, quarter(part, b), :] = moved.astype(BF16)

        loop(R // BLOCK, backward)
        send_home(j, 1)

    last = jnp.maximum(z, H - 1 - z)
    grads[...] = jnp.zeros_like(grads)

    def sent(i):
        for d in range(1, G):
            disp_copy(i // 2, i % 2, d, (e + d) % G).wait_send()

    def starts(up):
        return jnp.where(up == 1, z == 0, z == H - 1)

    def passes(up, to):
        return jnp.where(up == 1, (z > 0) & (z < to), (z < H - 1) & (z > to))

    def begin(to, j, up):
        def both(size):
            for a in range(2):
                for piece in range(PIECES):
                    red_copy(a, j, piece, to, up, size).start()

        with_rows(to, both)

    def pass_sum(a, j, to, up):
        def both(size):
            for piece in range(PIECES):
                red_in(a, j, piece, to, size).wait_recv()
                at = (a, j, to, pl.ds(*piece_of(size, piece)))
                sbuf[at] = (sbuf[at].astype(F32) + rbuf[at].astype(F32)).astype(BF16)
                red_copy(a, j, piece, to, up, size).start()

        with_rows(to, both)

    def item(q):
        s, j = q // J, q % J

        def forwarded(i):
            up, a = 1 - i // 2, i % 2
            chunk = jnp.where(up == 1, z - s, z + s)

            @pl.when((s > 0) & (chunk >= 0) & (chunk < H))
            def _():
                def pass_on(size):
                    gat_copy(a, j, chunk, up, size).wait_recv()
                    send_gat(a, j, chunk, up, size)

                with_rows(chunk, pass_on)

        loop(4, forwarded)

        def side(d):
            chunk = jnp.where(d == 0, z - s, z + s)

            @pl.when((chunk >= 0) & (chunk < H) & ((s > 0) | (d == 0)))
            def _():
                compute(chunk, j)

                @pl.when(starts(d) & (s > 0) & ((s > 1) | (j < J - 1)))
                def _():
                    begin(chunk, j, d)

        loop(2, side)

        def through(i):
            a, up = i // 2, (i + jnp.where(z >= H // 2, 0, 1)) % 2
            to = jnp.where(up == 1, s, H - 1 - s)
            near = (a == 1) & (to == z + 2 * up - 1) & (j == J - 1) & (s < H - 1)

            @pl.when((s > 0) & passes(up, to) & jnp.logical_not(near))
            def _():
                pass_sum(a, j, to, up)

        loop(4, through)

        @pl.when(q == H * J - 1)
        def _():
            for up in range(2):
                to = z + 2 * up - 1

                @pl.when(starts(up) & (to >= 0) & (to < H))
                def _(up=up, to=to):
                    begin(to, J - 1, up)

                @pl.when(passes(up, to) & (jnp.where(up == 1, to, H - 1 - to) < H - 1))
                def _(up=up, to=to):
                    pass_sum(1, J - 1, to, up)

        @pl.when((s == last) & (j == 0))
        def _():
            for d in range(1, H):
                zs_copy(d, (z - d + H) % H).wait_recv()
            both = zs[0]
            for h in range(1, H):
                both = both + zs[h]
            mg[e] = both[0:8] / jnp.maximum(both[8:16], 1.0)
            for d in range(1, G):
                mg_copy(d, e).start()

        @pl.when(s == last)
        def _():
            outer(gat[0, j], pg.at[j], o_win.at[j], D, F)
            outer(act[j], gat.at[1, j], o_wout.at[j], F, D)

    loop(H * J, item)
    loop(2 * J, sent)
    loop(J, finish)
    for d in range(1, H):
        gb_copy(d, z, (z + d) % H).start()

    gbuf[z] = grads[:, own_cols]
    for d in range(1, G):
        mg_copy(d, (e - d + G) % G).wait_recv()
    means = jnp.zeros((8, 128), F32)
    for k in range(G):
        v = mg[k] if k == 0 else pltpu.roll(mg[k], k * J, 1)
        means = jnp.where((lane8 >= k * J) & (lane8 < k * J + J), v, means)
    o_mean[...] = means[0:1, 0:E]

    for d in range(1, H):
        gb_copy(d, (z - d + H) % H, z).wait_recv()
    small = gbuf[0]
    for h in range(1, H):
        small = small + gbuf[h]
    o_gain[...] = small[0:J]
    o_bias[...] = small[J:2 * J]
    o_cent[...] = small[2 * J:3 * J]
    o_bout[...] = small[3 * J:4 * J]

    for d in range(1, H):
        par_copy(d, z).wait_send()
        zs_copy(d, z).wait_send()
        gb_copy(d, z, (z + d) % H).wait_send()
    for d in range(1, G):
        mg_copy(d, e).wait_send()

    def drain(i):
        a, j, h = i // (J * H), i // H % J, i % H

        def wait(size):
            @pl.when((z < H - 1) & (h <= z))
            def _():
                gat_copy(a, j, h, 1, size).wait_send()

            @pl.when((z > 0) & (h >= z))
            def _():
                gat_copy(a, j, h, 0, size).wait_send()

            @pl.when(h != z)
            def _():
                for piece in range(PIECES):
                    red_copy(a, j, piece, h, jnp.where(h > z, 1, 0), size).wait_send()

        with_rows(h, wait)

    loop(2 * J * H, drain)

    def arrived(i):
        j, a = i // 2, i % 2
        for d in range(1, G):
            ret_in(j, a, d).wait_recv()
            ret_copy(j, a, d, (e + d) % G).wait_send()

    loop(2 * J, arrived)


def deliver_kernel(dims, home, ret, slot, *refs):
    G, H, J, S, MSG, R, T, D, F, PW, seq_len = dims
    results, (o_mixed, o_tg, *outs), (mixed, moved, sem) = refs[:8], refs[8:18], refs[18:]
    copies = [pltpu.make_async_copy(a, b, sem.at[i]) for i, (a, b) in enumerate(zip(results, outs))]
    for i in (3, 5, 0, 1, 2, 4, 6, 7):
        copies[i].start()

    spot = jnp.transpose(jnp.broadcast_to(slot[pl.ds(0, 1), :].astype(F32), (128, T)))[:, 0:1].astype(jnp.int32)
    live_rows = spot >= 0
    m = iota((T, J * G * MSG), 1)
    for part in range(D // TILE):
        take = ones_where(spot + part * S == m)
        at = pl.ds(part * TILE, TILE)
        for a, to in enumerate((mixed, moved)):
            kept = home[a, pl.ds(part * T, T), :].astype(F32)
            to[:, at] = jnp.where(live_rows, contract(take, ret[a]), kept).astype(BF16)
    for i, (a, b) in enumerate(((mixed, o_mixed), (moved, o_tg))):
        copies.append(pltpu.make_async_copy(a, b, sem.at[8 + i]))
        copies[-1].start()
    for copy in copies:
        copy.wait()


def on_device(
    tokens, assignment, lengths, centroids, ln_gain, ln_bias, w_in, b_in, w_out, b_out, cotangent
):
    T, D = tokens.shape
    G, H = lax.axis_size("expert"), lax.axis_size("hidden")
    J, F = w_in.shape[0], w_in.shape[2]
    PW = centroids.shape[1]
    S = max(2, 9 * T // (8 * J * G))
    parts = D // TILE
    MSG = -(-(parts * S + 1) // 16) * 16
    R, GM, N = G * S, G * MSG, H * G * S
    seq_len = min(2048, H * T)
    dims = (G, H, J, S, MSG, R, T, D, F, PW, seq_len)
    vm = pl.BlockSpec(memory_space=pltpu.VMEM)
    hbm = pl.BlockSpec(memory_space=pl.ANY)
    sm = pl.BlockSpec(memory_space=pltpu.SMEM)
    dma = pltpu.SemaphoreType.DMA
    buffers = [
        ((J, D, F), BF16),
        ((J, F, D), BF16),
        ((2, J, N, D), BF16),
        ((J, N, F), BF16),
        ((J, N, F), BF16),
        ((2, J, H, R, D), BF16),
        ((2, J, H + 1, R, D), BF16),
        ((J, 2, GM, TILE), BF16),
        ((J, 2, GM, TILE), BF16),
        ((J, 2, parts * R, TILE), BF16),
        ((GM, parts * T), BF16),
        ((parts * R, GM), BF16),
        ((GM, parts * R), BF16),
        ((R, GM), BF16),
        ((4 * J, D), F32),
        ((4, J, R, 1), F32),
        ((H, 16, 128), F32),
        ((G, 8, 128), F32),
        ((4 * J, D), F32),
        ((H, 4 * J, PW), F32),
        ((J, R, D), F32),
        ((max(D, F), N), BF16),
    ]
    taken = sum(
        jnp.dtype(t).itemsize * -(-s[-1] // 128) * 128 * functools.reduce(lambda a, b: a * b, s[:-1]) for s, t in buffers
    )

    results = [(J, PW), (J, PW), (J, PW), (J, D, F), (J, F), (J, F, D), (J, PW), (1, G * J)]
    shape = jax.ShapeDtypeStruct

    def layer(number, sizes, *args):
        made = pl.pallas_call(
            functools.partial(layer_kernel, dims, sizes),
            name="layer",
            out_shape=[
                pltpu.VMEM((2, parts * T, TILE), BF16),
                pltpu.VMEM((2, J * GM, TILE), BF16),
                pltpu.VMEM((8, T), jnp.int32),
                *[pltpu.VMEM(s, F32) for s in results],
            ],
            in_specs=[vm, sm, vm, vm, vm, vm, vm, hbm, hbm, hbm, hbm],
            out_specs=[vm] * 11,
            scratch_shapes=[
                *[pltpu.VMEM(s, t) for s, t in buffers],
                dma((2 * parts + 2,)),
                dma((H,)), dma((H,)),
                dma((H,)), dma((H,)),
                dma((G,)), dma((G,)),
                dma((H,)), dma((H,)),
                dma((J, 2, G)), dma((J, 2, G)),
                dma((J, 2, G)), dma((J, 2, G)),
                dma((2, 2, J, H)), dma((2, J, H)),
                dma((2, J, PIECES, H)), dma((2, J, PIECES, H + 1)),
            ],
            compiler_params=pltpu.CompilerParams(
                collective_id=number, has_side_effects=True, vmem_limit_bytes=taken + 3 * 2**20
            ),
            cost_estimate=pl.CostEstimate(
                flops=12 * J * N * D * F, bytes_accessed=30 * 2**20, transcendentals=J * N * F
            ),
        )(*args)
        return pl.pallas_call(
            functools.partial(deliver_kernel, dims),
            name="deliver",
            out_shape=[shape((T, D), BF16), shape((T, D), BF16), *[shape(s, F32) for s in results]],
            in_specs=[vm] * 11,
            out_specs=[hbm] * 10,
            scratch_shapes=[pltpu.VMEM((T, D), BF16), pltpu.VMEM((T, D), BF16), dma((10,))],
            compiler_params=pltpu.CompilerParams(vmem_limit_bytes=8 * 2**20),
        )(*made)

    args = (
        assignment.reshape(1, T), lengths, centroids, ln_gain, ln_bias, b_out, b_in, tokens, cotangent, w_in, w_out
    )
    options = []
    for shares in SHAPES:
        needed = [-(-G * shares[4 * h // H] // 8) * S for h in range(H)]
        options.append(tuple(-(-r // 16) * 16 for r in needed))
    bits = G.bit_length()
    if len(options) > 1 and seq_len == H * T and bits * H < 32:
        alive = lengths[:, None] > jnp.asarray([h * T for h in range(H)], jnp.int32)
        packed = jnp.sum(jnp.where(alive, jnp.asarray([1 << bits * h for h in range(H)], jnp.int32), 0))
        which = jnp.int32(0)
        for i, rows in enumerate(options[1:]):
            fits = True
            for h in range(H):
                fits = fits & ((packed >> (bits * h)) % (1 << bits) * S <= rows[h])
            which = jnp.where(fits, i + 1, which)
    elif len(options) > 1:
        first = (jnp.arange(G, dtype=jnp.int32)[:, None] * H + jnp.arange(H, dtype=jnp.int32)[None, :]) * T
        needed = S * jnp.sum((lengths[first // seq_len] > first % seq_len).astype(jnp.int32), axis=0)
        fits = jnp.all(needed[None, :] <= jnp.asarray(options, jnp.int32), axis=1)
        which = jnp.max(jnp.where(fits, jnp.arange(len(options), dtype=jnp.int32), 0))

    def choose(low, high):
        if high - low == 1:
            return functools.partial(layer, low, options[low])
        middle = (low + high) // 2
        return lambda *args: lax.cond(which >= middle, choose(middle, high), choose(low, middle), *args)

    outs = choose(0, len(options))(*args)
    return (*outs[:9], outs[9].reshape(G * J))


def solution(mesh):
    tok = P(("expert", "hidden"), None)
    par = P("expert", "hidden")
    win = P("expert", None, "hidden")
    wout = P("expert", "hidden", None)
    return jax.shard_map(
        on_device,
        mesh=mesh,
        in_specs=(tok, tok, P(), par, par, par, win, par, wout, par, tok),
        out_specs=(tok, tok, par, par, par, win, par, wout, par, P()),
        check_vma=False,
    )
```

```python
import functools

import jax
import jax.numpy as jnp
from jax import lax
from jax.experimental import pallas as pl
from jax.experimental.pallas import tpu as pltpu
from jax.sharding import PartitionSpec as P

EPS = 1e-05
MESH = pl.DeviceIdType.MESH
F32 = jnp.float32
BF16 = jnp.bfloat16
TILE = 256
PIECES = 3
GELU_A = 0.7978845608028654
GELU_B = 0.044715
SHAPES = ((8, 8, 8, 8), (8, 7, 6, 5), (8, 6, 4, 3),)


def contract(a, b, dims=((1,), (0,))):
    return lax.dot_general(a, b, (dims, ((), ())), preferred_element_type=F32)


def iota(shape, axis):
    return lax.broadcasted_iota(jnp.int32, shape, axis)


def ones_where(mask):
    return mask.astype(F32).astype(BF16)


def per(index, size, count):
    return jnp.floor((index.astype(F32) + 0.5) * (1.0 / size)).astype(jnp.int32)


def layer_kernel(
    dims, sizes,
    asg, lens, cent, gain, bias, bout, bin_, tok_in, cot_in, win, wout,
    home, ret, o_slot, o_cent, o_gain, o_bias, o_win, o_bin, o_wout, o_bout, o_mean,
    vwin, vwout, gat, act, pg, sbuf, rbuf, snd, rcv, xg, spread, pick, unpick, pick_count,
    par, stats, zs, mg, grads, gbuf, normed_of, turned,
    w_sem, par_s, par_r, zs_s, zs_r, mg_s, mg_r, gb_s, gb_r,
    disp_s, disp_r, ret_s, ret_r, gat_s, gat_r, red_s, red_r,
):
    G, H, J, S, MSG, R, T, D, F, PW, seq_len = dims
    e, z = lax.axis_index("expert"), lax.axis_index("hidden")
    E, GM, N = G * J, G * MSG, H * R
    parts = D // TILE
    BLOCK = R

    def cols(t, size=TILE):
        return pl.ds(pl.multiple_of(t * size, size), size)

    def rows(start, size):
        return pl.ds(pl.multiple_of(start, 16), size)

    def loop(count, body):
        def step(i, _):
            body(i)
            return 0

        lax.fori_loop(0, count, step, 0)

    barrier = pltpu.get_barrier_semaphore()
    for d in range(1, H):
        pl.semaphore_signal(barrier, inc=1, device_id=(e, (z + d) % H), device_id_type=MESH)
    for d in range(1, G):
        pl.semaphore_signal(barrier, inc=1, device_id=((e + d) % G, z), device_id_type=MESH)

    loads = []
    for a, source in enumerate((tok_in, cot_in)):
        for part in range(parts):
            loads.append(pltpu.make_async_copy(
                source.at[:, pl.ds(part * TILE, TILE)], home.at[a, pl.ds(part * T, T), :],
                w_sem.at[a * parts + part]))
    weights = [
        pltpu.make_async_copy(win, vwin, w_sem.at[2 * parts]),
        pltpu.make_async_copy(wout, vwout, w_sem.at[2 * parts + 1]),
    ]
    for copy in loads + weights:
        copy.start()

    own_cols = cols(z, PW)
    par[pl.ds(0, J), own_cols] = gain[...]
    par[pl.ds(J, J), own_cols] = bias[...]
    par[pl.ds(2 * J, J), own_cols] = cent[...].astype(F32)
    par[pl.ds(3 * J, J), own_cols] = bout[...]

    expert = asg[...]
    place = (e * H + z) * T
    length = lens[place // seq_len]
    live = (place % seq_len + iota((1, T), 1)) < length
    sub_e = iota((E, 1), 0)
    hot = ((expert == sub_e) & live).astype(F32)
    earlier = ones_where(iota((T, T), 0) < iota((T, T), 1))
    before = contract(hot.astype(BF16), earlier)
    group = per(sub_e, J, G)
    inner = sub_e - group * J
    rank = jnp.sum(hot * before, axis=0, keepdims=True).astype(jnp.int32)
    to_group = jnp.sum(hot * group.astype(F32), axis=0, keepdims=True).astype(jnp.int32)
    to_inner = jnp.sum(hot * inner.astype(F32), axis=0, keepdims=True).astype(jnp.int32)
    to_inner = jnp.where(live, to_inner, -1)
    message = to_group * MSG
    o_slot[...] = jnp.broadcast_to(jnp.where(live, to_inner * GM + message + rank, -D * D), (8, T))

    pl.semaphore_wait(barrier, (H - 1) + (G - 1))

    def par_copy(d, source):
        return pltpu.make_async_remote_copy(
            src_ref=par.at[:, cols(source, PW)], dst_ref=par.at[:, cols(source, PW)],
            send_sem=par_s.at[d], recv_sem=par_r.at[d],
            device_id=(e, (z + d) % H), device_id_type=MESH)

    for d in range(1, H):
        par_copy(d, z).start()

    def msg(k):
        return pl.ds(pl.multiple_of(k * MSG, MSG), MSG)

    def disp_copy(j, a, d, target):
        return pltpu.make_async_remote_copy(
            src_ref=snd.at[j, a, msg(target)], dst_ref=rcv.at[j, a, msg(e)],
            send_sem=disp_s.at[j, a, d], recv_sem=disp_r.at[j, a, d],
            device_id=(target, z), device_id_type=MESH)

    def disp_in(j, a, d):
        k = (e - d + G) % G
        return pltpu.make_async_remote_copy(
            src_ref=snd.at[j, a, msg(k)], dst_ref=rcv.at[j, a, msg(k)],
            send_sem=disp_s.at[j, a, d], recv_sem=disp_r.at[j, a, d],
            device_id=((e + d) % G, z), device_id_type=MESH)

    def dispatch(i):
        j, a = i // 2, i % 2
        row = iota((GM, T), 0)
        mine = to_inner == j

        @pl.when(a == 0)
        def _():
            at = jnp.where(mine, message + rank, -D * D)
            for part in range(parts):
                spread[:, pl.ds(part * T, T)] = ones_where(at + part * S == row)

        for b in range(2):
            @pl.when(jnp.logical_and(j == 0, a == b))
            def _(b=b):
                for copy in loads[b * parts:(b + 1) * parts]:
                    copy.wait()

        counted = jnp.where(mine & (a == 0), message + parts * S, -1)
        v = contract(spread[...], home[a]) + contract(ones_where(counted == row), jnp.ones((T, TILE), BF16))
        snd[j, a] = v.astype(BF16)
        for d in range(1, G):
            disp_copy(j, a, d, (e + d) % G).start()
        rcv[j, a, msg(e), :] = snd[j, a, msg(e), :]

    loop(2 * J, dispatch)

    def row_of(c):
        k = per(c, MSG, G)
        start = jnp.full(c.shape, -D * D, jnp.int32)
        filled_before = jnp.int32(0)
        for i in range(G):
            first = (i * H + z) * T
            some = lens[first // seq_len] > first % seq_len
            start = jnp.where((k == i) & some, filled_before * S, start)
            filled_before = filled_before + some.astype(jnp.int32)
        return start, c - k * MSG

    start, within = row_of(iota((1, GM), 1))
    down = iota((R, GM), 0)
    for part in range(parts):
        i = within - part * S
        pick[pl.ds(part * R, R), :] = ones_where(jnp.where((i >= 0) & (i < S), start + i, -1) == down)
    counts_at = jnp.where(within == parts * S, start, -D * D)
    pick_count[...] = ones_where((down >= counts_at) & (down < counts_at + S))
    start, within = row_of(iota((GM, 1), 0))
    across = iota((1, parts * R), 1)
    across_part = per(across, R, parts)
    i = within - across_part * S
    unpick[...] = ones_where((i >= 0) & (i < S) & (start + i == across - across_part * R))

    for h in range(H):
        if sizes[h] < R:
            gat[:, :, pl.ds(h * R + sizes[h], R - sizes[h]), :] = jnp.zeros((2, J, R - sizes[h], D), BF16)

    def clear(slot_at):
        def one(i):
            rbuf[i // J, i % J, slot_at] = jnp.zeros((R, D), BF16)

        loop(2 * J, one)

    pl.when(z == 0)(lambda: clear(H))
    pl.when(z == H - 1)(lambda: clear(H - 1))

    o_bin[...] = jnp.zeros_like(o_bin)

    for d in range(1, H):
        par_copy(d, (z - d + H) % H).wait_recv()

    def with_rows(chunk, body):
        for size in sorted(set(sizes)):
            planes = [h for h in range(H) if sizes[h] == size]
            if len(planes) == H:
                body(size)
            else:
                hit = chunk == planes[0]
                for h in planes[1:]:
                    hit = jnp.logical_or(hit, chunk == h)
                pl.when(hit)(functools.partial(body, size))

    def gat_copy(a, j, chunk, up, size):
        at = (a, j, rows(chunk * R, size))
        return pltpu.make_async_remote_copy(
            src_ref=gat.at[at], dst_ref=gat.at[at],
            send_sem=gat_s.at[up, a, j, chunk], recv_sem=gat_r.at[a, j, chunk],
            device_id=(e, jnp.clip(z + 2 * up - 1, 0, H - 1)), device_id_type=MESH)

    def send_gat(a, j, chunk, up, size):
        @pl.when(jnp.where(up == 1, z < H - 1, z > 0))
        def _():
            gat_copy(a, j, chunk, up, size).start()

    def send_own(a, j):
        def both(size):
            send_gat(a, j, z, 1, size)
            send_gat(a, j, z, 0, size)

        with_rows(z, both)

    def piece_of(size, piece):
        start = 0
        for i in range(piece + 1):
            count = -(-(size - start) // (16 * (PIECES - i))) * 16
            start = start + count
        return start - count, count

    def red_copy(a, j, piece, to, up, size):
        slot_to = jnp.where(jnp.logical_and(up == 1, to == z + 1), H, to)
        at = pl.ds(*piece_of(size, piece))
        return pltpu.make_async_remote_copy(
            src_ref=sbuf.at[a, j, to, at], dst_ref=rbuf.at[a, j, slot_to, at],
            send_sem=red_s.at[a, j, piece, to], recv_sem=red_r.at[a, j, piece, slot_to],
            device_id=(e, jnp.clip(z + 2 * up - 1, 0, H - 1)), device_id_type=MESH)

    def red_in(a, j, piece, slot_at, size):
        at = pl.ds(*piece_of(size, piece))
        return pltpu.make_async_remote_copy(
            src_ref=sbuf.at[a, j, 0, at], dst_ref=rbuf.at[a, j, slot_at, at],
            send_sem=red_s.at[a, j, piece, 0], recv_sem=red_r.at[a, j, piece, slot_at],
            device_id=(e, jnp.clip(z + 1, 0, H - 1)), device_id_type=MESH)

    def quarter(part, b):
        return pl.ds(pl.multiple_of(part * R + b * BLOCK, 16), BLOCK)

    lane8 = iota((8, 128), 1)
    r1 = iota((R, 1), 0)
    rank_in = (r1 - S * per(r1, S, G)).astype(F32)
    zs[z] = jnp.zeros((16, 128), F32)

    def take_in(j, a):
        for d in range(1, G):
            disp_in(j, a, d).wait_recv()
        xg[j, a] = contract(pick[...], rcv[j, a]).astype(BF16)

    def prepare(j):
        take_in(j, 0)
        count = contract(pick_count[...], rcv[j, 0, :, pl.ds(0, 128)])[:, 0:1]
        stats[3, j] = (rank_in < count).astype(F32)

        def block(b):
            x = [xg[j, 0, quarter(part, b), :].astype(F32) for part in range(parts)]
            mean = sum(jnp.sum(v, axis=1, keepdims=True) for v in x) * (1.0 / D)
            x_mid = [v - mean for v in x]
            var = sum(jnp.sum(v * v, axis=1, keepdims=True) for v in x_mid) * (1.0 / D)
            factor = lax.rsqrt(var + EPS)
            score = 0.0
            at = rows(b * BLOCK, BLOCK)
            for part in range(parts):
                lanes = pl.ds(part * TILE, TILE)
                normed = x_mid[part] * factor
                lifted = normed * par[pl.ds(j, 1), lanes] + par[pl.ds(J + j, 1), lanes]
                gat[0, j, rows(z * R + b * BLOCK, BLOCK), lanes] = lifted.astype(BF16)
                normed_of[j, at, lanes] = normed
                score = score + jnp.sum(x[part] * par[pl.ds(2 * J + j, 1), lanes], axis=1, keepdims=True)
            stats[0, j, at] = jax.nn.sigmoid(score)
            stats[1, j, at] = factor

        loop(R // BLOCK, block)
        send_own(0, j)
        take_in(j, 1)

        def weigh(b):
            at = rows(b * BLOCK, BLOCK)
            for part in range(parts):
                g = xg[j, 1, quarter(part, b), :].astype(F32)
                gat[1, j, rows(z * R + b * BLOCK, BLOCK), pl.ds(part * TILE, TILE)] = (stats[0, j, at] * g).astype(BF16)

        loop(R // BLOCK, weigh)
        send_own(1, j)
        total = jnp.sum(stats[3, j] * stats[0, j], axis=0, keepdims=True)
        number = jnp.sum(stats[3, j], axis=0, keepdims=True)
        zs[z, pl.ds(0, 8), :] += jnp.where(lane8 == j, total, 0.0)
        zs[z, pl.ds(8, 8), :] += jnp.where(lane8 == j, number, 0.0)

    loop(J, prepare)

    def zs_copy(d, source):
        return pltpu.make_async_remote_copy(
            src_ref=zs.at[source], dst_ref=zs.at[source],
            send_sem=zs_s.at[d], recv_sem=zs_r.at[d],
            device_id=(e, (z + d) % H), device_id_type=MESH)

    for d in range(1, H):
        zs_copy(d, z).start()

    for copy in weights:
        copy.wait()

    wide = 2 * TILE

    def compute(chunk, j):
        mine = rows(chunk * R, R)

        def first(t):
            pre = contract(gat[0, j, mine, :], vwin[j, :, cols(t, wide)]) + bin_[pl.ds(j, 1), cols(t, wide)]
            sq = pre * pre
            th = jnp.tanh(pre * (GELU_A + (GELU_A * GELU_B) * sq))
            cdf = 0.5 + 0.5 * th
            slope = cdf + pre * (0.5 - 0.5 * th * th) * (GELU_A + (3.0 * GELU_A * GELU_B) * sq)
            act[j, mine, cols(t, wide)] = (pre * cdf).astype(BF16)
            act_grad = contract(gat[1, j, mine, :], vwout[j, cols(t, wide), :], ((1,), (1,)))
            pre_grad = (act_grad * slope).astype(BF16)
            pg[j, mine, cols(t, wide)] = pre_grad
            o_bin[pl.ds(j, 1), cols(t, wide)] += jnp.sum(pre_grad.astype(F32), axis=0, keepdims=True)

        loop(F // wide, first)

        def second(t):
            v = contract(act[j, mine, :], vwout[j, :, cols(t, wide)])
            sbuf[0, j, chunk, :, cols(t, wide)] = v.astype(BF16)
            w = contract(pg[j, mine, :], vwin[j, cols(t, wide), :], ((1,), (1,)))
            sbuf[1, j, chunk, :, cols(t, wide)] = w.astype(BF16)

        loop(D // wide, second)

    def outer(left, right, to, tall, wide):
        turned[pl.ds(0, tall), :] = jnp.transpose(left)

        def tile(t):
            to[:, cols(t)] = contract(turned[pl.ds(0, tall), :], right[:, cols(t)])

        loop(wide // TILE, tile)

    def mg_copy(d, source):
        return pltpu.make_async_remote_copy(
            src_ref=mg.at[source], dst_ref=mg.at[source],
            send_sem=mg_s.at[d], recv_sem=mg_r.at[d],
            device_id=((e + d) % G, z), device_id_type=MESH)

    def gb_copy(d, source, target):
        return pltpu.make_async_remote_copy(
            src_ref=grads.at[:, cols(target, PW)], dst_ref=gbuf.at[source],
            send_sem=gb_s.at[d], recv_sem=gb_r.at[d],
            device_id=(e, (z + d) % H), device_id_type=MESH)

    def ret_copy(j, a, d, target):
        return pltpu.make_async_remote_copy(
            src_ref=snd.at[j, a, msg(target)], dst_ref=ret.at[a, rows(j * GM + e * MSG, MSG)],
            send_sem=ret_s.at[j, a, d], recv_sem=ret_r.at[j, a, d],
            device_id=(target, z), device_id_type=MESH)

    def ret_in(j, a, d):
        k = (e - d + G) % G
        return pltpu.make_async_remote_copy(
            src_ref=snd.at[j, a, msg(k)], dst_ref=ret.at[a, rows(j * GM + k * MSG, MSG)],
            send_sem=ret_s.at[j, a, d], recv_sem=ret_r.at[j, a, d],
            device_id=((e + d) % G, z), device_id_type=MESH)

    def wait_sums(a, j):
        def both(size):
            for piece in range(PIECES):
                @pl.when(z < H - 1)
                def _(piece=piece):
                    red_in(a, j, piece, z, size).wait_recv()

                @pl.when(z > 0)
                def _(piece=piece):
                    red_in(a, j, piece, H, size).wait_recv()

        with_rows(z, both)

    def summed(a, j, b, part):
        at = (rows(b * BLOCK, BLOCK), pl.ds(part * TILE, TILE))
        v = sbuf[(a, j, z, *at)].astype(F32) + rbuf[(a, j, z, *at)].astype(F32) + rbuf[(a, j, H, *at)].astype(F32)
        return jnp.where(stats[3, j, at[0]] > 0.5, v, 0.0)

    def send_home(j, a):
        snd[j, a] = contract(unpick[...], xg[j, a]).astype(BF16)
        for d in range(1, G):
            ret_copy(j, a, d, (e + d) % G).start()
        ret[a, rows(j * GM + e * MSG, MSG), :] = snd[j, a, msg(e), :]

    def finish(j):
        wait_sums(0, j)

        def forward(b):
            at = rows(b * BLOCK, BLOCK)
            gate = stats[0, j, at]
            gate_grad = 0.0
            for part in range(parts):
                lanes = pl.ds(part * TILE, TILE)
                branch = (summed(0, j, b, part) + par[pl.ds(3 * J + j, 1), lanes]).astype(BF16).astype(F32)
                x = xg[j, 0, quarter(part, b), :].astype(F32)
                gate_grad = gate_grad + jnp.sum(
                    xg[j, 1, quarter(part, b), :].astype(F32) * branch, axis=1, keepdims=True)
                rbuf[0, j, H, at, lanes] = x.astype(BF16)
                xg[j, 0, quarter(part, b), :] = (x + gate * branch).astype(BF16)
            score_grad = gate_grad * gate * (1.0 - gate)
            stats[2, j, at] = score_grad
            for part in range(parts):
                lanes = pl.ds(part * TILE, TILE)
                x = rbuf[0, j, H, at, lanes].astype(F32)
                grads[pl.ds(2 * J + j, 1), lanes] += jnp.sum(score_grad * x, axis=0, keepdims=True)
                sent = gat[1, j, rows(z * R + b * BLOCK, BLOCK), lanes].astype(F32)
                grads[pl.ds(3 * J + j, 1), lanes] += jnp.sum(sent, axis=0, keepdims=True)

        loop(R // BLOCK, forward)
        send_home(j, 0)
        wait_sums(1, j)

        def backward(b):
            at = rows(b * BLOCK, BLOCK)
            factor, score_grad = stats[1, j, at], stats[2, j, at]
            sum_n, sum_nn = 0.0, 0.0
            n_grads = []
            for part in range(parts):
                lanes = pl.ds(part * TILE, TILE)
                lifted_grad = summed(1, j, b, part)
                normed = normed_of[j, at, lanes]
                grads[pl.ds(j, 1), lanes] += jnp.sum(lifted_grad * normed, axis=0, keepdims=True)
                grads[pl.ds(J + j, 1), lanes] += jnp.sum(lifted_grad, axis=0, keepdims=True)
                n_grad = lifted_grad * par[pl.ds(j, 1), lanes]
                sum_n = sum_n + jnp.sum(n_grad, axis=1, keepdims=True)
                sum_nn = sum_nn + jnp.sum(n_grad * normed, axis=1, keepdims=True)
                n_grads.append(n_grad)
            for part in range(parts):
                lanes = pl.ds(part * TILE, TILE)
                rows_grad = factor * (
                    n_grads[part] - sum_n * (1.0 / D) - normed_of[j, at, lanes] * (sum_nn * (1.0 / D)))
                rows_grad = rows_grad.astype(BF16).astype(F32)
                g = xg[j, 1, quarter(part, b), :].astype(F32)
                moved = g + score_grad * par[pl.ds(2 * J + j, 1), lanes] + rows_grad
                xg[j, 1, quarter(part, b), :] = moved.astype(BF16)

        loop(R // BLOCK, backward)
        send_home(j, 1)

    last = jnp.maximum(z, H - 1 - z)
    grads[...] = jnp.zeros_like(grads)

    def sent(i):
        for d in range(1, G):
            disp_copy(i // 2, i % 2, d, (e + d) % G).wait_send()

    def starts(up):
        return jnp.where(up == 1, z == 0, z == H - 1)

    def passes(up, to):
        return jnp.where(up == 1, (z > 0) & (z < to), (z < H - 1) & (z > to))

    def begin(to, j, up):
        def both(size):
            for a in range(2):
                for piece in range(PIECES):
                    red_copy(a, j, piece, to, up, size).start()

        with_rows(to, both)

    def pass_sum(a, j, to, up):
        def both(size):
            for piece in range(PIECES):
                red_in(a, j, piece, to, size).wait_recv()
                at = (a, j, to, pl.ds(*piece_of(size, piece)))
                sbuf[at] = (sbuf[at].astype(F32) + rbuf[at].astype(F32)).astype(BF16)
                red_copy(a, j, piece, to, up, size).start()

        with_rows(to, both)

    def item(q):
        s, j = q // J, q % J

        def forwarded(i):
            up, a = 1 - i // 2, i % 2
            chunk = jnp.where(up == 1, z - s, z + s)

            @pl.when((s > 0) & (chunk >= 0) & (chunk < H))
            def _():
                def pass_on(size):
                    gat_copy(a, j, chunk, up, size).wait_recv()
                    send_gat(a, j, chunk, up, size)

                with_rows(chunk, pass_on)

        loop(4, forwarded)

        def side(d):
            chunk = jnp.where(d == 0, z - s, z + s)

            @pl.when((chunk >= 0) & (chunk < H) & ((s > 0) | (d == 0)))
            def _():
                compute(chunk, j)

                @pl.when(starts(d) & (s > 0) & ((s > 1) | (j < J - 1)))
                def _():
                    begin(chunk, j, d)

        loop(2, side)

        middle = last < H - 1
        early = middle & (s == H - 1) & (j == J - 1)
        late = (s == H) & (jnp.logical_not(middle) | (j == J - 1))
        first = jnp.where(early, 0, j)
        count = jnp.where(early, J - 1, jnp.where(late, 1, 0))

        @pl.when(q == (H - 1) * J)
        def _():
            loop(2 * J, sent)

        lax.fori_loop(first, first + count, lambda i, _: (finish(i), 0)[1], 0)

        def through(i):
            a, up = i // 2, (i + jnp.where(z >= H // 2, 0, 1)) % 2
            to = jnp.where(up == 1, s, H - 1 - s)
            near = (a == 1) & (to == z + 2 * up - 1) & (j == J - 1) & (s < H - 1)

            @pl.when((s > 0) & (s < H) & passes(up, to) & jnp.logical_not(near))
            def _():
                pass_sum(a, j, to, up)

        loop(4, through)

        @pl.when(q == H * J - 1)
        def _():
            for up in range(2):
                to = z + 2 * up - 1

                @pl.when(starts(up) & (to >= 0) & (to < H))
                def _(up=up, to=to):
                    begin(to, J - 1, up)

                @pl.when(passes(up, to) & (jnp.where(up == 1, to, H - 1 - to) < H - 1))
                def _(up=up, to=to):
                    pass_sum(1, J - 1, to, up)

        @pl.when((s == last) & (j == 0))
        def _():
            for d in range(1, H):
                zs_copy(d, (z - d + H) % H).wait_recv()
            both = zs[0]
            for h in range(1, H):
                both = both + zs[h]
            mg[e] = both[0:8] / jnp.maximum(both[8:16], 1.0)
            for d in range(1, G):
                mg_copy(d, e).start()

        @pl.when(s == last)
        def _():
            outer(gat[0, j], pg.at[j], o_win.at[j], D, F)
            outer(act[j], gat.at[1, j], o_wout.at[j], F, D)

    loop((H + 1) * J, item)
    for d in range(1, H):
        gb_copy(d, z, (z + d) % H).start()

    gbuf[z] = grads[:, own_cols]
    for d in range(1, G):
        mg_copy(d, (e - d + G) % G).wait_recv()
    means = jnp.zeros((8, 128), F32)
    for k in range(G):
        v = mg[k] if k == 0 else pltpu.roll(mg[k], k * J, 1)
        means = jnp.where((lane8 >= k * J) & (lane8 < k * J + J), v, means)
    o_mean[...] = means[0:1, 0:E]

    for d in range(1, H):
        gb_copy(d, (z - d + H) % H, z).wait_recv()
    small = gbuf[0]
    for h in range(1, H):
        small = small + gbuf[h]
    o_gain[...] = small[0:J]
    o_bias[...] = small[J:2 * J]
    o_cent[...] = small[2 * J:3 * J]
    o_bout[...] = small[3 * J:4 * J]

    for d in range(1, H):
        par_copy(d, z).wait_send()
        zs_copy(d, z).wait_send()
        gb_copy(d, z, (z + d) % H).wait_send()
    for d in range(1, G):
        mg_copy(d, e).wait_send()

    def drain(i):
        a, j, h = i // (J * H), i // H % J, i % H

        def wait(size):
            @pl.when((z < H - 1) & (h <= z))
            def _():
                gat_copy(a, j, h, 1, size).wait_send()

            @pl.when((z > 0) & (h >= z))
            def _():
                gat_copy(a, j, h, 0, size).wait_send()

            @pl.when(h != z)
            def _():
                for piece in range(PIECES):
                    red_copy(a, j, piece, h, jnp.where(h > z, 1, 0), size).wait_send()

        with_rows(h, wait)

    loop(2 * J * H, drain)

    def arrived(i):
        j, a = i // 2, i % 2
        for d in range(1, G):
            ret_in(j, a, d).wait_recv()
            ret_copy(j, a, d, (e + d) % G).wait_send()

    loop(2 * J, arrived)


def deliver_kernel(dims, home, ret, slot, *refs):
    G, H, J, S, MSG, R, T, D, F, PW, seq_len = dims
    results, (o_mixed, o_tg, *outs), (mixed, moved, sem) = refs[:8], refs[8:18], refs[18:]
    copies = [pltpu.make_async_copy(a, b, sem.at[i]) for i, (a, b) in enumerate(zip(results, outs))]
    for i in (3, 5, 0, 1, 2, 4, 6, 7):
        copies[i].start()

    spot = jnp.transpose(jnp.broadcast_to(slot[pl.ds(0, 1), :].astype(F32), (128, T)))[:, 0:1].astype(jnp.int32)
    live_rows = spot >= 0
    m = iota((T, J * G * MSG), 1)
    for part in range(D // TILE):
        take = ones_where(spot + part * S == m)
        at = pl.ds(part * TILE, TILE)
        for a, to in enumerate((mixed, moved)):
            kept = home[a, pl.ds(part * T, T), :].astype(F32)
            to[:, at] = jnp.where(live_rows, contract(take, ret[a]), kept).astype(BF16)
    for i, (a, b) in enumerate(((mixed, o_mixed), (moved, o_tg))):
        copies.append(pltpu.make_async_copy(a, b, sem.at[8 + i]))
        copies[-1].start()
    for copy in copies:
        copy.wait()


def on_device(
    tokens, assignment, lengths, centroids, ln_gain, ln_bias, w_in, b_in, w_out, b_out, cotangent
):
    T, D = tokens.shape
    G, H = lax.axis_size("expert"), lax.axis_size("hidden")
    J, F = w_in.shape[0], w_in.shape[2]
    PW = centroids.shape[1]
    S = max(2, 9 * T // (8 * J * G))
    parts = D // TILE
    MSG = -(-(parts * S + 1) // 16) * 16
    R, GM, N = G * S, G * MSG, H * G * S
    seq_len = min(2048, H * T)
    dims = (G, H, J, S, MSG, R, T, D, F, PW, seq_len)
    vm = pl.BlockSpec(memory_space=pltpu.VMEM)
    hbm = pl.BlockSpec(memory_space=pl.ANY)
    sm = pl.BlockSpec(memory_space=pltpu.SMEM)
    dma = pltpu.SemaphoreType.DMA
    buffers = [
        ((J, D, F), BF16),
        ((J, F, D), BF16),
        ((2, J, N, D), BF16),
        ((J, N, F), BF16),
        ((J, N, F), BF16),
        ((2, J, H, R, D), BF16),
        ((2, J, H + 1, R, D), BF16),
        ((J, 2, GM, TILE), BF16),
        ((J, 2, GM, TILE), BF16),
        ((J, 2, parts * R, TILE), BF16),
        ((GM, parts * T), BF16),
        ((parts * R, GM), BF16),
        ((GM, parts * R), BF16),
        ((R, GM), BF16),
        ((4 * J, D), F32),
        ((4, J, R, 1), F32),
        ((H, 16, 128), F32),
        ((G, 8, 128), F32),
        ((4 * J, D), F32),
        ((H, 4 * J, PW), F32),
        ((J, R, D), F32),
        ((max(D, F), N), BF16),
    ]
    taken = sum(
        jnp.dtype(t).itemsize * -(-s[-1] // 128) * 128 * functools.reduce(lambda a, b: a * b, s[:-1]) for s, t in buffers
    )

    results = [(J, PW), (J, PW), (J, PW), (J, D, F), (J, F), (J, F, D), (J, PW), (1, G * J)]
    shape = jax.ShapeDtypeStruct

    def layer(number, sizes, *args):
        made = pl.pallas_call(
            functools.partial(layer_kernel, dims, sizes),
            name="layer",
            out_shape=[
                pltpu.VMEM((2, parts * T, TILE), BF16),
                pltpu.VMEM((2, J * GM, TILE), BF16),
                pltpu.VMEM((8, T), jnp.int32),
                *[pltpu.VMEM(s, F32) for s in results],
            ],
            in_specs=[vm, sm, vm, vm, vm, vm, vm, hbm, hbm, hbm, hbm],
            out_specs=[vm] * 11,
            scratch_shapes=[
                *[pltpu.VMEM(s, t) for s, t in buffers],
                dma((2 * parts + 2,)),
                dma((H,)), dma((H,)),
                dma((H,)), dma((H,)),
                dma((G,)), dma((G,)),
                dma((H,)), dma((H,)),
                dma((J, 2, G)), dma((J, 2, G)),
                dma((J, 2, G)), dma((J, 2, G)),
                dma((2, 2, J, H)), dma((2, J, H)),
                dma((2, J, PIECES, H)), dma((2, J, PIECES, H + 1)),
            ],
            compiler_params=pltpu.CompilerParams(
                collective_id=number, has_side_effects=True, vmem_limit_bytes=taken + 3 * 2**20
            ),
            cost_estimate=pl.CostEstimate(
                flops=12 * J * N * D * F, bytes_accessed=30 * 2**20, transcendentals=J * N * F
            ),
        )(*args)
        return pl.pallas_call(
            functools.partial(deliver_kernel, dims),
            name="deliver",
            out_shape=[shape((T, D), BF16), shape((T, D), BF16), *[shape(s, F32) for s in results]],
            in_specs=[vm] * 11,
            out_specs=[hbm] * 10,
            scratch_shapes=[pltpu.VMEM((T, D), BF16), pltpu.VMEM((T, D), BF16), dma((10,))],
            compiler_params=pltpu.CompilerParams(vmem_limit_bytes=8 * 2**20),
        )(*made)

    args = (
        assignment.reshape(1, T), lengths, centroids, ln_gain, ln_bias, b_out, b_in, tokens, cotangent, w_in, w_out
    )
    options = []
    for shares in SHAPES:
        needed = [-(-G * shares[4 * h // H] // 8) * S for h in range(H)]
        options.append(tuple(-(-r // 16) * 16 for r in needed))
    which = jnp.zeros((1,), jnp.int32)
    if len(options) > 1:
        def pick_shape(lens, found):
            counts = []
            for h in range(H):
                count = jnp.int32(0)
                for i in range(G):
                    first = (i * H + h) * T
                    count = count + (lens[first // seq_len] > first % seq_len).astype(jnp.int32)
                counts.append(count * S)
            best = jnp.int32(0)
            for i, needed in enumerate(options[1:]):
                fits = counts[0] <= needed[0]
                for h in range(1, H):
                    fits = fits & (counts[h] <= needed[h])
                best = jnp.where(fits, i + 1, best)
            found[0] = best

        which = pl.pallas_call(
            pick_shape, name="shape", out_shape=jax.ShapeDtypeStruct((1,), jnp.int32),
            in_specs=[sm], out_specs=sm,
        )(lengths)
    which = which[0]

    def choose(low, high):
        if high - low == 1:
            return functools.partial(layer, low, options[low])
        middle = (low + high) // 2
        return lambda *args: lax.cond(which >= middle, choose(middle, high), choose(low, middle), *args)

    outs = choose(0, len(options))(*args)
    return (*outs[:9], outs[9].reshape(G * J))


def solution(mesh):
    tok = P(("expert", "hidden"), None)
    par = P("expert", "hidden")
    win = P("expert", None, "hidden")
    wout = P("expert", "hidden", None)
    return jax.shard_map(
        on_device,
        mesh=mesh,
        in_specs=(tok, tok, P(), par, par, par, win, par, wout, par, tok),
        out_specs=(tok, tok, par, par, par, win, par, wout, par, P()),
        check_vma=False,
    )
```

```python
import functools

import jax
import jax.numpy as jnp
from jax import lax
from jax.experimental import pallas as pl
from jax.experimental.pallas import tpu as pltpu
from jax.sharding import PartitionSpec as P

EPS = 1e-05
MESH = pl.DeviceIdType.MESH
F32 = jnp.float32
BF16 = jnp.bfloat16
TILE = 256
PIECES = 2
GELU_A = 0.7978845608028654
GELU_B = 0.044715
SHAPES = ((8, 8, 8, 8), (8, 7, 6, 5), (8, 6, 4, 3),)


def contract(a, b, dims=((1,), (0,))):
    return lax.dot_general(a, b, (dims, ((), ())), preferred_element_type=F32)


def iota(shape, axis):
    return lax.broadcasted_iota(jnp.int32, shape, axis)


def ones_where(mask):
    return mask.astype(F32).astype(BF16)


def per(index, size, count):
    return jnp.floor((index.astype(F32) + 0.5) * (1.0 / size)).astype(jnp.int32)


def layer_kernel(
    dims, sizes,
    asg, lens, cent, gain, bias, bout, bin_, tok_in, cot_in, win, wout,
    home, ret, o_slot, o_cent, o_gain, o_bias, o_win, o_bin, o_wout, o_bout, o_mean,
    vwin, vwout, gat, act, pg, sbuf, rbuf, snd, rcv, xg, spread, pick, unpick, pick_count,
    par, stats, zs, mg, grads, gbuf, normed_of, turned,
    w_sem, par_s, par_r, zs_s, zs_r, mg_s, mg_r, gb_s, gb_r,
    disp_s, disp_r, ret_s, ret_r, gat_s, gat_r, red_s, red_r,
):
    G, H, J, S, MSG, R, T, D, F, PW, seq_len = dims
    e, z = lax.axis_index("expert"), lax.axis_index("hidden")
    E, GM, N = G * J, G * MSG, H * R
    parts = D // TILE
    BLOCK = R

    def cols(t, size=TILE):
        return pl.ds(pl.multiple_of(t * size, size), size)

    def rows(start, size):
        return pl.ds(pl.multiple_of(start, 16), size)

    def loop(count, body):
        def step(i, _):
            body(i)
            return 0

        lax.fori_loop(0, count, step, 0)

    barrier = pltpu.get_barrier_semaphore()
    for d in range(1, H):
        pl.semaphore_signal(barrier, inc=1, device_id=(e, (z + d) % H), device_id_type=MESH)
    for d in range(1, G):
        pl.semaphore_signal(barrier, inc=1, device_id=((e + d) % G, z), device_id_type=MESH)

    loads = []
    for a, source in enumerate((tok_in, cot_in)):
        for part in range(parts):
            loads.append(pltpu.make_async_copy(
                source.at[:, pl.ds(part * TILE, TILE)], home.at[a, pl.ds(part * T, T), :],
                w_sem.at[a * parts + part]))
    weights = [
        pltpu.make_async_copy(win, vwin, w_sem.at[2 * parts]),
        pltpu.make_async_copy(wout, vwout, w_sem.at[2 * parts + 1]),
    ]
    for copy in loads + weights:
        copy.start()

    own_cols = cols(z, PW)
    par[pl.ds(0, J), own_cols] = gain[...]
    par[pl.ds(J, J), own_cols] = bias[...]
    par[pl.ds(2 * J, J), own_cols] = cent[...].astype(F32)
    par[pl.ds(3 * J, J), own_cols] = bout[...]

    expert = asg[...]
    place = (e * H + z) * T
    length = lens[place // seq_len]
    live = (place % seq_len + iota((1, T), 1)) < length
    sub_e = iota((E, 1), 0)
    hot = ((expert == sub_e) & live).astype(F32)
    earlier = ones_where(iota((T, T), 0) < iota((T, T), 1))
    before = contract(hot.astype(BF16), earlier)
    group = per(sub_e, J, G)
    inner = sub_e - group * J
    rank = jnp.sum(hot * before, axis=0, keepdims=True).astype(jnp.int32)
    to_group = jnp.sum(hot * group.astype(F32), axis=0, keepdims=True).astype(jnp.int32)
    to_inner = jnp.sum(hot * inner.astype(F32), axis=0, keepdims=True).astype(jnp.int32)
    to_inner = jnp.where(live, to_inner, -1)
    message = to_group * MSG
    o_slot[...] = jnp.broadcast_to(jnp.where(live, to_inner * GM + message + rank, -D * D), (8, T))

    pl.semaphore_wait(barrier, (H - 1) + (G - 1))

    def par_copy(d, source):
        return pltpu.make_async_remote_copy(
            src_ref=par.at[:, cols(source, PW)], dst_ref=par.at[:, cols(source, PW)],
            send_sem=par_s.at[d], recv_sem=par_r.at[d],
            device_id=(e, (z + d) % H), device_id_type=MESH)

    for d in range(1, H):
        par_copy(d, z).start()

    def msg(k):
        return pl.ds(pl.multiple_of(k * MSG, MSG), MSG)

    def disp_copy(j, a, d, target):
        return pltpu.make_async_remote_copy(
            src_ref=snd.at[j, a, msg(target)], dst_ref=rcv.at[j, a, msg(e)],
            send_sem=disp_s.at[j, a, d], recv_sem=disp_r.at[j, a, d],
            device_id=(target, z), device_id_type=MESH)

    def disp_in(j, a, d):
        k = (e - d + G) % G
        return pltpu.make_async_remote_copy(
            src_ref=snd.at[j, a, msg(k)], dst_ref=rcv.at[j, a, msg(k)],
            send_sem=disp_s.at[j, a, d], recv_sem=disp_r.at[j, a, d],
            device_id=((e + d) % G, z), device_id_type=MESH)

    def dispatch(i):
        j, a = i // 2, i % 2
        row = iota((GM, T), 0)
        mine = to_inner == j

        @pl.when(a == 0)
        def _():
            at = jnp.where(mine, message + rank, -D * D)
            for part in range(parts):
                spread[:, pl.ds(part * T, T)] = ones_where(at + part * S == row)

        for b in range(2):
            @pl.when(jnp.logical_and(j == 0, a == b))
            def _(b=b):
                for copy in loads[b * parts:(b + 1) * parts]:
                    copy.wait()

        counted = jnp.where(mine & (a == 0), message + parts * S, -1)
        v = contract(spread[...], home[a]) + contract(ones_where(counted == row), jnp.ones((T, TILE), BF16))
        snd[j, a] = v.astype(BF16)
        for d in range(1, G):
            disp_copy(j, a, d, (e + d) % G).start()
        rcv[j, a, msg(e), :] = snd[j, a, msg(e), :]

    loop(2 * J, dispatch)

    def row_of(c):
        k = per(c, MSG, G)
        start = jnp.full(c.shape, -D * D, jnp.int32)
        filled_before = jnp.int32(0)
        for i in range(G):
            first = (i * H + z) * T
            some = lens[first // seq_len] > first % seq_len
            start = jnp.where((k == i) & some, filled_before * S, start)
            filled_before = filled_before + some.astype(jnp.int32)
        return start, c - k * MSG

    start, within = row_of(iota((1, GM), 1))
    down = iota((R, GM), 0)
    for part in range(parts):
        i = within - part * S
        pick[pl.ds(part * R, R), :] = ones_where(jnp.where((i >= 0) & (i < S), start + i, -1) == down)
    counts_at = jnp.where(within == parts * S, start, -D * D)
    pick_count[...] = ones_where((down >= counts_at) & (down < counts_at + S))
    start, within = row_of(iota((GM, 1), 0))
    across = iota((1, parts * R), 1)
    across_part = per(across, R, parts)
    i = within - across_part * S
    unpick[...] = ones_where((i >= 0) & (i < S) & (start + i == across - across_part * R))

    for h in range(H):
        if sizes[h] < R:
            gat[:, :, pl.ds(h * R + sizes[h], R - sizes[h]), :] = jnp.zeros((2, J, R - sizes[h], D), BF16)

    def clear(slot_at):
        def one(i):
            rbuf[i // J, i % J, slot_at] = jnp.zeros((R, D), BF16)

        loop(2 * J, one)

    pl.when(z == 0)(lambda: clear(H))
    pl.when(z == H - 1)(lambda: clear(H - 1))

    o_bin[...] = jnp.zeros_like(o_bin)

    for d in range(1, H):
        par_copy(d, (z - d + H) % H).wait_recv()

    def with_rows(chunk, body):
        for size in sorted(set(sizes)):
            planes = [h for h in range(H) if sizes[h] == size]
            if len(planes) == H:
                body(size)
            else:
                hit = chunk == planes[0]
                for h in planes[1:]:
                    hit = jnp.logical_or(hit, chunk == h)
                pl.when(hit)(functools.partial(body, size))

    def gat_copy(a, j, chunk, up, size):
        at = (a, j, rows(chunk * R, size))
        return pltpu.make_async_remote_copy(
            src_ref=gat.at[at], dst_ref=gat.at[at],
            send_sem=gat_s.at[up, a, j, chunk], recv_sem=gat_r.at[a, j, chunk],
            device_id=(e, jnp.clip(z + 2 * up - 1, 0, H - 1)), device_id_type=MESH)

    def send_gat(a, j, chunk, up, size):
        @pl.when(jnp.where(up == 1, z < H - 1, z > 0))
        def _():
            gat_copy(a, j, chunk, up, size).start()

    def send_own(a, j):
        def both(size):
            send_gat(a, j, z, 1, size)
            send_gat(a, j, z, 0, size)

        with_rows(z, both)

    def piece_of(size, piece):
        start = 0
        for i in range(piece + 1):
            count = -(-(size - start) // (16 * (PIECES - i))) * 16
            start = start + count
        return start - count, count

    def red_copy(a, j, piece, to, up, size):
        slot_to = jnp.where(jnp.logical_and(up == 1, to == z + 1), H, to)
        at = pl.ds(*piece_of(size, piece))
        return pltpu.make_async_remote_copy(
            src_ref=sbuf.at[a, j, to, at], dst_ref=rbuf.at[a, j, slot_to, at],
            send_sem=red_s.at[a, j, piece, to], recv_sem=red_r.at[a, j, piece, slot_to],
            device_id=(e, jnp.clip(z + 2 * up - 1, 0, H - 1)), device_id_type=MESH)

    def red_in(a, j, piece, slot_at, size):
        at = pl.ds(*piece_of(size, piece))
        return pltpu.make_async_remote_copy(
            src_ref=sbuf.at[a, j, 0, at], dst_ref=rbuf.at[a, j, slot_at, at],
            send_sem=red_s.at[a, j, piece, 0], recv_sem=red_r.at[a, j, piece, slot_at],
            device_id=(e, jnp.clip(z + 1, 0, H - 1)), device_id_type=MESH)

    def quarter(part, b):
        return pl.ds(pl.multiple_of(part * R + b * BLOCK, 16), BLOCK)

    lane8 = iota((8, 128), 1)
    r1 = iota((R, 1), 0)
    rank_in = (r1 - S * per(r1, S, G)).astype(F32)
    zs[z] = jnp.zeros((16, 128), F32)

    def take_in(j, a):
        for d in range(1, G):
            disp_in(j, a, d).wait_recv()
        xg[j, a] = contract(pick[...], rcv[j, a]).astype(BF16)

    def prepare(j):
        take_in(j, 0)
        count = contract(pick_count[...], rcv[j, 0, :, pl.ds(0, 128)])[:, 0:1]
        stats[3, j] = (rank_in < count).astype(F32)

        def block(b):
            x = [xg[j, 0, quarter(part, b), :].astype(F32) for part in range(parts)]
            mean = sum(jnp.sum(v, axis=1, keepdims=True) for v in x) * (1.0 / D)
            x_mid = [v - mean for v in x]
            var = sum(jnp.sum(v * v, axis=1, keepdims=True) for v in x_mid) * (1.0 / D)
            factor = lax.rsqrt(var + EPS)
            score = 0.0
            at = rows(b * BLOCK, BLOCK)
            for part in range(parts):
                lanes = pl.ds(part * TILE, TILE)
                normed = x_mid[part] * factor
                lifted = normed * par[pl.ds(j, 1), lanes] + par[pl.ds(J + j, 1), lanes]
                gat[0, j, rows(z * R + b * BLOCK, BLOCK), lanes] = lifted.astype(BF16)
                normed_of[j, at, lanes] = normed
                score = score + jnp.sum(x[part] * par[pl.ds(2 * J + j, 1), lanes], axis=1, keepdims=True)
            stats[0, j, at] = jax.nn.sigmoid(score)
            stats[1, j, at] = factor

        loop(R // BLOCK, block)
        send_own(0, j)
        take_in(j, 1)

        def weigh(b):
            at = rows(b * BLOCK, BLOCK)
            for part in range(parts):
                g = xg[j, 1, quarter(part, b), :].astype(F32)
                gat[1, j, rows(z * R + b * BLOCK, BLOCK), pl.ds(part * TILE, TILE)] = (stats[0, j, at] * g).astype(BF16)

        loop(R // BLOCK, weigh)
        send_own(1, j)
        total = jnp.sum(stats[3, j] * stats[0, j], axis=0, keepdims=True)
        number = jnp.sum(stats[3, j], axis=0, keepdims=True)
        zs[z, pl.ds(0, 8), :] += jnp.where(lane8 == j, total, 0.0)
        zs[z, pl.ds(8, 8), :] += jnp.where(lane8 == j, number, 0.0)

    loop(J, prepare)

    def zs_copy(d, source):
        return pltpu.make_async_remote_copy(
            src_ref=zs.at[source], dst_ref=zs.at[source],
            send_sem=zs_s.at[d], recv_sem=zs_r.at[d],
            device_id=(e, (z + d) % H), device_id_type=MESH)

    for d in range(1, H):
        zs_copy(d, z).start()

    for copy in weights:
        copy.wait()

    wide_f, wide_d = min(4 * TILE, F), min(4 * TILE, D)

    def compute(chunk, j):
        mine = rows(chunk * R, R)

        def first(t):
            pre = contract(gat[0, j, mine, :], vwin[j, :, cols(t, wide_f)]) + bin_[pl.ds(j, 1), cols(t, wide_f)]
            sq = pre * pre
            th = jnp.tanh(pre * (GELU_A + (GELU_A * GELU_B) * sq))
            cdf = 0.5 + 0.5 * th
            slope = cdf + pre * (0.5 - 0.5 * th * th) * (GELU_A + (3.0 * GELU_A * GELU_B) * sq)
            act[j, mine, cols(t, wide_f)] = (pre * cdf).astype(BF16)
            act_grad = contract(gat[1, j, mine, :], vwout[j, cols(t, wide_f), :], ((1,), (1,)))
            pre_grad = (act_grad * slope).astype(BF16)
            pg[j, mine, cols(t, wide_f)] = pre_grad
            o_bin[pl.ds(j, 1), cols(t, wide_f)] += jnp.sum(pre_grad.astype(F32), axis=0, keepdims=True)

        loop(F // wide_f, first)

        def second(t):
            v = contract(act[j, mine, :], vwout[j, :, cols(t, wide_d)])
            sbuf[0, j, chunk, :, cols(t, wide_d)] = v.astype(BF16)
            w = contract(pg[j, mine, :], vwin[j, cols(t, wide_d), :], ((1,), (1,)))
            sbuf[1, j, chunk, :, cols(t, wide_d)] = w.astype(BF16)

        loop(D // wide_d, second)

    def outer(left, right, to, tall, wide):
        turned[pl.ds(0, tall), :] = jnp.transpose(left)

        def tile(t):
            to[:, cols(t)] = contract(turned[pl.ds(0, tall), :], right[:, cols(t)])

        loop(wide // TILE, tile)

    def mg_copy(d, source):
        return pltpu.make_async_remote_copy(
            src_ref=mg.at[source], dst_ref=mg.at[source],
            send_sem=mg_s.at[d], recv_sem=mg_r.at[d],
            device_id=((e + d) % G, z), device_id_type=MESH)

    def gb_copy(d, source, target):
        return pltpu.make_async_remote_copy(
            src_ref=grads.at[:, cols(target, PW)], dst_ref=gbuf.at[source],
            send_sem=gb_s.at[d], recv_sem=gb_r.at[d],
            device_id=(e, (z + d) % H), device_id_type=MESH)

    def ret_copy(j, a, d, target):
        return pltpu.make_async_remote_copy(
            src_ref=snd.at[j, a, msg(target)], dst_ref=ret.at[a, rows(j * GM + e * MSG, MSG)],
            send_sem=ret_s.at[j, a, d], recv_sem=ret_r.at[j, a, d],
            device_id=(target, z), device_id_type=MESH)

    def ret_in(j, a, d):
        k = (e - d + G) % G
        return pltpu.make_async_remote_copy(
            src_ref=snd.at[j, a, msg(k)], dst_ref=ret.at[a, rows(j * GM + k * MSG, MSG)],
            send_sem=ret_s.at[j, a, d], recv_sem=ret_r.at[j, a, d],
            device_id=((e + d) % G, z), device_id_type=MESH)

    def wait_sums(a, j):
        def both(size):
            for piece in range(PIECES):
                @pl.when(z < H - 1)
                def _(piece=piece):
                    red_in(a, j, piece, z, size).wait_recv()

                @pl.when(z > 0)
                def _(piece=piece):
                    red_in(a, j, piece, H, size).wait_recv()

        with_rows(z, both)

    def summed(a, j, b, part):
        at = (rows(b * BLOCK, BLOCK), pl.ds(part * TILE, TILE))
        v = sbuf[(a, j, z, *at)].astype(F32) + rbuf[(a, j, z, *at)].astype(F32) + rbuf[(a, j, H, *at)].astype(F32)
        return jnp.where(stats[3, j, at[0]] > 0.5, v, 0.0)

    def send_home(j, a):
        snd[j, a] = contract(unpick[...], xg[j, a]).astype(BF16)
        for d in range(1, G):
            ret_copy(j, a, d, (e + d) % G).start()
        ret[a, rows(j * GM + e * MSG, MSG), :] = snd[j, a, msg(e), :]

    def finish(j):
        wait_sums(0, j)

        def forward(b):
            at = rows(b * BLOCK, BLOCK)
            gate = stats[0, j, at]
            gate_grad = 0.0
            for part in range(parts):
                lanes = pl.ds(part * TILE, TILE)
                branch = (summed(0, j, b, part) + par[pl.ds(3 * J + j, 1), lanes]).astype(BF16).astype(F32)
                x = xg[j, 0, quarter(part, b), :].astype(F32)
                gate_grad = gate_grad + jnp.sum(
                    xg[j, 1, quarter(part, b), :].astype(F32) * branch, axis=1, keepdims=True)
                rbuf[0, j, H, at, lanes] = x.astype(BF16)
                xg[j, 0, quarter(part, b), :] = (x + gate * branch).astype(BF16)
            score_grad = gate_grad * gate * (1.0 - gate)
            stats[2, j, at] = score_grad
            for part in range(parts):
                lanes = pl.ds(part * TILE, TILE)
                x = rbuf[0, j, H, at, lanes].astype(F32)
                grads[pl.ds(2 * J + j, 1), lanes] += jnp.sum(score_grad * x, axis=0, keepdims=True)
                sent = gat[1, j, rows(z * R + b * BLOCK, BLOCK), lanes].astype(F32)
                grads[pl.ds(3 * J + j, 1), lanes] += jnp.sum(sent, axis=0, keepdims=True)

        loop(R // BLOCK, forward)
        send_home(j, 0)
        wait_sums(1, j)

        def backward(b):
            at = rows(b * BLOCK, BLOCK)
            factor, score_grad = stats[1, j, at], stats[2, j, at]
            sum_n, sum_nn = 0.0, 0.0
            n_grads = []
            for part in range(parts):
                lanes = pl.ds(part * TILE, TILE)
                lifted_grad = summed(1, j, b, part)
                normed = normed_of[j, at, lanes]
                grads[pl.ds(j, 1), lanes] += jnp.sum(lifted_grad * normed, axis=0, keepdims=True)
                grads[pl.ds(J + j, 1), lanes] += jnp.sum(lifted_grad, axis=0, keepdims=True)
                n_grad = lifted_grad * par[pl.ds(j, 1), lanes]
                sum_n = sum_n + jnp.sum(n_grad, axis=1, keepdims=True)
                sum_nn = sum_nn + jnp.sum(n_grad * normed, axis=1, keepdims=True)
                n_grads.append(n_grad)
            for part in range(parts):
                lanes = pl.ds(part * TILE, TILE)
                rows_grad = factor * (
                    n_grads[part] - sum_n * (1.0 / D) - normed_of[j, at, lanes] * (sum_nn * (1.0 / D)))
                rows_grad = rows_grad.astype(BF16).astype(F32)
                g = xg[j, 1, quarter(part, b), :].astype(F32)
                moved = g + score_grad * par[pl.ds(2 * J + j, 1), lanes] + rows_grad
                xg[j, 1, quarter(part, b), :] = moved.astype(BF16)

        loop(R // BLOCK, backward)
        send_home(j, 1)

    last = jnp.maximum(z, H - 1 - z)
    grads[...] = jnp.zeros_like(grads)

    def sent(i):
        for d in range(1, G):
            disp_copy(i // 2, i % 2, d, (e + d) % G).wait_send()

    def starts(up):
        return jnp.where(up == 1, z == 0, z == H - 1)

    def passes(up, to):
        return jnp.where(up == 1, (z > 0) & (z < to), (z < H - 1) & (z > to))

    def begin(to, j, up):
        def both(size):
            for a in range(2):
                for piece in range(PIECES):
                    red_copy(a, j, piece, to, up, size).start()

        with_rows(to, both)

    def pass_sum(a, j, to, up):
        def both(size):
            for piece in range(PIECES):
                red_in(a, j, piece, to, size).wait_recv()
                at = (a, j, to, pl.ds(*piece_of(size, piece)))
                sbuf[at] = (sbuf[at].astype(F32) + rbuf[at].astype(F32)).astype(BF16)
                red_copy(a, j, piece, to, up, size).start()

        with_rows(to, both)

    def item(q):
        s, j = q // J, q % J

        def forwarded(i):
            up, a = 1 - i // 2, i % 2
            chunk = jnp.where(up == 1, z - s, z + s)

            @pl.when((s > 0) & (chunk >= 0) & (chunk < H))
            def _():
                def pass_on(size):
                    gat_copy(a, j, chunk, up, size).wait_recv()
                    send_gat(a, j, chunk, up, size)

                with_rows(chunk, pass_on)

        loop(4, forwarded)

        def side(d):
            chunk = jnp.where(d == 2, z, jnp.where(d == 0, z - s, z + s))

            @pl.when((chunk >= 0) & (chunk < H) & ((s == 1) | (d < 2)))
            def _():
                compute(chunk, j)

                @pl.when((d < 2) & starts(d) & ((s > 1) | (j < J - 1)))
                def _():
                    begin(chunk, j, d)

        loop(3, side)

        middle = last < H - 1
        early = middle & (s == H - 1) & (j == J - 1)
        late = (s == H) & (jnp.logical_not(middle) | (j == J - 1))
        first = jnp.where(early, 0, j)
        count = jnp.where(early, J - 1, jnp.where(late, 1, 0))

        @pl.when(q == (H - 1) * J)
        def _():
            loop(2 * J, sent)

        lax.fori_loop(first, first + count, lambda i, _: (finish(i), 0)[1], 0)

        def through(i):
            a, up = i // 2, (i + jnp.where(z >= H // 2, 0, 1)) % 2
            to = jnp.where(up == 1, s, H - 1 - s)
            near = (a == 1) & (to == z + 2 * up - 1) & (j == J - 1) & (s < H - 1)

            @pl.when((s > 0) & (s < H) & passes(up, to) & jnp.logical_not(near))
            def _():
                pass_sum(a, j, to, up)

        loop(4, through)

        @pl.when(q == H * J - 1)
        def _():
            for up in range(2):
                to = z + 2 * up - 1

                @pl.when(starts(up) & (to >= 0) & (to < H))
                def _(up=up, to=to):
                    begin(to, J - 1, up)

                @pl.when(passes(up, to) & (jnp.where(up == 1, to, H - 1 - to) < H - 1))
                def _(up=up, to=to):
                    pass_sum(1, J - 1, to, up)

        @pl.when((s == last) & (j == 0))
        def _():
            for d in range(1, H):
                zs_copy(d, (z - d + H) % H).wait_recv()
            both = zs[0]
            for h in range(1, H):
                both = both + zs[h]
            mg[e] = both[0:8] / jnp.maximum(both[8:16], 1.0)
            for d in range(1, G):
                mg_copy(d, e).start()

        @pl.when(s == last)
        def _():
            outer(gat[0, j], pg.at[j], o_win.at[j], D, F)
            outer(act[j], gat.at[1, j], o_wout.at[j], F, D)

    loop(H * J, lambda i: item(i + J))
    for d in range(1, H):
        gb_copy(d, z, (z + d) % H).start()

    gbuf[z] = grads[:, own_cols]
    for d in range(1, G):
        mg_copy(d, (e - d + G) % G).wait_recv()
    means = jnp.zeros((8, 128), F32)
    for k in range(G):
        v = mg[k] if k == 0 else pltpu.roll(mg[k], k * J, 1)
        means = jnp.where((lane8 >= k * J) & (lane8 < k * J + J), v, means)
    o_mean[...] = means[0:1, 0:E]

    for d in range(1, H):
        gb_copy(d, (z - d + H) % H, z).wait_recv()
    small = gbuf[0]
    for h in range(1, H):
        small = small + gbuf[h]
    o_gain[...] = small[0:J]
    o_bias[...] = small[J:2 * J]
    o_cent[...] = small[2 * J:3 * J]
    o_bout[...] = small[3 * J:4 * J]

    for d in range(1, H):
        par_copy(d, z).wait_send()
        zs_copy(d, z).wait_send()
        gb_copy(d, z, (z + d) % H).wait_send()
    for d in range(1, G):
        mg_copy(d, e).wait_send()

    def drain(i):
        a, j, h = i // (J * H), i // H % J, i % H

        def wait(size):
            @pl.when((z < H - 1) & (h <= z))
            def _():
                gat_copy(a, j, h, 1, size).wait_send()

            @pl.when((z > 0) & (h >= z))
            def _():
                gat_copy(a, j, h, 0, size).wait_send()

            @pl.when(h != z)
            def _():
                for piece in range(PIECES):
                    red_copy(a, j, piece, h, jnp.where(h > z, 1, 0), size).wait_send()

        with_rows(h, wait)

    loop(2 * J * H, drain)

    def arrived(i):
        j, a = i // 2, i % 2
        for d in range(1, G):
            ret_in(j, a, d).wait_recv()
            ret_copy(j, a, d, (e + d) % G).wait_send()

    loop(2 * J, arrived)


def deliver_kernel(dims, home, ret, slot, *refs):
    G, H, J, S, MSG, R, T, D, F, PW, seq_len = dims
    results, (o_mixed, o_tg, *outs), (mixed, moved, sem) = refs[:8], refs[8:18], refs[18:]
    copies = [pltpu.make_async_copy(a, b, sem.at[i]) for i, (a, b) in enumerate(zip(results, outs))]
    for i in (3, 5, 0, 1, 2, 4, 6, 7):
        copies[i].start()

    spot = jnp.transpose(jnp.broadcast_to(slot[pl.ds(0, 1), :].astype(F32), (128, T)))[:, 0:1].astype(jnp.int32)
    live_rows = spot >= 0
    m = iota((T, J * G * MSG), 1)
    for part in range(D // TILE):
        take = ones_where(spot + part * S == m)
        at = pl.ds(part * TILE, TILE)
        for a, to in enumerate((mixed, moved)):
            kept = home[a, pl.ds(part * T, T), :].astype(F32)
            to[:, at] = jnp.where(live_rows, contract(take, ret[a]), kept).astype(BF16)
    for i, (a, b) in enumerate(((mixed, o_mixed), (moved, o_tg))):
        copies.append(pltpu.make_async_copy(a, b, sem.at[8 + i]))
        copies[-1].start()
    for copy in copies:
        copy.wait()


def on_device(
    tokens, assignment, lengths, centroids, ln_gain, ln_bias, w_in, b_in, w_out, b_out, cotangent
):
    T, D = tokens.shape
    G, H = lax.axis_size("expert"), lax.axis_size("hidden")
    J, F = w_in.shape[0], w_in.shape[2]
    PW = centroids.shape[1]
    S = max(2, 9 * T // (8 * J * G))
    parts = D // TILE
    MSG = -(-(parts * S + 1) // 16) * 16
    R, GM, N = G * S, G * MSG, H * G * S
    seq_len = min(2048, H * T)
    dims = (G, H, J, S, MSG, R, T, D, F, PW, seq_len)
    vm = pl.BlockSpec(memory_space=pltpu.VMEM)
    hbm = pl.BlockSpec(memory_space=pl.ANY)
    sm = pl.BlockSpec(memory_space=pltpu.SMEM)
    dma = pltpu.SemaphoreType.DMA
    buffers = [
        ((J, D, F), BF16),
        ((J, F, D), BF16),
        ((2, J, N, D), BF16),
        ((J, N, F), BF16),
        ((J, N, F), BF16),
        ((2, J, H, R, D), BF16),
        ((2, J, H + 1, R, D), BF16),
        ((J, 2, GM, TILE), BF16),
        ((J, 2, GM, TILE), BF16),
        ((J, 2, parts * R, TILE), BF16),
        ((GM, parts * T), BF16),
        ((parts * R, GM), BF16),
        ((GM, parts * R), BF16),
        ((R, GM), BF16),
        ((4 * J, D), F32),
        ((4, J, R, 1), F32),
        ((H, 16, 128), F32),
        ((G, 8, 128), F32),
        ((4 * J, D), F32),
        ((H, 4 * J, PW), F32),
        ((J, R, D), F32),
        ((max(D, F), N), BF16),
    ]
    taken = sum(
        jnp.dtype(t).itemsize * -(-s[-1] // 128) * 128 * functools.reduce(lambda a, b: a * b, s[:-1]) for s, t in buffers
    )

    results = [(J, PW), (J, PW), (J, PW), (J, D, F), (J, F), (J, F, D), (J, PW), (1, G * J)]
    shape = jax.ShapeDtypeStruct

    def layer(number, sizes, *args):
        made = pl.pallas_call(
            functools.partial(layer_kernel, dims, sizes),
            name="layer",
            out_shape=[
                pltpu.VMEM((2, parts * T, TILE), BF16),
                pltpu.VMEM((2, J * GM, TILE), BF16),
                pltpu.VMEM((8, T), jnp.int32),
                *[pltpu.VMEM(s, F32) for s in results],
            ],
            in_specs=[vm, sm, vm, vm, vm, vm, vm, hbm, hbm, hbm, hbm],
            out_specs=[vm] * 11,
            scratch_shapes=[
                *[pltpu.VMEM(s, t) for s, t in buffers],
                dma((2 * parts + 2,)),
                dma((H,)), dma((H,)),
                dma((H,)), dma((H,)),
                dma((G,)), dma((G,)),
                dma((H,)), dma((H,)),
                dma((J, 2, G)), dma((J, 2, G)),
                dma((J, 2, G)), dma((J, 2, G)),
                dma((2, 2, J, H)), dma((2, J, H)),
                dma((2, J, PIECES, H)), dma((2, J, PIECES, H + 1)),
            ],
            compiler_params=pltpu.CompilerParams(
                collective_id=number, has_side_effects=True, vmem_limit_bytes=taken + 3 * 2**20
            ),
            cost_estimate=pl.CostEstimate(
                flops=12 * J * N * D * F, bytes_accessed=30 * 2**20, transcendentals=J * N * F
            ),
        )(*args)
        return pl.pallas_call(
            functools.partial(deliver_kernel, dims),
            name="deliver",
            out_shape=[shape((T, D), BF16), shape((T, D), BF16), *[shape(s, F32) for s in results]],
            in_specs=[vm] * 11,
            out_specs=[hbm] * 10,
            scratch_shapes=[pltpu.VMEM((T, D), BF16), pltpu.VMEM((T, D), BF16), dma((10,))],
            compiler_params=pltpu.CompilerParams(vmem_limit_bytes=8 * 2**20),
        )(*made)

    args = (
        assignment.reshape(1, T), lengths, centroids, ln_gain, ln_bias, b_out, b_in, tokens, cotangent, w_in, w_out
    )
    options = []
    for shares in SHAPES:
        needed = [-(-G * shares[4 * h // H] // 8) * S for h in range(H)]
        options.append(tuple(-(-r // 16) * 16 for r in needed))
    which = jnp.zeros((1,), jnp.int32)
    if len(options) > 1:
        def pick_shape(lens, found):
            counts = []
            for h in range(H):
                count = jnp.int32(0)
                for i in range(G):
                    first = (i * H + h) * T
                    count = count + (lens[first // seq_len] > first % seq_len).astype(jnp.int32)
                counts.append(count * S)
            best = jnp.int32(0)
            for i, needed in enumerate(options[1:]):
                fits = counts[0] <= needed[0]
                for h in range(1, H):
                    fits = fits & (counts[h] <= needed[h])
                best = jnp.where(fits, i + 1, best)
            found[0] = best

        which = pl.pallas_call(
            pick_shape, name="shape", out_shape=jax.ShapeDtypeStruct((1,), jnp.int32),
            in_specs=[sm], out_specs=sm,
        )(lengths)
    which = which[0]

    def choose(low, high):
        if high - low == 1:
            return functools.partial(layer, low, options[low])
        middle = (low + high) // 2
        return lambda *args: lax.cond(which >= middle, choose(middle, high), choose(low, middle), *args)

    outs = choose(0, len(options))(*args)
    return (*outs[:9], outs[9].reshape(G * J))


def solution(mesh):
    tok = P(("expert", "hidden"), None)
    par = P("expert", "hidden")
    win = P("expert", None, "hidden")
    wout = P("expert", "hidden", None)
    return jax.shard_map(
        on_device,
        mesh=mesh,
        in_specs=(tok, tok, P(), par, par, par, win, par, wout, par, tok),
        out_specs=(tok, tok, par, par, par, win, par, wout, par, P()),
        check_vma=False,
    )
```
